128 devices in a mesh: img: 32 (over z, y_hi, x), blk: 4 (over y_lo, core).
Axes of the slice: x: 4, y: 4 (y_hi: 2, y_lo: 2; y = y_hi * 2 + y_lo), z: 4, core: 2. Of those that a mesh axis runs over, the one named last changes fastest.
Arguments:
- patches: bfloat16 [1024, 64, 1024], P('blk', 'img'), may hold values from -6 to 6
- cls_tokens: bfloat16 [64, 1024], P('img'), may hold values from -6 to 6
- patch_masks: int32 [1024, 64], P('blk', 'img'), may hold values from 0 to 1, as said below
- mask_token: bfloat16 [1024], replicated, may hold values from -4 to 4
- pos_embed: bfloat16 [1024, 1024], P('blk'), may hold values from -3 to 3
- ln1_gain: float32 [1024], replicated, may hold values from 0.5 to 1.5
- ln1_bias: float32 [1024], replicated, may hold values from -1 to 1
- qkv_weight: bfloat16 [1024, 3072], replicated, may hold values from -0.1875 to 0.1875
- qv_bias: float32 [2048], replicated, may hold values from -3 to 3
- proj_weight: bfloat16 [1024, 1024], replicated, may hold values from -1.5 to 1.5
- proj_bias: float32 [1024], replicated, may hold values from -2 to 2
- scale_attn: float32 [1024], replicated, may hold values from 0.5 to 2
- ln2_gain: float32 [1024], replicated, may hold values from 0.5 to 1.5
- ln2_bias: float32 [1024], replicated, may hold values from -1 to 1
- fc1_weight: bfloat16 [1024, 4096], replicated, may hold values from -0.1875 to 0.1875
- fc1_bias: float32 [4096], replicated, may hold values from -3 to 3
- fc2_weight: bfloat16 [4096, 1024], replicated, may hold values from -0.09375 to 0.09375
- fc2_bias: float32 [1024], replicated, may hold values from -2 to 2
- scale_mlp: float32 [1024], replicated, may hold values from 0.5 to 2
- cot_patches: bfloat16 [1024, 64, 1024], P('blk', 'img'), may hold values from -6 to 6
- cot_cls: bfloat16 [64, 1024], P('img'), may hold values from -6 to 6
Outputs:
- out_patches: bfloat16 [1024, 64, 1024], P('blk', 'img')
- out_cls: bfloat16 [64, 1024], P('img')
- grad_patches: float32 [1024, 64, 1024], P('blk', 'img')
- grad_cls: float32 [64, 1024], P('img')
- grad_mask_token: float32 [1024], P(('img', 'blk'))
- grad_pos_embed: float32 [1024, 1024], P('blk', 'img')
- grad_ln1_gain: float32 [1024], P(('img', 'blk'))
- grad_ln1_bias: float32 [1024], P(('img', 'blk'))
- grad_qkv_weight: float32 [1024, 3072], P(('img', 'blk'))
- grad_qv_bias: float32 [2048], P(('img', 'blk'))
- grad_proj_weight: float32 [1024, 1024], P(('img', 'blk'))
- grad_proj_bias: float32 [1024], P(('img', 'blk'))
- grad_scale_attn: float32 [1024], P(('img', 'blk'))
- grad_ln2_gain: float32 [1024], P(('img', 'blk'))
- grad_ln2_bias: float32 [1024], P(('img', 'blk'))
- grad_fc1_weight: float32 [1024, 4096], P(('img', 'blk'))
- grad_fc1_bias: float32 [4096], P(('img', 'blk'))
- grad_fc2_weight: float32 [4096, 1024], P(('img', 'blk'))
- grad_fc2_bias: float32 [1024], P(('img', 'blk'))
- grad_scale_mlp: float32 [1024], P(('img', 'blk'))
The draws below stay inside these ranges and needn't reach their ends.
Inputs may be any that keep to these rules, and one draw needn't show every extreme that they name: `patch_masks`: each crop masks between 102 and 512 of its patches (inclusive).
All inputs are finite; a program needn't handle non-finite values.
Results may differ from the reference program's by a relative error of at most 0.012.
Values may be sent and summed in bfloat16 or wider, within the bound.
No kernel may reach another device: no remote copies, remote signals or barrier semaphores. Data moves between devices by JAX's collectives and lax.ppermute only.
A program may use at most 448 MiB of HBM per device.

```python
import math
import jax
import jax.numpy as jnp
from jax import lax

D = 1024
HEADS = 16
HEAD_DIM = 64
FF = 4096
PATCHES = 1024
MICRO = 2
CROPS_MB = 1
CROPS = 64


def permute_patches(subkey):
    return jax.random.permutation(subkey, PATCHES)


def draw_patch_masks(key, part):
    key = jax.random.fold_in(key, 7)
    count_key, order_key = jax.random.split(key)
    least_count = max(1, PATCHES // 10)
    counts = jax.random.randint(count_key, (CROPS,), least_count, PATCHES // 2 + 1)
    orders = jax.vmap(permute_patches)(jax.random.split(order_key, CROPS))
    chosen = (orders < counts[:, None]).astype(jnp.int32)
    return jnp.transpose(chosen)


def spiked(entries, key, source, target, parts, factor):
    def block_of(axis_at):
        return (jnp.arange(entries.shape[axis_at]) // (entries.shape[axis_at] // parts)).reshape((-1,) + (1,) * (entries.ndim - 1 - axis_at))

    one_side = jax.random.permutation(key, parts)[block_of(target)]
    other_side = (block_of(target) + parts // 2) % parts
    return jnp.where((block_of(source) == one_side) | (block_of(source) == other_side), factor * entries, entries)


def steps_of(own_key, extent, cuts, least, high):
    def one(axis_at, blocks):
        draws = jax.random.uniform(jax.random.fold_in(jax.random.fold_in(own_key, 6), axis_at), (blocks,), jnp.float32, least / len(cuts), high / len(cuts))
        return jnp.repeat(jnp.exp(draws), extent[axis_at] // blocks).reshape((-1,) + (1,) * (len(extent) - axis_at - 1))

    factor_of = one(*cuts[0])
    for cut in cuts[1:]:
        factor_of = factor_of * one(*cut)
    return factor_of


def normal_values(key, shape, width, limit, cuts=(), kind=jnp.bfloat16):
    level = steps_of(key, shape, cuts, -0.22, 0.18) if cuts else 1.0
    drawn = jax.random.normal(key, shape, jnp.float32) * width * level
    return jnp.minimum(jnp.maximum(drawn, -limit), limit).astype(kind)


def gaussian_with(key, dims, scale, bound, cuts, heavy, kind=jnp.bfloat16):
    values = scale * jax.random.normal(key, dims, jnp.float32)
    if cuts:
        values = values * steps_of(key, dims, cuts, -0.22, 0.18)
    return jnp.clip(spiked(values, jax.random.fold_in(key, 3), *heavy), -bound, bound).astype(kind)


def setup_inputs(seed: int = 0) -> dict:
    key_list = jax.random.split(jax.random.key(seed), 22)
    return {
        "patches": gaussian_with(key_list[0], (PATCHES, CROPS, D), 1.0, 6.0, ((0, 4), (1, 32)), (1, 2, 32, 2.75)),
        "cls_tokens": normal_values(key_list[1], (CROPS, D), 1.0, 6.0, ((0, 32),)),
        "patch_masks": draw_patch_masks(jax.random.fold_in(key_list[21], 71), 0),
        "mask_token": normal_values(key_list[3], (D,), 1.0, 4.0),
        "pos_embed": normal_values(key_list[4], (PATCHES, D), 0.5, 3.0, ((0, 4),)),
        "ln1_gain": jnp.clip(1.0 + 0.1 * jax.random.normal(key_list[5], (D,), jnp.float32), 0.5, 1.5),
        "ln1_bias": normal_values(key_list[6], (D,), 0.2, 1.0, (), jnp.float32),
        "qkv_weight": normal_values(key_list[7], (D, 3 * D), D ** -0.5, 0.1875),
        "qv_bias": normal_values(key_list[8], (2 * D,), 0.5, 3.0, (), jnp.float32),
        "proj_weight": normal_values(key_list[9], (D, D), (D // 64) ** -0.5, 1.5),
        "proj_bias": normal_values(key_list[10], (D,), 0.3, 2.0, (), jnp.float32),
        "scale_attn": jnp.clip(jnp.exp(jax.random.uniform(key_list[11], (D,), jnp.float32, math.log(0.5), math.log(2.0))), 0.5, 2.0),
        "ln2_gain": jnp.clip(1.0 + 0.1 * jax.random.normal(key_list[12], (D,), jnp.float32), 0.5, 1.5),
        "ln2_bias": normal_values(key_list[13], (D,), 0.2, 1.0, (), jnp.float32),
        "fc1_weight": normal_values(key_list[14], (D, FF), D ** -0.5, 0.1875),
        "fc1_bias": normal_values(key_list[15], (FF,), 0.5, 3.0, (), jnp.float32),
        "fc2_weight": normal_values(key_list[16], (FF, D), FF ** -0.5, 0.09375),
        "fc2_bias": normal_values(key_list[17], (D,), 0.3, 2.0, (), jnp.float32),
        "scale_mlp": jnp.clip(jnp.exp(jax.random.uniform(key_list[18], (D,), jnp.float32, math.log(0.5), math.log(2.0))), 0.5, 2.0),
        "cot_patches": gaussian_with(key_list[19], (PATCHES, CROPS, D), 1.0, 6.0, ((0, 4), (1, 32)), (1, 2, 32, 2.75)),
        "cot_cls": normal_values(key_list[20], (CROPS, D), 1.0, 6.0, ((0, 32),)),
    }


EPS = 1e-06
HIGH = lax.Precision.HIGHEST

@jax.custom_vjp
def low(v):
    return lax.optimization_barrier(v.astype(jnp.bfloat16)).astype(jnp.float32)

@jax.custom_vjp
def low_back(v):
    return v

def low_keep(v):
    return (low(v), None)

def low_pass(kept, grad):
    return (grad,)

def back_keep(v):
    return (v, None)

def back_low(kept, grad):
    return (low(grad),)
low.defvjp(low_keep, low_pass)
low_back.defvjp(back_keep, back_low)

def layer_norm(values, gain, bias):
    center = values - lax.optimization_barrier(jnp.mean(values, -1, keepdims=True))
    spread = lax.optimization_barrier(jnp.mean(center * center, -1, keepdims=True))
    return center * lax.rsqrt(spread + EPS) * gain + bias

def project(rows, weight):
    return jnp.einsum('tgd,de->tge', rows, weight, precision=HIGH)

def attend(queries, key_rows, value_rows):
    scores = jnp.einsum('qghe,kghe->ghqk', queries, key_rows, precision=HIGH) * 0.125
    scores = low_back(scores)
    probs = jax.nn.softmax(scores, axis=-1)
    return jnp.einsum('ghqk,kghe->qghe', low(probs), value_rows, precision=HIGH)

def forward(params, patch_vals, cls_vals, mask_vals):
    mask_token, pos_embed, ln1_gain, ln1_bias, qkv_weight, qv_bias, proj_weight, proj_bias, scale_attn, ln2_gain, ln2_bias, fc1_weight, fc1_bias, fc2_weight, fc2_bias, scale_mlp = params
    mixed_in = mask_vals * mask_token + (1.0 - mask_vals) * patch_vals + pos_embed[:, None, :]
    tokens = jnp.concatenate((cls_vals[None], mixed_in), 0)
    normed_one = low(layer_norm(tokens, ln1_gain, ln1_bias))
    joined = project(normed_one, qkv_weight)
    queries = low(low_back(joined[..., :D] + qv_bias[:D]))
    key_rows = low(low_back(joined[..., D:2 * D]))
    value_rows = low(low_back(joined[..., 2 * D:] + qv_bias[D:]))
    head_form = tokens.shape[:2] + (HEADS, HEAD_DIM)
    mixed = jax.checkpoint(attend)(queries.reshape(head_form), key_rows.reshape(head_form), value_rows.reshape(head_form))
    attended = low(low_back(mixed.reshape(tokens.shape)))
    branch_one = low_back(project(attended, proj_weight) + proj_bias)
    hidden = tokens + scale_attn * branch_one
    normed_two = low(layer_norm(hidden, ln2_gain, ln2_bias))
    pre_act = low_back(project(normed_two, fc1_weight) + fc1_bias)
    activ = low(jax.nn.gelu(pre_act, approximate=False))
    branch_two = low_back(project(activ, fc2_weight) + fc2_bias)
    return hidden + scale_mlp * branch_two

def accumulate(total, extra):
    return total + extra

def reference(patches, cls_tokens, patch_masks, mask_token, pos_embed, ln1_gain, ln1_bias, qkv_weight, qv_bias, proj_weight, proj_bias, scale_attn, ln2_gain, ln2_bias, fc1_weight, fc1_bias, fc2_weight, fc2_bias, scale_mlp, cot_patches, cot_cls):
    params = tuple((member.astype(jnp.float32) for member in (mask_token, pos_embed, ln1_gain, ln1_bias, qkv_weight, qv_bias, proj_weight, proj_bias, scale_attn, ln2_gain, ln2_bias, fc1_weight, fc1_bias, fc2_weight, fc2_bias, scale_mlp)))
    group_size = MICRO * CROPS_MB
    group_count = CROPS // group_size

    def split_groups(array):
        return jnp.moveaxis(array.reshape((PATCHES, group_count, group_size) + array.shape[2:]), 1, 0)
    pieces = (split_groups(patches), cls_tokens.reshape(group_count, group_size, D), split_groups(patch_masks), split_groups(cot_patches), cot_cls.reshape(group_count, group_size, D))

    def group_step(totals, piece):
        patch_grp, cls_grp, mask_grp, cot_patch_grp, cot_cls_grp = piece
        mask_vals = mask_grp.astype(jnp.float32)[..., None]

        def run_block(param_list, patch_vals, cls_vals):
            return forward(param_list, patch_vals, cls_vals, mask_vals)
        output, pullback = jax.vjp(run_block, params, patch_grp.astype(jnp.float32), cls_grp.astype(jnp.float32))
        cotangent = jnp.concatenate((cot_cls_grp.astype(jnp.float32)[None], cot_patch_grp.astype(jnp.float32) * mask_vals), 0)
        grad_params, grad_patch_grp, grad_cls_grp = pullback(cotangent)
        totals = jax.tree.map(accumulate, totals, grad_params)
        return (totals, (output[1:].astype(jnp.bfloat16), output[0].astype(jnp.bfloat16), grad_patch_grp, grad_cls_grp))
    start_totals = tuple((jnp.zeros_like(member) for member in params))
    totals, stacked = lax.scan(group_step, start_totals, pieces)
    out_patches = jnp.moveaxis(stacked[0], 0, 1).reshape(PATCHES, CROPS, D)
    out_cls = stacked[1].reshape(CROPS, D)
    grad_patches = jnp.moveaxis(stacked[2], 0, 1).reshape(PATCHES, CROPS, D)
    grad_cls = stacked[3].reshape(CROPS, D)
    return (out_patches, out_cls, grad_patches, grad_cls, totals[0], totals[1], totals[2], totals[3], totals[4], totals[5], totals[6], totals[7], totals[8], totals[9], totals[10], totals[11], totals[12], totals[13], totals[14], totals[15])
```

```python
import functools
import itertools

import jax
import jax.numpy as jnp
from jax import lax
from jax.experimental import pallas as pl
from jax.experimental.pallas import tpu as pltpu
from jax.sharding import Mesh
from jax.sharding import PartitionSpec as P

EPS = 1e-06
BF = jnp.bfloat16
F32 = jnp.float32
TAIL = 16
INV_SQRT2 = 0.7071067811865476
INV_SQRT2PI = 0.3989422804014327
PAN = 128

ALL = ("z", "yh", "x", "yl", "core")
SIZES = {"z": 4, "yh": 2, "x": 4, "yl": 2, "core": 2}
Y = ("yh", "yl")


def nn(a, b):
    return jnp.dot(a, b, preferred_element_type=F32)


def nt(a, b):
    return lax.dot_general(a, b, (((1,), (1,)), ((), ())), preferred_element_type=F32)


def tn(a, b):
    return lax.dot_general(a, b, (((0,), (0,)), ((), ())), preferred_element_type=F32)


def params(mib):
    return pltpu.CompilerParams(vmem_limit_bytes=mib << 20)


def cost(macs, nbytes, exps=0):
    return pl.CostEstimate(flops=2 * macs, bytes_accessed=nbytes, transcendentals=exps)


def whole(shape):
    return pl.BlockSpec(shape, lambda *_: (0,) * len(shape))


def sd(shape, dtype=BF):
    return jax.ShapeDtypeStruct(shape, dtype)


def unit_of(x):
    center = x - jnp.mean(x, -1, keepdims=True)
    inv = lax.rsqrt(jnp.mean(center * center, -1, keepdims=True) + EPS)
    return center * inv, inv


def unit_grad(gu, unit, inv):
    return (gu - jnp.mean(gu, -1, keepdims=True) - unit * jnp.mean(gu * unit, -1, keepdims=True)) * inv


def norm_project_body(x_ref, gain_ref, bias_ref, w_ref, add_ref, normed_ref, out_ref):
    @pl.when(pl.program_id(0) == 0)
    def _():
        unit, _ = unit_of(x_ref[...])
        normed_ref[...] = (unit * gain_ref[...] + bias_ref[...]).astype(BF)

    out_ref[...] = (nn(normed_ref[...], w_ref[...]) + add_ref[...]).astype(BF)


def project_body(scale, x_ref, w_ref, add_ref, out_ref):
    out_ref[...] = ((nn(x_ref[...], w_ref[...]) + add_ref[...]) * scale).astype(BF)


def project_call(x, w, add, first, stride, norm=None, scale=1.0, tile=512):
    rows, width = x.shape
    at = lambda i: (0, first + stride * i)
    mat, vec = whole((rows, width)), whole((1, width))
    out = pl.BlockSpec((rows, tile), lambda i: (0, i))
    shape = sd((rows, 2 * tile))
    ins = [pl.BlockSpec((width, tile), at), pl.BlockSpec((1, tile), at)]
    common = dict(grid=(2,), compiler_params=params(32),
                  cost_estimate=cost(rows * width * 2 * tile, 4 * (width * tile + rows * tile)))
    if norm is None:
        return pl.pallas_call(functools.partial(project_body, scale), in_specs=[mat] + ins, out_specs=out,
                              out_shape=shape, name="project", **common)(x, w, add)
    return pl.pallas_call(norm_project_body, in_specs=[mat, vec, vec] + ins, out_specs=[mat, out],
                          out_shape=[sd((rows, width)), shape], name="norm_project", **common)(x, *norm, w, add)


def half_mask(h):
    return (lax.broadcasted_iota(jnp.int32, (1, PAN), 1) // 64) == h


def att_fwd_body(np_, q_ref, ko_ref, vo_ref, kp_ref, vp_ref, *refs, chunk):
    out_ref, lse_ref = refs[-2:]
    rows = q_ref.shape[0]
    k_tail = ko_ref[np_:np_ + TAIL, :]
    v_cls = vo_ref[np_:np_ + 1, :].astype(F32)
    ko, kp = ko_ref[0:np_, :], kp_ref[0:np_, :]
    vo, vp = vo_ref[0:np_, :], vp_ref[0:np_, :]
    for r0 in range(0, rows, chunk):
        q = q_ref[r0:r0 + chunk, :]
        outs, lses = [], []
        for h in range(2):
            qh = jnp.where(half_mask(h), q, jnp.zeros_like(q))
            s1, s2 = nt(qh, ko), nt(qh, kp)
            sc = nt(qh, k_tail)[:, 0:1]
            top = jnp.maximum(jnp.maximum(jnp.max(s1, -1, keepdims=True), jnp.max(s2, -1, keepdims=True)), sc)
            p1, p2, pc = jnp.exp(s1 - top), jnp.exp(s2 - top), jnp.exp(sc - top)
            total = jnp.sum(p1, -1, keepdims=True) + jnp.sum(p2, -1, keepdims=True) + pc
            o = nn(p1.astype(BF), vo) + nn(p2.astype(BF), vp) + pc * v_cls
            outs.append(o / total)
            lses.append(top + jnp.log(total))
        out_ref[r0:r0 + chunk, :] = jnp.where(half_mask(0), outs[0], outs[1]).astype(BF)
        lse_ref[r0:r0 + chunk, :] = jnp.where(half_mask(0), lses[0], lses[1])


def att_fwd_call(q, kv, kv_p, group, pairs, into=None, chunk=264):
    rows, width = q.shape
    np_ = rows - TAIL
    col = lambda a: pl.BlockSpec((rows, PAN), lambda i: (0, a + i))
    at = group * pairs
    ins = [col(at), col(0), col(pairs), col(0), col(pairs)]
    args = [q, kv, kv, kv_p, kv_p]
    if into is not None:
        ins.append(pl.BlockSpec(memory_space=pl.ANY))
        args.append(into)
    return pl.pallas_call(
        functools.partial(att_fwd_body, np_, chunk=chunk),
        grid=(pairs,),
        in_specs=ins,
        out_specs=[col(at), col(0)],
        out_shape=[sd((rows, width)), sd((rows, pairs * PAN), F32)],
        input_output_aliases={} if into is None else {5: 0},
        compiler_params=params(40),
        cost_estimate=cost(rows * 2 * np_ * PAN * 2 * pairs * 2, 2 * rows * PAN * pairs * 8, rows * 2 * np_ * 2 * pairs),
        name="att_fwd",
    )(*args)


def att_bwd_body(np_, q_ref, ko_ref, vo_ref, kp_ref, vp_ref, go_ref, o_ref, lse_ref, dq_ref, own_ref, part_ref):
    q, go = q_ref[...], go_ref[...]
    ko, kp = ko_ref[0:np_, :], kp_ref[0:np_, :]
    vo, vp = vo_ref[0:np_, :], vp_ref[0:np_, :]
    k_tail, v_tail = ko_ref[np_:np_ + TAIL, :], vo_ref[np_:np_ + TAIL, :]
    k_cls = k_tail[0:1].astype(F32)
    qt, gt = q.T, go.T
    qf, gf = q.astype(F32), go.astype(F32)
    prod = gf * o_ref[...].astype(F32)
    dq = dkc = dvc = None
    dk1, dk2, dv1, dv2 = [], [], [], []
    for h in range(2):
        mask = half_mask(h)
        qh = jnp.where(mask, q, jnp.zeros_like(q))
        gh = jnp.where(mask, go, jnp.zeros_like(go))
        delta = jnp.sum(jnp.where(mask, prod, 0.0), -1, keepdims=True)
        lse = lse_ref[:, 64 * h:64 * h + 1]
        qth, gth = qt[64 * h:64 * h + 64], gt[64 * h:64 * h + 64]
        dqh = None
        for k, v, dk, dv in ((ko, vo, dk1, dv1), (kp, vp, dk2, dv2)):
            p = jnp.exp(nt(qh, k) - lse)
            ds = (p * (nt(gh, v) - delta)).astype(BF)
            part = nn(ds, k)
            dqh = part if dqh is None else dqh + part
            dk.append(nn(qth, ds))
            dv.append(nn(gth, p.astype(BF)))
        pc = jnp.exp(nt(qh, k_tail)[:, 0:1] - lse)
        dsc = pc * (nt(gh, v_tail)[:, 0:1] - delta)
        dqh = (dqh + dsc * k_cls) * 0.125
        kc = jnp.sum(dsc * qf, 0, keepdims=True)
        vc = jnp.sum(pc * gf, 0, keepdims=True)
        dq = dqh if h == 0 else jnp.where(mask, dqh, dq)
        dkc = kc if h == 0 else jnp.where(mask, kc, dkc)
        dvc = vc if h == 0 else jnp.where(mask, vc, dvc)
    dq_ref[...] = dq.astype(BF)
    both = lambda parts: jnp.concatenate(parts, 0).T.astype(BF)
    own_ref[0:np_, 0:PAN] = both(dk1)
    own_ref[0:np_, PAN:2 * PAN] = both(dv1)
    part_ref[:, 0:PAN] = both(dk2)
    part_ref[:, PAN:2 * PAN] = both(dv2)
    first = lax.broadcasted_iota(jnp.int32, (TAIL, PAN), 0) == 0
    own_ref[np_:np_ + TAIL, 0:PAN] = jnp.where(first, dkc, 0.0).astype(BF)
    own_ref[np_:np_ + TAIL, PAN:2 * PAN] = jnp.where(first, dvc, 0.0).astype(BF)


def att_bwd_call(q, kv, kv_p, go, o, lse, group, pairs):
    rows = q.shape[0]
    np_ = rows - TAIL
    at = group * pairs
    col = lambda a: pl.BlockSpec((rows, PAN), lambda i: (0, a + i))
    two = lambda n: pl.BlockSpec((n, 2 * PAN), lambda i: (0, i))
    return pl.pallas_call(
        functools.partial(att_bwd_body, np_),
        grid=(pairs,),
        in_specs=[col(at), col(0), col(pairs), col(0), col(pairs), col(at), col(at), col(0)],
        out_specs=[col(0), two(rows), two(np_)],
        out_shape=[sd((rows, pairs * PAN)), sd((rows, pairs * 2 * PAN)), sd((np_, pairs * 2 * PAN))],
        compiler_params=params(48),
        cost_estimate=cost(rows * 2 * np_ * PAN * 5 * pairs * 2, 2 * rows * PAN * pairs * 16, rows * 2 * np_ * 2 * pairs),
        name="att_bwd",
    )(q, kv, kv, kv_p, kv_p, go, o, lse)


def trip_body(np_, pairs, order_ref, dq_ref, own_ref, came_ref, mine_ref, send_ref):
    core = order_ref[0]
    n = pairs // 2 * PAN
    for out_ref, side in ((mine_ref, core), (send_ref, 1 - core)):
        out_ref[:, 0:n] = dq_ref[:, pl.ds(pl.multiple_of(side * n, PAN), n)]
        for j in range(pairs // 2):
            for kind in range(2):
                src = pl.ds(pl.multiple_of(side * 2 * n + (2 * j + kind) * PAN, PAN), PAN)
                dst = slice((1 + kind) * n + j * PAN, (1 + kind) * n + (j + 1) * PAN)
                out_ref[0:np_, dst] = (own_ref[0:np_, src].astype(F32) + came_ref[:, src].astype(F32)).astype(BF)
                out_ref[np_:, dst] = own_ref[np_:, src]


def trip_call(order, dq, own, came):
    rows, n = dq.shape
    np_ = rows - TAIL
    shape = sd((rows, n // 2 * 3))
    return pl.pallas_call(
        functools.partial(trip_body, np_, n // PAN),
        grid_spec=pltpu.PrefetchScalarGridSpec(
            num_scalar_prefetch=1, grid=(1,),
            in_specs=[whole(a.shape) for a in (dq, own, came)],
            out_specs=[whole(shape.shape)] * 2),
        out_shape=[shape, shape],
        compiler_params=params(24),
        cost_estimate=cost(0, 2 * rows * n * 8),
        name="trip",
    )(order, dq, own, came)


def mlp_fwd_body(order_ref, att_ref, tok_ref, wp_ref, bp_ref, sa_ref, gain_ref, bias_ref, w1_ref, b1_ref, w2_ref, b2_ref,
                 sm_ref, gout_ref, hid_ref, br1_ref, n2_ref, act_ref, dg_ref, out_ref, gb2_ref, gb2s_ref, vec_ref, acc_ref):
    i = pl.program_id(0)

    @pl.when(i == 0)
    def _():
        br1 = nn(att_ref[...], wp_ref[...]) + bp_ref[...]
        br1_ref[...] = br1.astype(BF)
        hid = tok_ref[...] + sa_ref[...] * br1
        hid_ref[...] = hid
        unit, _ = unit_of(hid)
        n2_ref[...] = (unit * gain_ref[...] + bias_ref[...]).astype(BF)

    pre = nn(n2_ref[...], w1_ref[...]) + b1_ref[...]
    cdf = 0.5 + 0.5 * lax.erf(pre * INV_SQRT2)
    act = (pre * cdf).astype(BF)
    act_ref[...] = act
    dg_ref[...] = (cdf + pre * (jnp.exp(-0.5 * pre * pre) * INV_SQRT2PI)).astype(BF)
    part = nn(act, w2_ref[...])

    @pl.when(i == 0)
    def _():
        acc_ref[...] = part

    @pl.when(i > 0)
    def _():
        acc_ref[...] += part

    @pl.when(i == pl.num_programs(0) - 1)
    def _():
        br2 = acc_ref[...] + b2_ref[...]
        out_ref[...] = (hid_ref[...] + sm_ref[...] * br2).astype(BF)
        gout = gout_ref[...].astype(F32)
        gb2 = (sm_ref[...] * gout).astype(BF)
        gb2_ref[...] = gb2
        vec_ref[0:1, :] = jnp.sum(gout * br2, 0, keepdims=True)
        vec_ref[1:2, :] = jnp.sum(gb2.astype(F32), 0, keepdims=True)
        n = gb2s_ref.shape[1]
        gb2s_ref[...] = gb2_ref[:, pl.ds(pl.multiple_of((1 - order_ref[0]) * n, PAN), n)]


def mlp_fwd_call(order, att, tok, wp, bp, sa, gain, bias, w1, b1, w2, b2, sm, gout, tile=512):
    rows, width = tok.shape
    ff = w1.shape[1]
    mat, vec = whole((rows, width)), whole((1, width))
    col = pl.BlockSpec((rows, tile), lambda i, c: (0, i))
    return pl.pallas_call(
        mlp_fwd_body,
        grid_spec=pltpu.PrefetchScalarGridSpec(
            num_scalar_prefetch=1,
            grid=(ff // tile,),
            in_specs=[mat, mat, whole((width, width)), vec, vec, vec, vec,
                      pl.BlockSpec((width, tile), lambda i, c: (0, i)), pl.BlockSpec((1, tile), lambda i, c: (0, i)),
                      pl.BlockSpec((tile, width), lambda i, c: (i, 0)), vec, vec, mat],
            out_specs=[mat, mat, mat, col, col, mat, mat, whole((rows, width // 2)), whole((8, width))],
            scratch_shapes=[pltpu.VMEM((rows, width), F32)]),
        out_shape=[sd((rows, width), F32), sd((rows, width)), sd((rows, width)), sd((rows, ff)), sd((rows, ff)),
                   sd((rows, width)), sd((rows, width)), sd((rows, width // 2)), sd((8, width), F32)],
        compiler_params=params(56),
        cost_estimate=cost(rows * width * (2 * ff + width), 2 * (2 * width * ff + 2 * rows * ff + 6 * rows * width), rows * ff),
        name="mlp_fwd",
    )(order, att, tok, wp, bp, sa, gain, bias, w1, b1, w2, b2, sm, gout)


def mlp_bwd_body(half, order_ref, gb2_ref, dg_ref, w1_ref, w2_ref, hid_ref, br1_ref, gout_ref, wp_ref, sa_ref, gain_ref,
                 gpre_ref, gpres_ref, b1_ref, ghid_ref, gb1_ref, gb1s_ref, gatt_ref, vec_ref, acc_ref):
    i = pl.program_id(0)
    gpre = (nt(gb2_ref[...], w2_ref[...]) * dg_ref[...].astype(F32)).astype(BF)
    gpre_ref[...] = gpre

    @pl.when(i < half)
    def _():
        gpres_ref[...] = gpre

    b1_ref[0:1, :] = jnp.sum(gpre.astype(F32), 0, keepdims=True)
    part = nt(gpre, w1_ref[...])

    @pl.when(i == 0)
    def _():
        acc_ref[...] = part

    @pl.when(i > 0)
    def _():
        acc_ref[...] += part

    @pl.when(i == pl.num_programs(0) - 1)
    def _():
        unit, inv = unit_of(hid_ref[...])
        gn = acc_ref[...]
        vec_ref[0:1, :] = jnp.sum(gn * unit, 0, keepdims=True)
        vec_ref[1:2, :] = jnp.sum(gn, 0, keepdims=True)
        ghid = gout_ref[...].astype(F32) + unit_grad(gn * gain_ref[...], unit, inv)
        ghid_ref[...] = ghid
        vec_ref[2:3, :] = jnp.sum(ghid * br1_ref[...].astype(F32), 0, keepdims=True)
        gb1 = (sa_ref[...] * ghid).astype(BF)
        gb1_ref[...] = gb1
        vec_ref[3:4, :] = jnp.sum(gb1.astype(F32), 0, keepdims=True)
        n = gb1s_ref.shape[1]
        gb1s_ref[...] = gb1_ref[:, pl.ds(pl.multiple_of((1 - order_ref[0]) * n, PAN), n)]
        gatt_ref[...] = nt(gb1, wp_ref[...]).astype(BF)


def mlp_bwd_call(order, gb2, dg, w1, w2, hid, br1, gout, wp, sa, gain, tile=512):
    rows, width = hid.shape
    ff = w1.shape[1]
    steps = ff // tile
    half = steps // 2
    mat, vec, halfm = whole((rows, width)), whole((1, width)), whole((rows, width // 2))
    at = lambda i, c: (i + half * (1 - c[0])) % steps
    col = lambda n: pl.BlockSpec((n, tile), lambda i, c: (0, at(i, c)))
    return pl.pallas_call(
        functools.partial(mlp_bwd_body, half),
        grid_spec=pltpu.PrefetchScalarGridSpec(
            num_scalar_prefetch=1,
            grid=(steps,),
            in_specs=[mat, col(rows), col(width), pl.BlockSpec((tile, width), lambda i, c: (at(i, c), 0)),
                      mat, mat, mat, whole((width, width)), vec, vec],
            out_specs=[col(rows), pl.BlockSpec((rows, tile), lambda i, c: (0, jnp.minimum(i, half - 1))), col(8),
                       mat, mat, halfm, mat, whole((8, width))],
            scratch_shapes=[pltpu.VMEM((rows, width), F32)]),
        out_shape=[sd((rows, ff)), sd((rows, ff // 2)), sd((8, ff), F32), sd((rows, width), F32), sd((rows, width)),
                   sd((rows, width // 2)), sd((rows, width)), sd((8, width), F32)],
        compiler_params=params(56),
        cost_estimate=cost(rows * width * (2 * ff + width), 2 * (2 * width * ff + 2 * rows * ff + 6 * rows * width)),
        name="mlp_bwd",
    )(order, gb2, dg, w1, w2, hid, br1, gout, wp, sa, gain)


def put_panels(ref, lead, base, value, rows):
    n = value.shape[1] // PAN
    for chip, place in enumerate(lead):
        for rg in range(rows // 16):
            for pc in range(n):
                r0 = chip * rows + rg * 16
                ref[(0,) + place + (base + rg * n + pc,)] = value[r0:r0 + 16, pc * PAN:(pc + 1) * PAN]


CHIPS_OF_Z = list(itertools.product(range(2), range(4), range(2)))


def vector_panels(vec_refs, wide_refs):
    r = lax.broadcasted_iota(jnp.int32, (256, 1), 0)
    device = jnp.where(r % 16 < 2, r // 16 * 2 + r % 16, -1)
    total, at = None, 0
    for ref, row, per in [(v, i, 8) for v, rows in vec_refs for i in rows] + wide_refs:
        n = 32 * per
        lane = lax.broadcasted_iota(jnp.int32, (1, n), 1)
        spread = jnp.where(lane // per == device, ref[row:row + 1, :], 0.0).astype(BF)
        pick_r = lax.broadcasted_iota(jnp.int32, (n, PAN), 0)
        pick_c = lax.broadcasted_iota(jnp.int32, (n, PAN), 1)
        part = nn(spread, jnp.where(pick_r % per + at == pick_c, 1.0, 0.0).astype(BF))
        total = part if total is None else total + part
        at += per
    return total.astype(BF)


def dw_near_body(jobs, extra, order_ref, *refs):
    send_ref, keep_ref = refs[-2:]
    i = pl.program_id(0)
    done, at, base = [], 0, 0
    for rows, panels in jobs:
        a0, a1, g0, g1 = (ref[...] for ref in refs[at:at + 4])
        done.append(((tn(a0, g0) + tn(a1, g1)).astype(BF), base, rows))
        at, base = at + 4, base + panels
    if extra:
        pos_ref, vf, vb, vt, b1, qv = refs[at:at + 6]
        done.append((vector_panels([(vf, (0, 1)), (vb, (0, 1, 2, 3)), (vt, (0, 1, 2))], [(b1, 0, 32), (qv, 0, 16)]),
                     base + 4, 16))

    def write(ref):
        for value, first, rows in done:
            put_panels(ref, CHIPS_OF_Z, first, value, rows)
        if extra:
            half = pos_ref.shape[1] // 2
            for yh, x, side, rg, pc in itertools.product(range(2), range(4), range(2), range(2), range(2)):
                r0, c0 = (yh * 4 + x) * 32 + rg * 16, side * half + pc * PAN
                yl = order_ref[9] if side == 0 else 1 - order_ref[9]
                ref[0, yh, x, yl, base + rg * 2 + pc] = pos_ref[r0:r0 + 16, c0:c0 + PAN]

    pl.when(i < 2)(lambda: write(send_ref))
    pl.when(i >= 2)(lambda: write(keep_ref))


def dw_near_call(order, jobs, extra=()):
    ins, args, shapes, macs = [], [], [], 0
    for a0, a1, g0, g1 in jobs:
        rows, k = a0.shape
        n = g0.shape[1]
        lhs = pl.BlockSpec((rows, k // 4), lambda i, c: (0, c[1 + i]))
        ins += [lhs, lhs, whole((rows, n)), whole((rows, n))]
        args += [a0, a1, g0, g1]
        shapes.append((k // 64, k // 1024 * (n // PAN)))
        macs += 2 * rows * k * n
    panels = sum(p for _, p in shapes)
    if extra:
        pos, *vecs = extra
        ins.append(pl.BlockSpec((pos.shape[0] // 4, pos.shape[1]), lambda i, c: (c[1 + i], 0)))
        ins += [pl.BlockSpec((8, v.shape[1] // 4), lambda i, c: (0, c[1 + i])) for v in vecs]
        args += list(extra)
        panels += 5
    block = (1, 2, 4, 2, panels, 16, PAN)
    out = sd((2,) + block[1:])
    at = lambda f: pl.BlockSpec(block, lambda i, c: (f(i),) + (0,) * 6)
    return pl.pallas_call(
        functools.partial(dw_near_body, tuple(shapes), bool(extra)),
        grid_spec=pltpu.PrefetchScalarGridSpec(
            num_scalar_prefetch=1, grid=(4,), in_specs=ins,
            out_specs=[at(lambda i: jnp.minimum(i, 1)), at(lambda i: jnp.maximum(i - 2, 0))]),
        out_shape=[out, out],
        compiler_params=params(48),
        cost_estimate=cost(macs, 2 * sum(a.size for a in args) + 4 * out.size),
        name="dw_near",
    )(order, *args)


def dw_far_body(order_ref, a0_ref, a1_ref, g0_ref, g1_ref, send_ref, keep_ref):
    i = pl.program_id(0)
    n = g1_ref.shape[1] // PAN
    total = (tn(a0_ref[...], g0_ref[...]) + tn(a1_ref[...], g1_ref[...])).astype(BF)
    for target in range(4):
        at = order_ref[5 + target]

        def write(ref, slot):
            for yh, yl, pc in itertools.product(range(2), range(2), range(n)):
                r0 = (yh * 4 + target) * 32 + yl * 16
                ref[slot, i, yh, yl, pc] = total[r0:r0 + 16, pc * PAN:(pc + 1) * PAN]

        pl.when(at < 2)(functools.partial(write, send_ref, at))
        pl.when(at >= 2)(functools.partial(write, keep_ref, at - 2))


def dw_far_call(order, a0, a1, g0, g1):
    rows, k = a0.shape
    nh = g1.shape[1]
    lhs = pl.BlockSpec((rows, k // 4), lambda i, c: (0, i))
    shape = (2, 4, 2, 2, nh // PAN, 16, PAN)
    return pl.pallas_call(
        dw_far_body,
        grid_spec=pltpu.PrefetchScalarGridSpec(
            num_scalar_prefetch=1,
            grid=(4,),
            in_specs=[lhs, lhs, pl.BlockSpec((rows, nh), lambda i, c: (0, c[0])), whole((rows, nh))],
            out_specs=[whole(shape), whole(shape)]),
        out_shape=[sd(shape)] * 2,
        compiler_params=params(48),
        cost_estimate=cost(2 * rows * k * nh, 2 * (2 * rows * k + 2 * rows * nh + k * nh)),
        name="dw_far",
    )(order, a0, a1, g0, g1)


def tok_bwd_body(half, order_ref, g_mine0, g_mine1, g_send0, g_send1, wq_ref, wk_ref, wv_ref, tok_ref, ghid_ref, gain_ref,
                 mask_ref, own_ref, send_ref, pos_ref, cls_ref, vec_ref, qv_ref, acc_ref):
    i = pl.program_id(0)
    n = wq_ref.shape[1]
    width = tok_ref.shape[1]
    core = order_ref[0]
    for step, g_ref in enumerate((g_mine0, g_mine1, g_send0, g_send1)):
        @pl.when(i == step)
        def _():
            part = nt(g_ref[:, 0:n], wq_ref[...]) + nt(g_ref[:, n:2 * n], wk_ref[...]) + nt(g_ref[:, 2 * n:], wv_ref[...])
            if step == 0:
                acc_ref[...] = part
            else:
                acc_ref[...] += part
            sums = jnp.sum(g_ref[...].astype(F32), 0, keepdims=True)
            side = core if step < 2 else 1 - core
            at = pl.multiple_of((step % 2) * 2 * n + side * n, PAN)
            qv_ref[0:1, pl.ds(at, n)] = sums[:, 0:n]
            qv_ref[0:1, pl.ds(width + at, n)] = sums[:, 2 * n:]

    @pl.when(i == 3)
    def _():
        unit, inv = unit_of(tok_ref[...])
        gn = acc_ref[...]
        vec_ref[0:1, :] = jnp.sum(gn * unit, 0, keepdims=True)
        vec_ref[1:2, :] = jnp.sum(gn, 0, keepdims=True)
        gtok = ghid_ref[...] + unit_grad(gn * gain_ref[...], unit, inv)
        vec_ref[2:3, :] = jnp.sum(gtok * mask_ref[:, 0:1].astype(F32), 0, keepdims=True)
        own_ref[...] = gtok[0:half]
        send_ref[...] = gtok[half:].astype(BF)
        cls_ref[...] = gtok[2 * half:2 * half + 8]
        pos_ref[...] = gtok[0:2 * half].T.astype(BF)


def tok_bwd_call(order, mine, send, w, tok, ghid, gain, mask):
    rows, width = tok.shape
    half = (rows - TAIL) // 2
    n = mine[0].shape[1] // 3
    per = width // n
    mat, vec = whole((rows, width)), whole((1, width))
    gs = whole((rows, 3 * n))
    head = lambda i, c: (i % 2) * 2 + jnp.where(i < 2, c[0], 1 - c[0])
    ws = [pl.BlockSpec((width, n), lambda i, c, j=j: (0, j * per + head(i, c))) for j in range(3)]
    return pl.pallas_call(
        functools.partial(tok_bwd_body, half),
        grid_spec=pltpu.PrefetchScalarGridSpec(
            num_scalar_prefetch=1,
            grid=(4,),
            in_specs=[gs] * 4 + ws + [mat, mat, vec, whole((rows, PAN))],
            out_specs=[whole((half, width)), whole((half + TAIL, width)), whole((width, 2 * half)), whole((8, width)),
                       whole((8, width)), whole((8, 2 * width))],
            scratch_shapes=[pltpu.VMEM((rows, width), F32)]),
        out_shape=[sd((half, width), F32), sd((half + TAIL, width)), sd((width, 2 * half)), sd((8, width), F32),
                   sd((8, width), F32), sd((8, 2 * width), F32)],
        compiler_params=params(48),
        cost_estimate=cost(rows * width * 3 * width, 2 * (3 * width * width + 8 * rows * width)),
        name="tok_bwd",
    )(order, *mine, *send, w, w, w, tok, ghid, gain, mask)


def near_sum_body(keep_ref, came_ref, kept_ref, send_ref):
    kept_ref[...] = keep_ref[0].astype(F32) + came_ref[0].astype(F32)
    send_ref[...] = (keep_ref[1].astype(F32) + came_ref[1].astype(F32)).astype(BF)


def near_sum(keep, came, parts=4):
    shape = keep.shape
    m = keep.size // (2 * 16 * PAN)
    flat = lambda a: a.reshape(2, m, 16, PAN)
    parts = parts if m % parts == 0 and m >= 16 else 1
    two = pl.BlockSpec((2, m // parts, 16, PAN), lambda i: (0, i, 0, 0))
    one = pl.BlockSpec((m // parts, 16, PAN), lambda i: (i, 0, 0))
    kept, send = pl.pallas_call(
        near_sum_body, grid=(parts,), in_specs=[two, two], out_specs=[one, one],
        out_shape=[sd((m, 16, PAN), F32), sd((m, 16, PAN))],
        compiler_params=params(24), cost_estimate=cost(0, keep.size * 6), name="near_sum",
    )(flat(keep), flat(came))
    return kept.reshape(shape[1:]), send.reshape(shape[1:])


def far_sum_body(axis, count, order_ref, *refs):
    send_ref, keep_ref = refs[-2:]
    for slot in range(4):
        target = order_ref[1 + slot]
        at = 0
        for j in range(count):
            keep, came = refs[2 * j], refs[2 * j + 1]
            n = keep.shape[-3]
            if axis == "y":
                where = (target // 2, target % 2)
            elif axis == "z":
                where = (target,)
            else:
                where = (slice(None), target)
            total = keep[where].astype(F32) + came[where].astype(F32)
            out = (slot % 2,) + (slice(None),) * (total.ndim - 3) + (slice(at, at + n),)
            if slot < 2:
                send_ref[out] = total.astype(BF)
            else:
                keep_ref[out] = total
            at += n


def far_sum(order, pairs, axis):
    lead = {"z": 1, "x": 2, "y": 2}[axis]
    shape = pairs[0][0].shape
    rest = ((shape[0],) if axis == "x" else ()) + shape[lead:-3]
    panels = sum(k.shape[-3] for k, _ in pairs)
    out = (2,) + rest + (panels, 16, PAN)
    args = [a for pair in pairs for a in pair]
    return pl.pallas_call(
        functools.partial(far_sum_body, axis, len(pairs)),
        grid_spec=pltpu.PrefetchScalarGridSpec(
            num_scalar_prefetch=1, grid=(1,),
            in_specs=[whole(a.shape) for a in args],
            out_specs=[whole(out)] * 2),
        out_shape=[sd(out), sd(out, F32)],
        compiler_params=params(40), cost_estimate=cost(0, sum(a.size for a in args) * 6), name="far_sum",
    )(order, *args)


def last_sum_body(order_ref, keep_ref, came_ref, cls_ref, mine_ref, gone_ref, pos_ref, tot_ref):
    core = order_ref[0]
    tot_ref[...] = keep_ref[...] + came_ref[...].astype(F32)
    at = 0

    def put(panel, start):
        nonlocal at
        for ref, side in ((mine_ref, core), (gone_ref, 1 - core)):
            ref[at] = tot_ref[panel, pl.ds(pl.multiple_of(start(side), 8), 8), :]
        at += 1

    for rg, pc, part in itertools.product(range(2), range(4), range(2)):
        for ref, side in ((mine_ref, core), (gone_ref, 1 - core)):
            ref[at] = tot_ref[(2 * side + rg) * 4 + pc, 8 * part:8 * part + 8, :]
        at += 1
    for panel in list(range(16, 42)):
        if panel < 42:
            put(panel, lambda side: side * 8)
    for panel in range(42, 48):
        put(panel, lambda side: side * 8)
    mine_ref[at] = tot_ref[52, 0:8, :]
    gone_ref[at] = tot_ref[52, 0:8, :]
    for part in range(2):
        mine_ref[at + 1 + part] = cls_ref[8 * part:8 * part + 8, :]
        gone_ref[at + 1 + part] = cls_ref[8 * part:8 * part + 8, :]
    for rg, pc in itertools.product(range(2), range(2)):
        pos_ref[16 * rg:16 * rg + 16, pc * PAN:(pc + 1) * PAN] = tot_ref[48 + rg * 2 + pc]


SWAPPED = 16 + 26 + 6 + 3


def last_sum(order, keep, came, cls16):
    shape = sd((SWAPPED, 8, PAN), F32)
    return pl.pallas_call(
        last_sum_body,
        grid_spec=pltpu.PrefetchScalarGridSpec(
            num_scalar_prefetch=1, grid=(1,),
            in_specs=[whole(keep.shape), whole(came.shape), whole(cls16.shape)],
            out_specs=[whole(shape.shape), whole(shape.shape), whole((32, 256))],
            scratch_shapes=[pltpu.VMEM(keep.shape, F32)]),
        out_shape=[shape, shape, sd((32, 256), F32)],
        compiler_params=params(24), cost_estimate=cost(0, keep.size * 10), name="last_sum",
    )(order, keep, came, cls16)


def finish_body(order_ref, mine_ref, came_ref, fc2_ref, fc1_ref, proj_ref, qkv_ref, vec_ref, cls_ref):
    first = order_ref[0] == 0
    at = 0

    def halves():
        nonlocal at
        mine, came = mine_ref[at], came_ref[at]
        at += 1
        return jnp.where(first, mine, came), jnp.where(first, came, mine)

    for rg, pc, part in itertools.product(range(2), range(4), range(2)):
        r0 = rg * 16 + part * 8
        for h, value in enumerate(halves()):
            fc2_ref[r0:r0 + 8, 512 * h + pc * PAN:512 * h + (pc + 1) * PAN] = value
    for pc in range(16):
        for h, value in enumerate(halves()):
            fc1_ref[:, 2048 * h + pc * PAN:2048 * h + (pc + 1) * PAN] = value
    for pc in range(4):
        for h, value in enumerate(halves()):
            proj_ref[:, 512 * h + pc * PAN:512 * h + (pc + 1) * PAN] = value
    for group, kind, pc in itertools.product(range(2), range(3), range(2)):
        for h, value in enumerate(halves()):
            c0 = kind * 1024 + group * 512 + h * 256 + pc * PAN
            qkv_ref[:, c0:c0 + PAN] = value
    vec_ref[...] = mine_ref[at] + came_ref[at]
    for part in range(2):
        cls_ref[8 * part:8 * part + 8, :] = mine_ref[at + 1 + part] + came_ref[at + 1 + part]


def finish(order, mine, came):
    outs = [(32, 1024), (8, 4096), (8, 1024), (8, 3072), (8, PAN), (16, PAN)]
    return pl.pallas_call(
        finish_body,
        grid_spec=pltpu.PrefetchScalarGridSpec(
            num_scalar_prefetch=1, grid=(1,), in_specs=[whole(mine.shape)] * 2, out_specs=[whole(s) for s in outs]),
        out_shape=[sd(s, F32) for s in outs],
        compiler_params=params(24), cost_estimate=cost(0, mine.size * 16), name="finish",
    )(order, mine, came)


def swap(x, axis):
    return lax.ppermute(x, axis, [(0, 1), (1, 0)])


def after(x, *others):
    return lax.optimization_barrier((x,) + others)[0]


def partners(axis, turn):
    pairs = []
    for z, yh, x, yl, core in itertools.product(*(range(SIZES[a]) for a in ALL)):
        at = {"z": z, "y": yh * 2 + yl, "x": x}
        flat = lambda p: (((p["z"] * 2 + p["y"] // 2) * 4 + p["x"]) * 2 + p["y"] % 2) * 2 + core
        there = dict(at)
        there[axis] ^= 1 if core == turn else 3
        pairs.append((flat(at), flat(there)))
    return pairs


def pass_on(x, axis, turn):
    return lax.ppermute(x, ALL, partners(axis, turn))


def order_of(axis):
    me = lax.axis_index("yh") * 2 + lax.axis_index("yl") if axis == "y" else lax.axis_index(axis)
    first = jnp.where(lax.axis_index("core") == 0, 1, 3)
    targets = [me ^ first, me ^ 2, me, me ^ first ^ 2]
    places = [sum(jnp.where(t == want, at, 0) for at, t in enumerate(targets)) for want in range(4)]
    return jnp.stack([lax.axis_index("core")] + targets + places + [lax.axis_index("yl")]).astype(jnp.int32)


class Scatter:
    def __init__(self, orders, send, keep, axis):
        self.orders, self.axis, self.keep = orders, axis, keep
        self.came = pass_on(send, axis, 0)

    def near(self):
        self.kept, send = near_sum(self.keep, self.came)
        self.came = pass_on(send, self.axis, 1)
        return send

    def far(self, axis, *others):
        pairs = [(s.kept, s.came) for s in (self,) + others]
        send, self.keep = far_sum(self.orders[axis], pairs, axis)
        self.axis = axis
        self.came = pass_on(send, axis, 0)
        return send


def local(patches, cls_tokens, patch_masks, mask_token, pos_embed, ln1_gain, ln1_bias, qkv_weight, qv_bias, proj_weight,
          proj_bias, scale_attn, ln2_gain, ln2_bias, fc1_weight, fc1_bias, fc2_weight, fc2_bias, scale_mlp, cot_patches,
          cot_cls):
    half, _, width = patches.shape
    pairs = 4
    core, yl = lax.axis_index("core"), lax.axis_index("yl")
    row = lambda v: v.reshape(1, -1)
    sides = lambda a: (jnp.where(yl == 0, a[:, 0], a[:, 1]), jnp.where(yl == 0, a[:, 1], a[:, 0]))
    both = lambda mine, other, axis: jnp.where(yl == 0, jnp.stack((mine, other), axis), jnp.stack((other, mine), axis))
    pad = jnp.zeros((TAIL - 1, width), BF)
    orders = {a: order_of(a) for a in "zxy"}
    order = orders["z"]

    mask_f = patch_masks.astype(F32)
    mask3 = patch_masks[..., None]
    mixed = jnp.where(mask3 != 0, mask_token, patches)
    own, send = sides(mixed)
    came = swap(send, "yl")
    pos_came = lax.ppermute(pos_embed, Y, [(0, 3), (3, 0), (1, 2), (2, 1)])
    cls_row = jnp.where(yl == 0, cls_tokens[0:1], cls_tokens[1:2])
    tok = jnp.concatenate((own.astype(F32) + pos_embed.astype(F32), came.astype(F32) + pos_came.astype(F32),
                           cls_row.astype(F32), pad.astype(F32)), 0)

    add = row(jnp.concatenate((qv_bias[:width], jnp.zeros((width,), F32), qv_bias[width:])))
    n1, kv0 = project_call(tok, qkv_weight, add, 2, 2, norm=(row(ln1_gain), row(ln1_bias)))
    kv0_p = swap(kv0, "core")
    kv1 = project_call(after(n1, kv0), qkv_weight, add, 3, 2)
    kv1_p = swap(after(kv1, kv0_p), "core")
    q = project_call(after(n1, kv1), qkv_weight, add, 0, 1, scale=0.125)

    mask_own, mask_send = sides(mask_f)
    cot_own, cot_send = sides(jnp.where(mask3 != 0, cot_patches, jnp.zeros_like(cot_patches)))
    lanes = lambda m: jnp.broadcast_to(m.astype(BF)[:, None], (half, PAN))
    cot_came = swap(after(jnp.concatenate((cot_send, lanes(mask_send)), 1), came), "yl")

    att, lse0 = att_fwd_call(q, kv0, kv0_p, 0, pairs)
    att, lse1 = att_fwd_call(q, kv1, kv1_p, 1, pairs, into=att)
    n1_p = swap(after(n1, kv1_p), "core")
    cot_came = after(cot_came, att)
    cls_cot = jnp.where(yl == 0, cot_cls[0:1], cot_cls[1:2]) * (core == 0).astype(BF)
    gout = jnp.concatenate((cot_own, cot_came[:, :width], cls_cot, pad), 0)
    mask_rows = jnp.concatenate((lanes(mask_own), cot_came[:, width:], jnp.zeros((TAIL, PAN), BF)), 0)
    hid, br1, n2, act, dg, out, gb2, gb2_send, vec_f = mlp_fwd_call(
        order, att, tok, proj_weight, row(proj_bias), row(scale_attn), row(ln2_gain), row(ln2_bias), fc1_weight,
        row(fc1_bias), fc2_weight, row(fc2_bias), row(scale_mlp), gout)
    gb2_p = swap(gb2_send, "core")
    act_p = swap(after(act, gb2_p), "core")
    mine_half = lambda g: lax.dynamic_slice_in_dim(g, core * (g.shape[1] // 2), g.shape[1] // 2, 1)
    att_p = swap(after(att, act_p), "core")
    n2_p = swap(after(n2, att_p), "core")
    out_came = swap(out[half:], "yl")

    send, keep = dw_near_call(order, [(act, act_p, mine_half(gb2), gb2_p)])
    fc2 = Scatter(orders, send, keep, "z")
    gpre, gpre_send, fc1_vec, ghid, gb1, gb1_send, gatt, vec_b = mlp_bwd_call(
        order, after(gb2, send), dg, fc1_weight, fc2_weight, hid, br1, gout, proj_weight, row(scale_attn), row(ln2_gain))
    gpre_p = swap(gpre_send, "core")
    gb1_p = swap(after(gb1_send, gpre_p), "core")
    done = fc2.near()
    send, keep = dw_far_call(orders["x"], after(n2, done), n2_p, gpre, gpre_p)
    fc1 = Scatter(orders, send, keep, "x")
    dq, dkv, part = att_bwd_call(q, kv0, kv0_p, after(gatt, send), att, lse0, 0, pairs)
    mine0, send0 = trip_call(order, dq, dkv, swap(part, "core"))
    done1, done2 = fc1.near(), fc2.far("x")
    trip0 = swap(send0, "core")
    dq, dkv, part = att_bwd_call(q, kv1, kv1_p, after(gatt, send0, done1, done2), att, lse1, 1, pairs)
    came1 = swap(part, "core")
    done1, done2 = fc1.far("z"), fc2.near()
    send, keep = dw_near_call(order, [(att, att_p, mine_half(gb1), gb1_p), (after(n1, done1, done2, dq), n1_p, mine0, trip0)])
    mid = Scatter(orders, send, keep, "z")
    mine1, send1 = trip_call(order, dq, dkv, after(came1, send))
    trip1 = swap(send1, "core")
    own, gtok_send, pos, cls8, vec_t, qv = tok_bwd_call(
        order, (mine0, mine1), (send0, send1), qkv_weight, tok, ghid, row(ln1_gain), mask_rows)
    gtok_came = swap(gtok_send, "yl")
    send, keep = dw_near_call(order, [(after(n1, pos), n1_p, mine1, trip1)], extra=(pos, vec_f, vec_b, vec_t, fc1_vec, qv))
    end = Scatter(orders, send, keep, "z")
    fc1.near(), mid.near(), end.near()
    mid.far("x"), end.far("x")
    mid.near(), end.near()
    fc2.far("y", fc1, mid, end)
    fc2.near()

    gtok_came = gtok_came.astype(F32)
    grad_patches = both(own, gtok_came[:half], 1) * (1.0 - mask_f[..., None])
    cls_part = both(cls8[0], gtok_came[half], 0)
    gone = (order, fc2.kept, fc2.came, cls_part.reshape(16, PAN))
    mine, gone, grad_pos = last_sum(*gone)
    fc2_g, fc1_g, proj_g, qkv_g, vec8, cls16 = finish(order, mine, swap(gone, "core"))
    sums = lax.dynamic_index_in_dim(vec8, core, 0, False)
    v = [sums[8 * j:8 * j + 8] for j in range(9)] + [sums[72:104], sums[104:120]]
    out_came = after(out_came, gtok_send)
    out_patches = both(out[:half], out_came[:half], 1)
    out_cls = both(out[2 * half], out_came[half], 0)
    return (out_patches, out_cls, grad_patches, cls16.reshape(2, width), v[8], grad_pos.T, v[6], v[7], qkv_g, v[10],
            proj_g, v[5], v[4], v[2], v[3], fc1_g, v[9], fc2_g, v[1], v[0])


def solution(mesh):
    fine = Mesh(mesh.devices.reshape([SIZES[a] for a in ALL]), ALL)
    img, blk = ("z", "yh", "x"), ("yl", "core")
    every = img + blk
    rep, crops, rows = P(), P(img, None), P(blk, img, None)
    vec, mat = P(every), P(every, None)
    return jax.shard_map(
        local,
        mesh=fine,
        in_specs=(rows, crops, P(blk, img), rep, P(blk, None)) + (rep,) * 14 + (rows, crops),
        out_specs=(rows, crops, rows, crops, vec, P(blk, img), vec, vec, mat, vec, mat, vec, vec, vec, vec, mat, vec, mat,
                   vec, vec),
        check_vma=False,
    )
```

```python
import functools
import itertools

import jax
import jax.numpy as jnp
from jax import lax
from jax.experimental import pallas as pl
from jax.experimental.pallas import tpu as pltpu
from jax.sharding import Mesh
from jax.sharding import PartitionSpec as P

EPS = 1e-06
BF = jnp.bfloat16
F32 = jnp.float32
TAIL = 16
INV_SQRT2 = 0.7071067811865476
INV_SQRT2PI = 0.3989422804014327
PAN = 128

ALL = ("z", "yh", "x", "yl", "core")
SIZES = {"z": 4, "yh": 2, "x": 4, "yl": 2, "core": 2}
Y = ("yh", "yl")


def nn(a, b):
    return jnp.dot(a, b, preferred_element_type=F32)


def nt(a, b):
    return lax.dot_general(a, b, (((1,), (1,)), ((), ())), preferred_element_type=F32)


def tn(a, b):
    return lax.dot_general(a, b, (((0,), (0,)), ((), ())), preferred_element_type=F32)


def params(mib):
    return pltpu.CompilerParams(vmem_limit_bytes=mib << 20)


def cost(macs, nbytes, exps=0):
    return pl.CostEstimate(flops=2 * macs, bytes_accessed=nbytes, transcendentals=exps)


def whole(shape):
    return pl.BlockSpec(shape, lambda *_: (0,) * len(shape))


def sd(shape, dtype=BF):
    return jax.ShapeDtypeStruct(shape, dtype)


def unit_of(x):
    center = x - jnp.mean(x, -1, keepdims=True)
    inv = lax.rsqrt(jnp.mean(center * center, -1, keepdims=True) + EPS)
    return center * inv, inv


def unit_grad(gu, unit, inv):
    return (gu - jnp.mean(gu, -1, keepdims=True) - unit * jnp.mean(gu * unit, -1, keepdims=True)) * inv


def norm_project_body(x_ref, gain_ref, bias_ref, w_ref, add_ref, normed_ref, out_ref):
    @pl.when(pl.program_id(0) == 0)
    def _():
        unit, _ = unit_of(x_ref[...])
        normed_ref[...] = (unit * gain_ref[...] + bias_ref[...]).astype(BF)

    out_ref[...] = (nn(normed_ref[...], w_ref[...]) + add_ref[...]).astype(BF)


def project_body(scale, x_ref, w_ref, add_ref, out_ref):
    out_ref[...] = ((nn(x_ref[...], w_ref[...]) + add_ref[...]) * scale).astype(BF)


def project_call(x, w, add, at, steps, norm=None, scale=1.0, tile=256):
    rows, width = x.shape
    mat, vec = whole((rows, width)), whole((1, width))
    out = pl.BlockSpec((rows, tile), lambda i: (0, i))
    shape = sd((rows, steps * tile))
    ins = [pl.BlockSpec((width, tile), lambda i: (0, at(i))), pl.BlockSpec((1, tile), lambda i: (0, at(i)))]
    common = dict(grid=(steps,), compiler_params=params(32),
                  cost_estimate=cost(rows * width * steps * tile, 2 * steps * (width * tile + rows * tile)))
    if norm is None:
        return pl.pallas_call(functools.partial(project_body, scale), in_specs=[mat] + ins, out_specs=out,
                              out_shape=shape, name="project", **common)(x, w, add)
    return pl.pallas_call(norm_project_body, in_specs=[mat, vec, vec] + ins, out_specs=[mat, out],
                          out_shape=[sd((rows, width)), shape], name="norm_project", **common)(x, *norm, w, add)


def half_mask(h):
    return (lax.broadcasted_iota(jnp.int32, (1, PAN), 1) // 64) == h


def att_fwd_body(np_, q_ref, ko_ref, vo_ref, kp_ref, vp_ref, *refs, chunk):
    out_ref, lse_ref = refs[-2:]
    rows = q_ref.shape[0]
    k_tail = ko_ref[np_:np_ + TAIL, :]
    v_cls = vo_ref[np_:np_ + 1, :].astype(F32)
    ko, kp = ko_ref[0:np_, :], kp_ref[0:np_, :]
    vo, vp = vo_ref[0:np_, :], vp_ref[0:np_, :]
    for r0 in range(0, rows, chunk):
        q = q_ref[r0:r0 + chunk, :]
        outs, lses = [], []
        for h in range(2):
            qh = jnp.where(half_mask(h), q, jnp.zeros_like(q))
            s1, s2 = nt(qh, ko), nt(qh, kp)
            sc = nt(qh, k_tail)[:, 0:1]
            top = jnp.maximum(jnp.maximum(jnp.max(s1, -1, keepdims=True), jnp.max(s2, -1, keepdims=True)), sc)
            p1, p2, pc = jnp.exp(s1 - top), jnp.exp(s2 - top), jnp.exp(sc - top)
            total = jnp.sum(p1, -1, keepdims=True) + jnp.sum(p2, -1, keepdims=True) + pc
            o = nn(p1.astype(BF), vo) + nn(p2.astype(BF), vp) + pc * v_cls
            outs.append(o / total)
            lses.append(top + jnp.log(total))
        out_ref[r0:r0 + chunk, :] = jnp.where(half_mask(0), outs[0], outs[1]).astype(BF)
        lse_ref[r0:r0 + chunk, :] = jnp.where(half_mask(0), lses[0], lses[1])


def att_fwd_call(q, kv, kv_p, at, pairs, into=None, chunk=264):
    rows, width = q.shape
    np_ = rows - TAIL
    col = lambda a: pl.BlockSpec((rows, PAN), lambda i: (0, a + i))
    ins = [col(at), col(0), col(pairs), col(0), col(pairs)]
    args = [q, kv, kv, kv_p, kv_p]
    if into is not None:
        ins.append(pl.BlockSpec(memory_space=pl.ANY))
        args.append(into)
    return pl.pallas_call(
        functools.partial(att_fwd_body, np_, chunk=chunk),
        grid=(pairs,),
        in_specs=ins,
        out_specs=[col(at), col(0)],
        out_shape=[sd((rows, width)), sd((rows, pairs * PAN), F32)],
        input_output_aliases={} if into is None else {5: 0},
        compiler_params=params(40),
        cost_estimate=cost(rows * 2 * np_ * PAN * 2 * pairs * 2, 2 * rows * PAN * pairs * 8, rows * 2 * np_ * 2 * pairs),
        name="att_fwd",
    )(*args)


def att_bwd_body(np_, q_ref, ko_ref, vo_ref, kp_ref, vp_ref, go_ref, o_ref, lse_ref, dq_ref, own_ref, part_ref):
    q, go = q_ref[...], go_ref[...]
    ko, kp = ko_ref[0:np_, :], kp_ref[0:np_, :]
    vo, vp = vo_ref[0:np_, :], vp_ref[0:np_, :]
    k_tail, v_tail = ko_ref[np_:np_ + TAIL, :], vo_ref[np_:np_ + TAIL, :]
    k_cls = k_tail[0:1].astype(F32)
    qt, gt = q.T, go.T
    qf, gf = q.astype(F32), go.astype(F32)
    prod = gf * o_ref[...].astype(F32)
    dq = dkc = dvc = None
    dk1, dk2, dv1, dv2 = [], [], [], []
    for h in range(2):
        mask = half_mask(h)
        qh = jnp.where(mask, q, jnp.zeros_like(q))
        gh = jnp.where(mask, go, jnp.zeros_like(go))
        delta = jnp.sum(jnp.where(mask, prod, 0.0), -1, keepdims=True)
        lse = lse_ref[:, 64 * h:64 * h + 1]
        qth, gth = qt[64 * h:64 * h + 64], gt[64 * h:64 * h + 64]
        dqh = None
        for k, v, dk, dv in ((ko, vo, dk1, dv1), (kp, vp, dk2, dv2)):
            p = jnp.exp(nt(qh, k) - lse)
            ds = (p * (nt(gh, v) - delta)).astype(BF)
            part = nn(ds, k)
            dqh = part if dqh is None else dqh + part
            dk.append(nn(qth, ds))
            dv.append(nn(gth, p.astype(BF)))
        pc = jnp.exp(nt(qh, k_tail)[:, 0:1] - lse)
        dsc = pc * (nt(gh, v_tail)[:, 0:1] - delta)
        dqh = (dqh + dsc * k_cls) * 0.125
        kc = jnp.sum(dsc * qf, 0, keepdims=True)
        vc = jnp.sum(pc * gf, 0, keepdims=True)
        dq = dqh if h == 0 else jnp.where(mask, dqh, dq)
        dkc = kc if h == 0 else jnp.where(mask, kc, dkc)
        dvc = vc if h == 0 else jnp.where(mask, vc, dvc)
    dq_ref[...] = dq.astype(BF)
    both = lambda parts: jnp.concatenate(parts, 0).T.astype(BF)
    own_ref[0:np_, 0:PAN] = both(dk1)
    own_ref[0:np_, PAN:2 * PAN] = both(dv1)
    part_ref[:, 0:PAN] = both(dk2)
    part_ref[:, PAN:2 * PAN] = both(dv2)
    first = lax.broadcasted_iota(jnp.int32, (TAIL, PAN), 0) == 0
    own_ref[np_:np_ + TAIL, 0:PAN] = jnp.where(first, dkc, 0.0).astype(BF)
    own_ref[np_:np_ + TAIL, PAN:2 * PAN] = jnp.where(first, dvc, 0.0).astype(BF)


def att_bwd_call(q, kv, kv_p, go, o, lse, at, pairs):
    rows = q.shape[0]
    np_ = rows - TAIL
    col = lambda a: pl.BlockSpec((rows, PAN), lambda i: (0, a + i))
    two = lambda n: pl.BlockSpec((n, 2 * PAN), lambda i: (0, i))
    return pl.pallas_call(
        functools.partial(att_bwd_body, np_),
        grid=(pairs,),
        in_specs=[col(at), col(0), col(pairs), col(0), col(pairs), col(at), col(at), col(0)],
        out_specs=[col(0), two(rows), two(np_)],
        out_shape=[sd((rows, pairs * PAN)), sd((rows, pairs * 2 * PAN)), sd((np_, pairs * 2 * PAN))],
        compiler_params=params(48),
        cost_estimate=cost(rows * 2 * np_ * PAN * 5 * pairs * 2, 2 * rows * PAN * pairs * 16, rows * 2 * np_ * 2 * pairs),
        name="att_bwd",
    )(q, kv, kv, kv_p, kv_p, go, o, lse)


def trip_body(np_, pairs, order_ref, dq_ref, own_ref, came_ref, mine_ref, send_ref):
    core = order_ref[0]
    n = pairs // 2 * PAN
    for out_ref, side in ((mine_ref, core), (send_ref, 1 - core)):
        out_ref[:, 0:n] = dq_ref[:, pl.ds(pl.multiple_of(side * n, PAN), n)]
        for j in range(pairs // 2):
            for kind in range(2):
                src = pl.ds(pl.multiple_of(side * 2 * n + (2 * j + kind) * PAN, PAN), PAN)
                dst = slice((1 + kind) * n + j * PAN, (1 + kind) * n + (j + 1) * PAN)
                out_ref[0:np_, dst] = (own_ref[0:np_, src].astype(F32) + came_ref[:, src].astype(F32)).astype(BF)
                out_ref[np_:, dst] = own_ref[np_:, src]


def trip_call(order, dq, own, came):
    rows, n = dq.shape
    np_ = rows - TAIL
    shape = sd((rows, n // 2 * 3))
    return pl.pallas_call(
        functools.partial(trip_body, np_, n // PAN),
        grid_spec=pltpu.PrefetchScalarGridSpec(
            num_scalar_prefetch=1, grid=(1,),
            in_specs=[whole(a.shape) for a in (dq, own, came)],
            out_specs=[whole(shape.shape)] * 2),
        out_shape=[shape, shape],
        compiler_params=params(24),
        cost_estimate=cost(0, 2 * rows * n * 8),
        name="trip",
    )(order, dq, own, came)


def mlp_fwd_body(order_ref, att_ref, tok_ref, wp_ref, bp_ref, sa_ref, gain_ref, bias_ref, w1_ref, b1_ref, w2_ref, b2_ref,
                 sm_ref, gout_ref, hid_ref, br1_ref, n2_ref, act_ref, dg_ref, out_ref, gb2_ref, gb2m_ref, gb2s_ref, vec_ref, acc_ref):
    i = pl.program_id(0)

    @pl.when(i == 0)
    def _():
        br1 = nn(att_ref[...], wp_ref[...]) + bp_ref[...]
        br1_ref[...] = br1.astype(BF)
        hid = tok_ref[...] + sa_ref[...] * br1
        hid_ref[...] = hid
        unit, _ = unit_of(hid)
        n2_ref[...] = (unit * gain_ref[...] + bias_ref[...]).astype(BF)

    pre = nn(n2_ref[...], w1_ref[...]) + b1_ref[...]
    cdf = 0.5 + 0.5 * lax.erf(pre * INV_SQRT2)
    act = (pre * cdf).astype(BF)
    act_ref[...] = act
    dg_ref[...] = (cdf + pre * (jnp.exp(-0.5 * pre * pre) * INV_SQRT2PI)).astype(BF)
    part = nn(act, w2_ref[...])

    @pl.when(i == 0)
    def _():
        acc_ref[...] = part

    @pl.when(i > 0)
    def _():
        acc_ref[...] += part

    @pl.when(i == pl.num_programs(0) - 1)
    def _():
        br2 = acc_ref[...] + b2_ref[...]
        out_ref[...] = (hid_ref[...] + sm_ref[...] * br2).astype(BF)
        gout = gout_ref[...].astype(F32)
        gb2 = (sm_ref[...] * gout).astype(BF)
        gb2_ref[...] = gb2
        vec_ref[0:1, :] = jnp.sum(gout * br2, 0, keepdims=True)
        vec_ref[1:2, :] = jnp.sum(gb2.astype(F32), 0, keepdims=True)
        n = gb2s_ref.shape[1]
        gb2m_ref[...] = gb2_ref[:, pl.ds(pl.multiple_of(order_ref[0] * n, PAN), n)]
        gb2s_ref[...] = gb2_ref[:, pl.ds(pl.multiple_of((1 - order_ref[0]) * n, PAN), n)]


def mlp_fwd_call(order, att, tok, wp, bp, sa, gain, bias, w1, b1, w2, b2, sm, gout, tile=512):
    rows, width = tok.shape
    ff = w1.shape[1]
    mat, vec = whole((rows, width)), whole((1, width))
    col = pl.BlockSpec((rows, tile), lambda i, c: (0, i))
    return pl.pallas_call(
        mlp_fwd_body,
        grid_spec=pltpu.PrefetchScalarGridSpec(
            num_scalar_prefetch=1,
            grid=(ff // tile,),
            in_specs=[mat, mat, whole((width, width)), vec, vec, vec, vec,
                      pl.BlockSpec((width, tile), lambda i, c: (0, i)), pl.BlockSpec((1, tile), lambda i, c: (0, i)),
                      pl.BlockSpec((tile, width), lambda i, c: (i, 0)), vec, vec, mat],
            out_specs=[mat, mat, mat, col, col, mat, mat] + [whole((rows, width // 2))] * 2 + [whole((8, width))],
            scratch_shapes=[pltpu.VMEM((rows, width), F32)]),
        out_shape=[sd((rows, width), F32), sd((rows, width)), sd((rows, width)), sd((rows, ff)), sd((rows, ff)),
                   sd((rows, width)), sd((rows, width))] + [sd((rows, width // 2))] * 2 + [sd((8, width), F32)],
        compiler_params=params(44),
        cost_estimate=cost(rows * width * (2 * ff + width), 2 * (2 * width * ff + 2 * rows * ff + 6 * rows * width), rows * ff),
        name="mlp_fwd",
    )(order, att, tok, wp, bp, sa, gain, bias, w1, b1, w2, b2, sm, gout)


def mlp_bwd_step(gb2_ref, dg_ref, w1_ref, w2_ref, gpre_ref, b1_ref, at):
    gpre = (nt(gb2_ref[...], w2_ref[...]) * dg_ref[...].astype(F32)).astype(BF)
    gpre_ref[...] = gpre
    b1_ref[0:1, at] = jnp.sum(gpre.astype(F32), 0, keepdims=True)
    return nt(gpre, w1_ref[...])


def mlp_bwd_first_body(order_ref, gb2_ref, dg_ref, w1_ref, w2_ref, gpre_ref, b1_ref, acc_ref):
    i = pl.program_id(0)
    part = mlp_bwd_step(gb2_ref, dg_ref, w1_ref, w2_ref, gpre_ref, b1_ref, slice(None))

    @pl.when(i == 0)
    def _():
        acc_ref[...] = part

    @pl.when(i > 0)
    def _():
        acc_ref[...] += part


def mlp_bwd_second_body(order_ref, gb2_ref, dg_ref, w1_ref, w2_ref, first_ref, b1_first_ref, hid_ref, br1_ref, gout_ref,
                        wp_ref, sa_ref, gain_ref, gpre_ref, b1_ref, ghid_ref, gb1_ref, gb1m_ref, gb1s_ref, gatt_ref,
                        vec_ref, acc_ref):
    i = pl.program_id(0)
    core = order_ref[0]
    tile, half = gpre_ref.shape[1], b1_first_ref.shape[1]
    part = mlp_bwd_step(gb2_ref, dg_ref, w1_ref, w2_ref, gpre_ref, b1_ref,
                        pl.ds(pl.multiple_of(core * half + i * tile, PAN), tile))

    @pl.when(i == 0)
    def _():
        acc_ref[...] = first_ref[...] + part
        b1_ref[0:1, pl.ds(pl.multiple_of((1 - core) * half, PAN), half)] = b1_first_ref[0:1, :]

    @pl.when(i > 0)
    def _():
        acc_ref[...] += part

    @pl.when(i == pl.num_programs(0) - 1)
    def _():
        unit, inv = unit_of(hid_ref[...])
        gn = acc_ref[...]
        vec_ref[0:1, :] = jnp.sum(gn * unit, 0, keepdims=True)
        vec_ref[1:2, :] = jnp.sum(gn, 0, keepdims=True)
        ghid = gout_ref[...].astype(F32) + unit_grad(gn * gain_ref[...], unit, inv)
        ghid_ref[...] = ghid
        vec_ref[2:3, :] = jnp.sum(ghid * br1_ref[...].astype(F32), 0, keepdims=True)
        gb1 = (sa_ref[...] * ghid).astype(BF)
        gb1_ref[...] = gb1
        vec_ref[3:4, :] = jnp.sum(gb1.astype(F32), 0, keepdims=True)
        n = gb1s_ref.shape[1]
        gb1m_ref[...] = gb1_ref[:, pl.ds(pl.multiple_of(core * n, PAN), n)]
        gb1s_ref[...] = gb1_ref[:, pl.ds(pl.multiple_of((1 - core) * n, PAN), n)]
        gatt_ref[...] = nt(gb1, wp_ref[...]).astype(BF)


def mlp_bwd_specs(rows, width, ff, tile, mine):
    half = ff // tile // 2
    at = lambda i, c: i + half * (c[0] if mine else 1 - c[0])
    col = lambda n: pl.BlockSpec((n, tile), lambda i, c: (0, at(i, c)))
    return half, [whole((rows, width)), col(rows), col(width), pl.BlockSpec((tile, width), lambda i, c: (at(i, c), 0))]


def mlp_bwd_first_call(order, gb2, dg, w1, w2, tile=512):
    rows, width = gb2.shape
    ff = w1.shape[1]
    half, ins = mlp_bwd_specs(rows, width, ff, tile, False)
    return pl.pallas_call(
        mlp_bwd_first_body,
        grid_spec=pltpu.PrefetchScalarGridSpec(
            num_scalar_prefetch=1, grid=(half,), in_specs=ins,
            out_specs=[pl.BlockSpec((rows, tile), lambda i, c: (0, i)), pl.BlockSpec((8, tile), lambda i, c: (0, i)),
                       whole((rows, width))]),
        out_shape=[sd((rows, ff // 2)), sd((8, ff // 2), F32), sd((rows, width), F32)],
        compiler_params=params(40),
        cost_estimate=cost(rows * width * ff, 2 * (width * ff + rows * ff)),
        name="mlp_bwd_first",
    )(order, gb2, dg, w1, w2)


def mlp_bwd_second_call(order, gb2, dg, w1, w2, first, b1_first, hid, br1, gout, wp, sa, gain, tile=512):
    rows, width = hid.shape
    ff = w1.shape[1]
    half, ins = mlp_bwd_specs(rows, width, ff, tile, True)
    mat, vec, halfm = whole((rows, width)), whole((1, width)), whole((rows, width // 2))
    return pl.pallas_call(
        mlp_bwd_second_body,
        grid_spec=pltpu.PrefetchScalarGridSpec(
            num_scalar_prefetch=1, grid=(half,),
            in_specs=ins + [mat, whole((8, ff // 2)), mat, mat, mat, whole((width, width)), vec, vec],
            out_specs=[pl.BlockSpec((rows, tile), lambda i, c: (0, i)), whole((8, ff)), mat, mat, halfm, halfm, mat,
                       whole((8, width))],
            scratch_shapes=[pltpu.VMEM((rows, width), F32)]),
        out_shape=[sd((rows, ff // 2)), sd((8, ff), F32), sd((rows, width), F32), sd((rows, width)),
                   sd((rows, width // 2)), sd((rows, width // 2)), sd((rows, width)), sd((8, width), F32)],
        compiler_params=params(44),
        cost_estimate=cost(rows * width * (ff + width), 2 * (width * ff + rows * ff + 6 * rows * width)),
        name="mlp_bwd_second",
    )(order, gb2, dg, w1, w2, first, b1_first, hid, br1, gout, wp, sa, gain)


def vector_panels(vectors, z):
    r = lax.broadcasted_iota(jnp.int32, (256, 1), 0)
    device = jnp.where(r % 16 < 2, r // 16 * 2 + r % 16, -1)
    total, at = None, 0
    for vector in vectors:
        n = vector.shape[1] // 4
        per = n // 32
        lane = lax.broadcasted_iota(jnp.int32, (1, n), 1)
        spread = jnp.where(lane // per == device, vector[:, z * n:(z + 1) * n], 0.0).astype(BF)
        pick_r = lax.broadcasted_iota(jnp.int32, (n, PAN), 0)
        pick_c = lax.broadcasted_iota(jnp.int32, (n, PAN), 1)
        part = nn(spread, jnp.where(pick_r % per + at == pick_c, 1.0, 0.0).astype(BF))
        total = part if total is None else total + part
        at += per
    return total.astype(BF)


def dw_body(jobs, axis, order_ref, *refs):
    send_ref, keep_ref = refs[-2:]
    i = pl.program_id(0)
    done, at, base = [], 0, 0
    for rows, panels in jobs:
        a0, a1, g0, g1 = (ref[...] for ref in refs[at:at + 4])
        done.append(((tn(a0, g0) + tn(a1, g1)).astype(BF), base, rows))
        at, base = at + 4, base + panels

    def write(ref, place, xs):
        for value, first, rows in done:
            n = value.shape[1] // PAN
            for yh, x, yl, rg, pc in itertools.product(range(2), xs, range(2), range(rows // 16), range(n)):
                r0 = ((yh * 4 + x) * 2 + yl) * rows + rg * 16
                ref[place(yh, x, yl) + (first + rg * n + pc,)] = value[r0:r0 + 16, pc * PAN:(pc + 1) * PAN]

    if axis == "z":
        place = lambda yh, x, yl: (0, yh, x, yl)
        pl.when(i < 2)(lambda: write(send_ref, place, range(4)))
        pl.when(i >= 2)(lambda: write(keep_ref, place, range(4)))
    else:
        for target in range(4):
            slot = order_ref[5 + target]
            pl.when(slot < 2)(lambda: write(send_ref, lambda yh, x, yl: (slot, i, yh, yl), (target,)))
            pl.when(slot >= 2)(lambda: write(keep_ref, lambda yh, x, yl: (slot - 2, i, yh, yl), (target,)))


def dw_call(order, axis, jobs):
    ins, args, shapes, macs = [], [], [], 0
    at = (lambda i, c: c[1 + i]) if axis == "z" else (lambda i, c: i)
    for a0, a1, g0, g1 in jobs:
        rows, k = a0.shape
        n = g0.shape[1]
        lhs = pl.BlockSpec((rows, k // 4), lambda i, c: (0, at(i, c)))
        ins += [lhs, lhs, whole((rows, n)), whole((rows, n))]
        args += [a0, a1, g0, g1]
        shapes.append((k // 64, k // 1024 * (n // PAN)))
        macs += 2 * rows * k * n
    panels = sum(p for _, p in shapes)
    if axis == "z":
        out = sd((2, 2, 4, 2, panels, 16, PAN))
        block = lambda f: pl.BlockSpec((1,) + out.shape[1:], lambda i, c: (f(i),) + (0,) * 6)
        outs = [block(lambda i: jnp.minimum(i, 1)), block(lambda i: jnp.maximum(i - 2, 0))]
    else:
        out = sd((2, 4, 2, 2, panels, 16, PAN))
        outs = [whole(out.shape)] * 2
    return pl.pallas_call(
        functools.partial(dw_body, tuple(shapes), axis),
        grid_spec=pltpu.PrefetchScalarGridSpec(num_scalar_prefetch=1, grid=(4,), in_specs=ins, out_specs=outs),
        out_shape=[out, out],
        compiler_params=params(48),
        cost_estimate=cost(macs, 2 * sum(a.size for a in args) + 4 * out.size),
        name="dw",
    )(order, *args)


def tok_bwd_body(half, order_ref, g0_mine, g0_send, g1_mine, g1_send, *refs):
    w0, w1 = refs[0:3], refs[3:6]
    (tok_ref, ghid_ref, gain_ref, mask_ref, vf_ref, vb_ref, b1_ref, own_ref, send_ref, cls_ref, *panel_refs,
     qv_ref, pos_ref, vecs_ref, acc_ref) = refs[6:]
    i = pl.program_id(0)
    width = tok_ref.shape[1]
    core = order_ref[0]
    first = 0
    for step, (g_ref, ws) in enumerate(((g0_mine, w0), (g0_send, w0), (g1_mine, w1), (g1_send, w1))):
        n = ws[0].shape[1]
        side = core if step % 2 == 0 else 1 - core

        @pl.when(i == step)
        def _():
            part = sum(nt(g_ref[:, j * n:(j + 1) * n], w[...]) for j, w in enumerate(ws))
            if step == 0:
                acc_ref[...] = part
            else:
                acc_ref[...] += part
            sums = jnp.sum(g_ref[...].astype(F32), 0, keepdims=True)
            at = pl.multiple_of(first + side * n, PAN)
            qv_ref[0:1, pl.ds(at, n)] = sums[:, 0:n]
            qv_ref[0:1, pl.ds(width + at, n)] = sums[:, 2 * n:]

        if step == 1:
            first = 2 * n

    @pl.when(i == 3)
    def _():
        unit, inv = unit_of(tok_ref[...])
        gn = acc_ref[...]
        gtok = ghid_ref[...] + unit_grad(gn * gain_ref[...], unit, inv)
        own_ref[...] = gtok[0:half]
        send_ref[...] = gtok[half:].astype(BF)
        cls_ref[...] = gtok[2 * half:2 * half + 8]
        pos_ref[...] = gtok[0:2 * half].T.astype(BF)
        column = lambda v: jnp.sum(v, 0, keepdims=True)
        vectors = [vf_ref[0:1, :], vf_ref[1:2, :]] + [vb_ref[j:j + 1, :] for j in range(4)]
        vectors += [column(gn * unit), column(gn), column(gtok * mask_ref[:, 0:1].astype(F32)), b1_ref[0:1, :],
                    qv_ref[0:1, :]]
        for z in range(4):
            vecs_ref[z] = vector_panels(vectors, z)
        for slot in range(4):
            ref = panel_refs[slot // 2]
            target = order_ref[1 + slot]
            for z, yh, part in itertools.product(range(4), range(2), range(2)):
                rows = pl.ds(pl.multiple_of(z * 256 + (yh * 4 + target) * 32 + part * 16, 16), 16)
                for side, pc in itertools.product(range(2), range(2)):
                    yl = order_ref[9] if side == 0 else 1 - order_ref[9]
                    c0 = side * half + pc * PAN
                    ref[slot % 2, z, yh, yl, part * 2 + pc] = pos_ref[rows, c0:c0 + PAN]
                chip = pl.ds(pl.multiple_of((yh * 4 + target) * 32 + part * 16, 16), 16)
                ref[slot % 2, z, yh, part, 4] = vecs_ref[z, chip, :]


def tok_bwd_call(order, gs, w, tok, ghid, gain, mask, vf, vb, b1):
    rows, width = tok.shape
    half = (rows - TAIL) // 2
    mat, vec = whole((rows, width)), whole((1, width))
    n0, n1 = gs[0].shape[1] // 3, gs[2].shape[1] // 3
    panels = (2, 4, 2, 2, 5, 16, PAN)
    side = lambda i, c: jnp.where(i % 2 == 0, c[0], 1 - c[0])
    ws = [pl.BlockSpec((pl.Element(width), pl.Element(n0)),
                       lambda i, c, j=j: (0, pl.multiple_of(j * width + side(jnp.minimum(i, 1), c) * n0, PAN))) for j in range(3)]
    ws += [pl.BlockSpec((pl.Element(width), pl.Element(n1)),
                        lambda i, c, j=j: (0, pl.multiple_of(j * width + 2 * n0 + side(jnp.maximum(i, 2), c) * n1, PAN)))
           for j in range(3)]
    return pl.pallas_call(
        functools.partial(tok_bwd_body, half),
        grid_spec=pltpu.PrefetchScalarGridSpec(
            num_scalar_prefetch=1,
            grid=(4,),
            in_specs=[whole(g.shape) for g in gs] + ws + [mat, mat, vec, whole((rows, PAN))]
            + [whole(v.shape) for v in (vf, vb, b1)],
            out_specs=[whole((half, width)), whole((half + TAIL, width)), whole((8, width))] + [whole(panels)] * 2,
            scratch_shapes=[pltpu.VMEM((8, 2 * width), F32), pltpu.VMEM((width, 2 * half), BF),
                            pltpu.VMEM((4, 256, PAN), BF), pltpu.VMEM((rows, width), F32)]),
        out_shape=[sd((half, width), F32), sd((half + TAIL, width)), sd((8, width), F32)] + [sd(panels)] * 2,
        compiler_params=params(48),
        cost_estimate=cost(rows * width * 3 * width, 2 * (3 * width * width + 8 * rows * width)),
        name="tok_bwd",
    )(order, *gs, *[w] * 6, tok, ghid, gain, mask, vf, vb, b1)


def near_sum_body(keep_ref, came_ref, kept_ref, send_ref):
    kept_ref[...] = keep_ref[0].astype(F32) + came_ref[0].astype(F32)
    send_ref[...] = (keep_ref[1].astype(F32) + came_ref[1].astype(F32)).astype(BF)


def near_sum(keep, came, parts=4):
    shape = keep.shape
    m = keep.size // (2 * 16 * PAN)
    flat = lambda a: a.reshape(2, m, 16, PAN)
    parts = parts if m % parts == 0 and m >= 16 else 1
    two = pl.BlockSpec((2, m // parts, 16, PAN), lambda i: (0, i, 0, 0))
    one = pl.BlockSpec((m // parts, 16, PAN), lambda i: (i, 0, 0))
    kept, send = pl.pallas_call(
        near_sum_body, grid=(parts,), in_specs=[two, two], out_specs=[one, one],
        out_shape=[sd((m, 16, PAN), F32), sd((m, 16, PAN))],
        compiler_params=params(24), cost_estimate=cost(0, keep.size * 6), name="near_sum",
    )(flat(keep), flat(came))
    return kept.reshape(shape[1:]), send.reshape(shape[1:])


def far_sum_body(labels, axis, counts, order_ref, *refs):
    ins, outs = refs[:-2], refs[-2:]
    for slot in range(4):
        target = order_ref[1 + slot]
        place = {"y": {"yh": target // 2, "yl": target % 2}}.get(axis, {axis: target})
        where = tuple(place.get(label, slice(None)) for label in labels)
        out = outs[slot // 2]
        at, j = 0, 0
        for count in counts:
            n = ins[j].shape[-3]
            total = ins[j][where].astype(F32)
            for came in ins[j + 1:j + count]:
                total = total + came[where].astype(F32)
            out[(slot % 2,) + (slice(None),) * (total.ndim - 3) + (slice(at, at + n),)] = total.astype(out.dtype)
            at += n
            j += count


def far_sum(order, items, labels, axis):
    gone = ("yh", "yl") if axis == "y" else (axis,)
    left = [l for l in labels if l not in gone]
    panels = sum(item[0].shape[-3] for item in items)
    out = (2,) + tuple(SIZES[l] for l in left) + (panels, 16, PAN)
    args = [a for item in items for a in item]
    outs = [sd(out), sd(out, F32)]
    return left, pl.pallas_call(
        functools.partial(far_sum_body, labels, axis, tuple(len(item) for item in items)),
        grid_spec=pltpu.PrefetchScalarGridSpec(
            num_scalar_prefetch=1, grid=(1,),
            in_specs=[whole(a.shape) for a in args],
            out_specs=[whole(o.shape) for o in outs]),
        out_shape=outs,
        compiler_params=params(24), cost_estimate=cost(0, sum(a.size for a in args) * 6), name="far_sum",
    )(order, *args)


def last_sum_body(counts, order_ref, *refs):
    ins, (cls_ref, mine_ref, gone_ref, pos_ref, tot_ref) = refs[:-5], refs[-5:]
    core = order_ref[0]
    at, j = 0, 0
    for count in counts:
        total = ins[j][...]
        for came in ins[j + 1:j + count]:
            total = total + came[...].astype(F32)
        tot_ref[at:at + total.shape[0]] = total
        at += total.shape[0]
        j += count
    at = 0

    def put(panel, start):
        nonlocal at
        for ref, side in ((mine_ref, core), (gone_ref, 1 - core)):
            ref[at] = tot_ref[panel, pl.ds(pl.multiple_of(start(side), 8), 8), :]
        at += 1

    for rg, pc, part in itertools.product(range(2), range(4), range(2)):
        for ref, side in ((mine_ref, core), (gone_ref, 1 - core)):
            ref[at] = tot_ref[(2 * side + rg) * 4 + pc, 8 * part:8 * part + 8, :]
        at += 1
    for panel in range(16, 48):
        put(panel, lambda side: side * 8)
    mine_ref[at] = tot_ref[52, 0:8, :]
    gone_ref[at] = tot_ref[52, 0:8, :]
    for part in range(2):
        mine_ref[at + 1 + part] = cls_ref[8 * part:8 * part + 8, :]
        gone_ref[at + 1 + part] = cls_ref[8 * part:8 * part + 8, :]
    for rg, pc in itertools.product(range(2), range(2)):
        pos_ref[16 * rg:16 * rg + 16, pc * PAN:(pc + 1) * PAN] = tot_ref[48 + rg * 2 + pc]


SWAPPED = 16 + 32 + 3


def last_sum(order, items, cls16):
    shape = sd((SWAPPED, 8, PAN), F32)
    args = [a for item in items for a in item] + [cls16]
    panels = sum(item[0].shape[0] for item in items)
    return pl.pallas_call(
        functools.partial(last_sum_body, tuple(len(item) for item in items)),
        grid_spec=pltpu.PrefetchScalarGridSpec(
            num_scalar_prefetch=1, grid=(1,),
            in_specs=[whole(a.shape) for a in args],
            out_specs=[whole(shape.shape), whole(shape.shape), whole((32, 256))],
            scratch_shapes=[pltpu.VMEM((panels, 16, PAN), F32)]),
        out_shape=[shape, shape, sd((32, 256), F32)],
        compiler_params=params(24), cost_estimate=cost(0, panels * 2048 * 10), name="last_sum",
    )(order, *args)


def finish_body(order_ref, mine_ref, came_ref, fc2_ref, fc1_ref, proj_ref, qkv_ref, vec_ref, cls_ref):
    first = order_ref[0] == 0
    at = 0

    def halves():
        nonlocal at
        mine, came = mine_ref[at], came_ref[at]
        at += 1
        return jnp.where(first, mine, came), jnp.where(first, came, mine)

    for rg, pc, part in itertools.product(range(2), range(4), range(2)):
        r0 = rg * 16 + part * 8
        for h, value in enumerate(halves()):
            fc2_ref[r0:r0 + 8, 512 * h + pc * PAN:512 * h + (pc + 1) * PAN] = value
    for pc in range(16):
        for h, value in enumerate(halves()):
            fc1_ref[:, 2048 * h + pc * PAN:2048 * h + (pc + 1) * PAN] = value
    for pc in range(4):
        for h, value in enumerate(halves()):
            proj_ref[:, 512 * h + pc * PAN:512 * h + (pc + 1) * PAN] = value
    for c0, per in ((0, 3), (768, 1)):
        for kind, pc in itertools.product(range(3), range(per)):
            for h, value in enumerate(halves()):
                at0 = kind * 1024 + c0 + (h * per + pc) * PAN
                qkv_ref[:, at0:at0 + PAN] = value
    vec_ref[...] = mine_ref[at] + came_ref[at]
    for part in range(2):
        cls_ref[8 * part:8 * part + 8, :] = mine_ref[at + 1 + part] + came_ref[at + 1 + part]


def finish(order, mine, came):
    outs = [(32, 1024), (8, 4096), (8, 1024), (8, 3072), (8, PAN), (16, PAN)]
    return pl.pallas_call(
        finish_body,
        grid_spec=pltpu.PrefetchScalarGridSpec(
            num_scalar_prefetch=1, grid=(1,), in_specs=[whole(mine.shape)] * 2, out_specs=[whole(s) for s in outs]),
        out_shape=[sd(s, F32) for s in outs],
        compiler_params=params(24), cost_estimate=cost(0, mine.size * 16), name="finish",
    )(order, mine, came)


def swap(x, axis):
    return lax.ppermute(x, axis, [(0, 1), (1, 0)])


def after(x, *others):
    return lax.optimization_barrier((x,) + others)[0] if others else x


def partners(axis, turn):
    pairs = []
    for z, yh, x, yl, core in itertools.product(*(range(SIZES[a]) for a in ALL)):
        at = {"z": z, "y": yh * 2 + yl, "x": x}
        flat = lambda p: (((p["z"] * 2 + p["y"] // 2) * 4 + p["x"]) * 2 + p["y"] % 2) * 2 + core
        there = dict(at)
        there[axis] ^= 1 if core == turn else 3
        pairs.append((flat(at), flat(there)))
    return pairs


def pass_on(x, axis, turn):
    return lax.ppermute(x, ALL, partners(axis, turn))


def order_of(axis):
    me = lax.axis_index("yh") * 2 + lax.axis_index("yl") if axis == "y" else lax.axis_index(axis)
    first = jnp.where(lax.axis_index("core") == 0, 1, 3)
    targets = [me ^ first, me ^ 2, me, me ^ first ^ 2]
    places = [sum(jnp.where(t == want, at, 0) for at, t in enumerate(targets)) for want in range(4)]
    return jnp.stack([lax.axis_index("core")] + targets + places + [lax.axis_index("yl")]).astype(jnp.int32)


class Scatter:
    def __init__(self, orders, sums, axis, *others):
        self.orders, self.axis = orders, axis
        self.labels = {"z": ["yh", "x", "yl"], "x": ["z", "yh", "yl"]}[axis]
        self.begin(sums, others)

    def begin(self, sums, others):
        send, self.keep = sums
        self.came = pass_on(after(send, *others), self.axis, 0)

    def near(self, *others):
        kept, send = near_sum(self.keep, self.came)
        self.item = [kept, pass_on(after(send, *others), self.axis, 1)]

    def far(self, axis, *others, merge=()):
        items = [s.item for s in (self,) + tuple(merge)]
        self.labels, sums = far_sum(self.orders[axis], items, self.labels, axis)
        self.axis = axis
        self.begin(sums, others)


def local(patches, cls_tokens, patch_masks, mask_token, pos_embed, ln1_gain, ln1_bias, qkv_weight, qv_bias, proj_weight,
          proj_bias, scale_attn, ln2_gain, ln2_bias, fc1_weight, fc1_bias, fc2_weight, fc2_bias, scale_mlp, cot_patches,
          cot_cls):
    half, _, width = patches.shape
    core, yl = lax.axis_index("core"), lax.axis_index("yl")
    row = lambda v: v.reshape(1, -1)
    sides = lambda a: (jnp.where(yl == 0, a[:, 0], a[:, 1]), jnp.where(yl == 0, a[:, 1], a[:, 0]))
    both = lambda mine, other, axis: jnp.where(yl == 0, jnp.stack((mine, other), axis), jnp.stack((other, mine), axis))
    pad = jnp.zeros((TAIL - 1, width), BF)
    orders = {a: order_of(a) for a in "zxy"}
    order = orders["z"]

    mask_f = patch_masks.astype(F32)
    mask3 = patch_masks[..., None]
    mixed = jnp.where(mask3 != 0, mask_token, patches)
    own, send = sides(mixed)
    came = swap(send, "yl")
    pos_came = lax.ppermute(pos_embed, Y, [(0, 3), (3, 0), (1, 2), (2, 1)])
    cls_row = jnp.where(yl == 0, cls_tokens[0:1], cls_tokens[1:2])
    tok = jnp.concatenate((own.astype(F32) + pos_embed.astype(F32), came.astype(F32) + pos_came.astype(F32),
                           cls_row.astype(F32), pad.astype(F32)), 0)

    add = row(jnp.concatenate((qv_bias[:width], jnp.zeros((width,), F32), qv_bias[width:])))
    n1, kv0 = project_call(tok, qkv_weight, add, lambda i: 4 + i % 3 + i // 3 * 4, 6, norm=(row(ln1_gain), row(ln1_bias)))
    kv0_p = swap(kv0, "core")
    kv1 = project_call(after(n1, kv0), qkv_weight, add, lambda i: 7 + i * 4, 2)
    q = project_call(after(n1, kv1), qkv_weight, add, lambda i: i, 4, scale=0.125)
    kv1_p = swap(after(kv1, kv0_p), "core")

    mask_own, mask_send = sides(mask_f)
    cot_own, cot_send = sides(jnp.where(mask3 != 0, cot_patches, jnp.zeros_like(cot_patches)))
    lanes = lambda m: jnp.broadcast_to(m.astype(BF)[:, None], (half, PAN))
    cot_came = swap(after(jnp.concatenate((cot_send, lanes(mask_send)), 1), came, q), "yl")

    att, lse0 = att_fwd_call(after(q, kv0_p), kv0, kv0_p, 0, 6)
    n1_p = swap(after(n1, kv1_p), "core")
    att, lse1 = att_fwd_call(after(q, cot_came, n1_p), kv1, kv1_p, 6, 2, into=att)
    cot_came = after(cot_came, att)
    att_p = swap(after(att, n1_p), "core")
    cls_cot = jnp.where(yl == 0, cot_cls[0:1], cot_cls[1:2]) * (core == 0).astype(BF)
    gout = jnp.concatenate((cot_own, cot_came[:, :width], cls_cot, pad), 0)
    mask_rows = jnp.concatenate((lanes(mask_own), cot_came[:, width:], jnp.zeros((TAIL, PAN), BF)), 0)
    hid, br1, n2, act, dg, out, gb2, gb2_mine, gb2_send, vec_f = mlp_fwd_call(
        order, att, tok, proj_weight, row(proj_bias), row(scale_attn), row(ln2_gain), row(ln2_bias), fc1_weight,
        row(fc1_bias), fc2_weight, row(fc2_bias), row(scale_mlp), gout)

    act_p = swap(after(act, att_p), "core")
    gb2_p = swap(gb2_send, "core")
    gpre_send, b1_first, first = mlp_bwd_first_call(order, gb2, dg, fc1_weight, fc2_weight)
    gpre_p = swap(after(gpre_send, act_p, gb2_p), "core")
    n2_p = swap(after(n2, act_p, gb2_p, gpre_send), "core")
    sums = dw_call(order, "z", [(act, act_p, gb2_mine, gb2_p)])
    fc2 = Scatter(orders, sums, "z", gpre_p, n2_p)
    out_came = swap(after(out[half:], gpre_p, n2_p, sums[0]), "yl")
    gpre, fc1_vec, ghid, gb1, gb1_mine, gb1_send, gatt, vec_b = mlp_bwd_second_call(
        order, after(gb2, sums[0]), dg, fc1_weight, fc2_weight, first, b1_first, hid, br1, gout, proj_weight,
        row(scale_attn), row(ln2_gain))
    gb1_p = swap(gb1_send, "core")
    sums = dw_call(orders["x"], "x", [(n2, n2_p, gpre, gpre_p), (att, att_p, gb1_mine, gb1_p)])
    fc1 = Scatter(orders, sums, "x", fc2.came, out_came)
    fc2.near(sums[0])
    dq0, dkv0, part0 = att_bwd_call(q, kv0, kv0_p, after(gatt, sums[0], fc2.item[0]), att, lse0, 0, 6)
    part0_p = swap(after(part0, fc1.came, fc2.item[1]), "core")
    fc1.near(part0)
    fc2.far("x", part0)
    dq1, dkv1, part1 = att_bwd_call(q, kv1, kv1_p, after(gatt, fc1.item[0], fc2.keep), att, lse1, 6, 2)
    mine0, send0 = trip_call(order, dq0, dkv0, after(part0_p, part1))
    part1_p = swap(after(part1, part0_p), "core")
    trip0_p = swap(after(send0, part1_p), "core")
    mine1, send1 = trip_call(order, dq1, dkv1, after(part1_p, send0))
    trip1_p = swap(after(send1, trip0_p), "core")
    sums = dw_call(order, "z", [(after(n1, trip0_p), n1_p, mine0, trip0_p), (n1, n1_p, mine1, trip1_p)])
    mid = Scatter(orders, sums, "z", fc1.item[1], fc2.came)
    fc1.far("z", sums[0])
    fc2.near(sums[0])
    own, gtok_send, cls8, *panels = tok_bwd_call(
        orders["x"], (mine0, send0, after(mine1, sums[0], fc1.keep, fc2.item[0]), send1), qkv_weight, tok, ghid,
        row(ln1_gain), mask_rows, vec_f, vec_b, fc1_vec)
    end = Scatter(orders, panels, "x", fc2.item[1])
    gtok_came = swap(after(gtok_send, own), "yl")
    mid.near(panels[0])
    fc1.near(panels[0])
    end.near()
    mid.far("x")
    end.far("z")
    mid.near()
    end.near()
    fc2.far("y", merge=(fc1, mid, end))
    fc2.near()

    gtok_came = gtok_came.astype(F32)
    grad_patches = both(own, gtok_came[:half], 1) * (1.0 - mask_f[..., None])
    cls_part = both(cls8[0], gtok_came[half], 0)
    mine, gone, grad_pos = last_sum(order, [fc2.item], cls_part.reshape(16, PAN))
    fc2_g, fc1_g, proj_g, qkv_g, vec8, cls16 = finish(order, mine, swap(gone, "core"))
    sums = lax.dynamic_index_in_dim(vec8, core, 0, False)
    v = [sums[8 * j:8 * j + 8] for j in range(9)] + [sums[72:104], sums[104:120]]
    out_came = after(out_came, gtok_send)
    out_patches = both(out[:half], out_came[:half], 1)
    out_cls = both(out[2 * half], out_came[half], 0)
    return (out_patches, out_cls, grad_patches, cls16.reshape(2, width), v[8], grad_pos.T, v[6], v[7], qkv_g, v[10],
            proj_g, v[5], v[4], v[2], v[3], fc1_g, v[9], fc2_g, v[1], v[0])


def solution(mesh):
    fine = Mesh(mesh.devices.reshape([SIZES[a] for a in ALL]), ALL)
    img, blk = ("z", "yh", "x"), ("yl", "core")
    every = img + blk
    rep, crops, rows = P(), P(img, None), P(blk, img, None)
    vec, mat = P(every), P(every, None)
    return jax.shard_map(
        local,
        mesh=fine,
        in_specs=(rows, crops, P(blk, img), rep, P(blk, None)) + (rep,) * 14 + (rows, crops),
        out_specs=(rows, crops, rows, crops, vec, P(blk, img), vec, vec, mat, vec, mat, vec, vec, vec, vec, mat, vec, mat,
                   vec, vec),
        check_vma=False,
    )
```

```python
import functools
import itertools

import jax
import jax.numpy as jnp
from jax import lax
from jax.experimental import pallas as pl
from jax.experimental.pallas import tpu as pltpu
from jax.sharding import Mesh
from jax.sharding import PartitionSpec as P

EPS = 1e-06
BF = jnp.bfloat16
F32 = jnp.float32
TAIL = 16
INV_SQRT2 = 0.7071067811865476
INV_SQRT2PI = 0.3989422804014327
PAN = 128

ALL = ("z", "yh", "x", "yl", "core")
SIZES = {"z": 4, "yh": 2, "x": 4, "yl": 2, "core": 2}
Y = ("yh", "yl")


def nn(a, b):
    return jnp.dot(a, b, preferred_element_type=F32)


def nt(a, b):
    return lax.dot_general(a, b, (((1,), (1,)), ((), ())), preferred_element_type=F32)


def tn(a, b):
    return lax.dot_general(a, b, (((0,), (0,)), ((), ())), preferred_element_type=F32)


def params(mib):
    return pltpu.CompilerParams(vmem_limit_bytes=mib << 20)


def cost(macs, nbytes, exps=0):
    return pl.CostEstimate(flops=2 * macs, bytes_accessed=nbytes, transcendentals=exps)


def whole(shape):
    return pl.BlockSpec(shape, lambda *_: (0,) * len(shape))


def sd(shape, dtype=BF):
    return jax.ShapeDtypeStruct(shape, dtype)


def far_in(*arrays):
    return [pltpu.with_memory_space_constraint(a, pltpu.HBM) for a in arrays]


def unit_of(x):
    center = x - jnp.mean(x, -1, keepdims=True)
    inv = lax.rsqrt(jnp.mean(center * center, -1, keepdims=True) + EPS)
    return center * inv, inv


def unit_grad(gu, unit, inv):
    return (gu - jnp.mean(gu, -1, keepdims=True) - unit * jnp.mean(gu * unit, -1, keepdims=True)) * inv


def norm_project_body(x_ref, gain_ref, bias_ref, w_ref, add_ref, normed_ref, out_ref):
    @pl.when(pl.program_id(0) == 0)
    def _():
        unit, _ = unit_of(x_ref[...])
        normed_ref[...] = (unit * gain_ref[...] + bias_ref[...]).astype(BF)

    out_ref[...] = (nn(normed_ref[...], w_ref[...]) + add_ref[...]).astype(BF)


def project_body(scale, x_ref, w_ref, add_ref, out_ref):
    out_ref[...] = ((nn(x_ref[...], w_ref[...]) + add_ref[...]) * scale).astype(BF)


def project_call(x, w, add, at, steps, norm=None, scale=1.0, tile=256):
    rows, width = x.shape
    mat, vec = whole((rows, width)), whole((1, width))
    out = pl.BlockSpec((rows, tile), lambda i: (0, i))
    shape = sd((rows, steps * tile))
    ins = [pl.BlockSpec((width, tile), lambda i: (0, at(i))), pl.BlockSpec((1, tile), lambda i: (0, at(i)))]
    common = dict(grid=(steps,), compiler_params=params(32),
                  cost_estimate=cost(rows * width * steps * tile, 2 * steps * (width * tile + rows * tile)))
    if norm is None:
        return pl.pallas_call(functools.partial(project_body, scale), in_specs=[mat] + ins, out_specs=out,
                              out_shape=shape, name="project", **common)(x, w, add)
    return pl.pallas_call(norm_project_body, in_specs=[mat, vec, vec] + ins, out_specs=[mat, out],
                          out_shape=[sd((rows, width)), shape], name="norm_project", **common)(x, *norm, w, add)


def half_mask(h):
    return (lax.broadcasted_iota(jnp.int32, (1, PAN), 1) // 64) == h


def att_fwd_body(np_, q_ref, ko_ref, vo_ref, kp_ref, vp_ref, *refs, chunk):
    out_ref, lse_ref = refs[-2:]
    rows = q_ref.shape[0]
    k_tail = ko_ref[np_:np_ + TAIL, :]
    v_cls = vo_ref[np_:np_ + 1, :].astype(F32)
    ko, kp = ko_ref[0:np_, :], kp_ref[0:np_, :]
    vo, vp = vo_ref[0:np_, :], vp_ref[0:np_, :]
    for r0 in range(0, rows, chunk):
        q = q_ref[r0:r0 + chunk, :]
        outs, lses = [], []
        for h in range(2):
            qh = jnp.where(half_mask(h), q, jnp.zeros_like(q))
            s1, s2 = nt(qh, ko), nt(qh, kp)
            sc = nt(qh, k_tail)[:, 0:1]
            top = jnp.maximum(jnp.maximum(jnp.max(s1, -1, keepdims=True), jnp.max(s2, -1, keepdims=True)), sc)
            p1, p2, pc = jnp.exp(s1 - top), jnp.exp(s2 - top), jnp.exp(sc - top)
            total = jnp.sum(p1, -1, keepdims=True) + jnp.sum(p2, -1, keepdims=True) + pc
            o = nn(p1.astype(BF), vo) + nn(p2.astype(BF), vp) + pc * v_cls
            outs.append(o / total)
            lses.append(top + jnp.log(total))
        out_ref[r0:r0 + chunk, :] = jnp.where(half_mask(0), outs[0], outs[1]).astype(BF)
        lse_ref[r0:r0 + chunk, :] = jnp.where(half_mask(0), lses[0], lses[1])


def att_fwd_call(q, kv, kv_p, at, pairs, into=None, chunk=264):
    rows, width = q.shape
    np_ = rows - TAIL
    col = lambda a: pl.BlockSpec((rows, PAN), lambda i: (0, a + i))
    ins = [col(at), col(0), col(pairs), col(0), col(pairs)]
    args = far_in(q, kv, kv, kv_p, kv_p)
    if into is not None:
        ins.append(pl.BlockSpec(memory_space=pl.ANY))
        args.append(into)
    return pl.pallas_call(
        functools.partial(att_fwd_body, np_, chunk=chunk),
        grid=(pairs,),
        in_specs=ins,
        out_specs=[col(at), col(0)],
        out_shape=[sd((rows, width)), pltpu.HBM((rows, pairs * PAN), F32)],
        input_output_aliases={} if into is None else {5: 0},
        compiler_params=params(24),
        cost_estimate=cost(rows * 2 * np_ * PAN * 2 * pairs * 2, 2 * rows * PAN * pairs * 8, rows * 2 * np_ * 2 * pairs),
        name="att_fwd",
    )(*args)


def att_bwd_body(np_, q_ref, ko_ref, vo_ref, kp_ref, vp_ref, go_ref, o_ref, lse_ref, dq_ref, own_ref, part_ref):
    q, go = q_ref[...], go_ref[...]
    ko, kp = ko_ref[0:np_, :], kp_ref[0:np_, :]
    vo, vp = vo_ref[0:np_, :], vp_ref[0:np_, :]
    k_tail, v_tail = ko_ref[np_:np_ + TAIL, :], vo_ref[np_:np_ + TAIL, :]
    k_cls = k_tail[0:1].astype(F32)
    qt, gt = q.T, go.T
    qf, gf = q.astype(F32), go.astype(F32)
    prod = gf * o_ref[...].astype(F32)
    dq = dkc = dvc = None
    dk1, dk2, dv1, dv2 = [], [], [], []
    for h in range(2):
        mask = half_mask(h)
        qh = jnp.where(mask, q, jnp.zeros_like(q))
        gh = jnp.where(mask, go, jnp.zeros_like(go))
        delta = jnp.sum(jnp.where(mask, prod, 0.0), -1, keepdims=True)
        lse = lse_ref[:, 64 * h:64 * h + 1]
        qth, gth = qt[64 * h:64 * h + 64], gt[64 * h:64 * h + 64]
        dqh = None
        for k, v, dk, dv in ((ko, vo, dk1, dv1), (kp, vp, dk2, dv2)):
            p = jnp.exp(nt(qh, k) - lse)
            ds = (p * (nt(gh, v) - delta)).astype(BF)
            part = nn(ds, k)
            dqh = part if dqh is None else dqh + part
            dk.append(nn(qth, ds))
            dv.append(nn(gth, p.astype(BF)))
        pc = jnp.exp(nt(qh, k_tail)[:, 0:1] - lse)
        dsc = pc * (nt(gh, v_tail)[:, 0:1] - delta)
        dqh = (dqh + dsc * k_cls) * 0.125
        kc = jnp.sum(dsc * qf, 0, keepdims=True)
        vc = jnp.sum(pc * gf, 0, keepdims=True)
        dq = dqh if h == 0 else jnp.where(mask, dqh, dq)
        dkc = kc if h == 0 else jnp.where(mask, kc, dkc)
        dvc = vc if h == 0 else jnp.where(mask, vc, dvc)
    dq_ref[...] = dq.astype(BF)
    both = lambda parts: jnp.concatenate(parts, 0).T.astype(BF)
    own_ref[0:np_, 0:PAN] = both(dk1)
    own_ref[0:np_, PAN:2 * PAN] = both(dv1)
    part_ref[:, 0:PAN] = both(dk2)
    part_ref[:, PAN:2 * PAN] = both(dv2)
    first = lax.broadcasted_iota(jnp.int32, (TAIL, PAN), 0) == 0
    own_ref[np_:np_ + TAIL, 0:PAN] = jnp.where(first, dkc, 0.0).astype(BF)
    own_ref[np_:np_ + TAIL, PAN:2 * PAN] = jnp.where(first, dvc, 0.0).astype(BF)


def att_bwd_call(q, kv, kv_p, go, o, lse, at, pairs):
    rows = q.shape[0]
    np_ = rows - TAIL
    col = lambda a: pl.BlockSpec((rows, PAN), lambda i: (0, a + i))
    two = lambda n: pl.BlockSpec((n, 2 * PAN), lambda i: (0, i))
    return pl.pallas_call(
        functools.partial(att_bwd_body, np_),
        grid=(pairs,),
        in_specs=[col(at), col(0), col(pairs), col(0), col(pairs), col(at), col(at), col(0)],
        out_specs=[col(0), two(rows), two(np_)],
        out_shape=[sd((rows, pairs * PAN)), sd((rows, pairs * 2 * PAN)), sd((np_, pairs * 2 * PAN))],
        compiler_params=params(32),
        cost_estimate=cost(rows * 2 * np_ * PAN * 5 * pairs * 2, 2 * rows * PAN * pairs * 16, rows * 2 * np_ * 2 * pairs),
        name="att_bwd",
    )(*far_in(q, kv, kv, kv_p, kv_p, go, o, lse))


def trip_body(np_, pairs, order_ref, dq_ref, own_ref, came_ref, mine_ref, send_ref):
    core = order_ref[0]
    n = pairs // 2 * PAN
    for out_ref, side in ((mine_ref, core), (send_ref, 1 - core)):
        out_ref[:, 0:n] = dq_ref[:, pl.ds(pl.multiple_of(side * n, PAN), n)]
        for j in range(pairs // 2):
            for kind in range(2):
                src = pl.ds(pl.multiple_of(side * 2 * n + (2 * j + kind) * PAN, PAN), PAN)
                dst = slice((1 + kind) * n + j * PAN, (1 + kind) * n + (j + 1) * PAN)
                out_ref[0:np_, dst] = (own_ref[0:np_, src].astype(F32) + came_ref[:, src].astype(F32)).astype(BF)
                out_ref[np_:, dst] = own_ref[np_:, src]


def trip_call(order, dq, own, came):
    rows, n = dq.shape
    np_ = rows - TAIL
    shape = sd((rows, n // 2 * 3))
    return pl.pallas_call(
        functools.partial(trip_body, np_, n // PAN),
        grid_spec=pltpu.PrefetchScalarGridSpec(
            num_scalar_prefetch=1, grid=(1,),
            in_specs=[whole(a.shape) for a in (dq, own, came)],
            out_specs=[whole(shape.shape)] * 2),
        out_shape=[shape, shape],
        compiler_params=params(24),
        cost_estimate=cost(0, 2 * rows * n * 8),
        name="trip",
    )(order, dq, own, came)


def mlp_fwd_body(order_ref, att_ref, tok_ref, wp_ref, bp_ref, sa_ref, gain_ref, bias_ref, w1_ref, b1_ref, w2_ref, b2_ref,
                 sm_ref, gout_ref, hid_ref, br1_ref, n2_ref, act_ref, dg_ref, out_ref, gb2_ref, gb2m_ref, gb2s_ref, vec_ref, acc_ref):
    i = pl.program_id(0)

    @pl.when(i == 0)
    def _():
        br1 = nn(att_ref[...], wp_ref[...]) + bp_ref[...]
        br1_ref[...] = br1.astype(BF)
        hid = tok_ref[...] + sa_ref[...] * br1
        hid_ref[...] = hid
        unit, _ = unit_of(hid)
        n2_ref[...] = (unit * gain_ref[...] + bias_ref[...]).astype(BF)

    pre = nn(n2_ref[...], w1_ref[...]) + b1_ref[...]
    cdf = 0.5 + 0.5 * lax.erf(pre * INV_SQRT2)
    act = (pre * cdf).astype(BF)
    act_ref[...] = act
    dg_ref[...] = (cdf + pre * (jnp.exp(-0.5 * pre * pre) * INV_SQRT2PI)).astype(BF)
    part = nn(act, w2_ref[...])

    @pl.when(i == 0)
    def _():
        acc_ref[...] = part

    @pl.when(i > 0)
    def _():
        acc_ref[...] += part

    @pl.when(i == pl.num_programs(0) - 1)
    def _():
        br2 = acc_ref[...] + b2_ref[...]
        out_ref[...] = (hid_ref[...] + sm_ref[...] * br2).astype(BF)
        gout = gout_ref[...].astype(F32)
        gb2 = (sm_ref[...] * gout).astype(BF)
        gb2_ref[...] = gb2
        vec_ref[0:1, :] = jnp.sum(gout * br2, 0, keepdims=True)
        vec_ref[1:2, :] = jnp.sum(gb2.astype(F32), 0, keepdims=True)
        n = gb2s_ref.shape[1]
        gb2m_ref[...] = gb2_ref[:, pl.ds(pl.multiple_of(order_ref[0] * n, PAN), n)]
        gb2s_ref[...] = gb2_ref[:, pl.ds(pl.multiple_of((1 - order_ref[0]) * n, PAN), n)]


def mlp_fwd_call(order, att, tok, wp, bp, sa, gain, bias, w1, b1, w2, b2, sm, gout, tile=512):
    rows, width = tok.shape
    ff = w1.shape[1]
    mat, vec = whole((rows, width)), whole((1, width))
    col = pl.BlockSpec((rows, tile), lambda i, c: (0, i))
    return pl.pallas_call(
        mlp_fwd_body,
        grid_spec=pltpu.PrefetchScalarGridSpec(
            num_scalar_prefetch=1,
            grid=(ff // tile,),
            in_specs=[mat, mat, whole((width, width)), vec, vec, vec, vec,
                      pl.BlockSpec((width, tile), lambda i, c: (0, i)), pl.BlockSpec((1, tile), lambda i, c: (0, i)),
                      pl.BlockSpec((tile, width), lambda i, c: (i, 0)), vec, vec, mat],
            out_specs=[mat, mat, mat, col, col, mat, mat] + [whole((rows, width // 2))] * 2 + [whole((8, width))],
            scratch_shapes=[pltpu.VMEM((rows, width), F32)]),
        out_shape=[sd((rows, width), F32), pltpu.HBM((rows, width), BF), sd((rows, width)), sd((rows, ff)), pltpu.HBM((rows, ff), BF),
                   sd((rows, width)), sd((rows, width))] + [sd((rows, width // 2))] * 2 + [sd((8, width), F32)],
        compiler_params=params(36),
        cost_estimate=cost(rows * width * (2 * ff + width), 2 * (2 * width * ff + 2 * rows * ff + 6 * rows * width), rows * ff),
        name="mlp_fwd",
    )(order, att, tok, wp, bp, sa, gain, bias, w1, b1, w2, b2, sm, gout)


def mlp_bwd_step(gb2_ref, dg_ref, w1_ref, w2_ref, gpre_ref, b1_ref, at):
    gpre = (nt(gb2_ref[...], w2_ref[...]) * dg_ref[...].astype(F32)).astype(BF)
    gpre_ref[...] = gpre
    b1_ref[0:1, at] = jnp.sum(gpre.astype(F32), 0, keepdims=True)
    return nt(gpre, w1_ref[...])


def mlp_bwd_first_body(order_ref, gb2_ref, dg_ref, w1_ref, w2_ref, gpre_ref, b1_ref, acc_ref):
    i = pl.program_id(0)
    part = mlp_bwd_step(gb2_ref, dg_ref, w1_ref, w2_ref, gpre_ref, b1_ref, slice(None))

    @pl.when(i == 0)
    def _():
        acc_ref[...] = part

    @pl.when(i > 0)
    def _():
        acc_ref[...] += part


def mlp_bwd_second_body(order_ref, gb2_ref, dg_ref, w1_ref, w2_ref, first_ref, b1_first_ref, hid_ref, br1_ref, gout_ref,
                        wp_ref, sa_ref, gain_ref, gpre_ref, b1_ref, ghid_ref, gb1_ref, gb1m_ref, gb1s_ref, gatt_ref,
                        vec_ref, acc_ref):
    i = pl.program_id(0)
    core = order_ref[0]
    tile, half = gpre_ref.shape[1], b1_first_ref.shape[1]
    part = mlp_bwd_step(gb2_ref, dg_ref, w1_ref, w2_ref, gpre_ref, b1_ref,
                        pl.ds(pl.multiple_of(core * half + i * tile, PAN), tile))

    @pl.when(i == 0)
    def _():
        acc_ref[...] = first_ref[...] + part
        b1_ref[0:1, pl.ds(pl.multiple_of((1 - core) * half, PAN), half)] = b1_first_ref[0:1, :]

    @pl.when(i > 0)
    def _():
        acc_ref[...] += part

    @pl.when(i == pl.num_programs(0) - 1)
    def _():
        unit, inv = unit_of(hid_ref[...])
        gn = acc_ref[...]
        vec_ref[0:1, :] = jnp.sum(gn * unit, 0, keepdims=True)
        vec_ref[1:2, :] = jnp.sum(gn, 0, keepdims=True)
        ghid = gout_ref[...].astype(F32) + unit_grad(gn * gain_ref[...], unit, inv)
        ghid_ref[...] = ghid
        vec_ref[2:3, :] = jnp.sum(ghid * br1_ref[...].astype(F32), 0, keepdims=True)
        gb1 = (sa_ref[...] * ghid).astype(BF)
        gb1_ref[...] = gb1
        vec_ref[3:4, :] = jnp.sum(gb1.astype(F32), 0, keepdims=True)
        n = gb1s_ref.shape[1]
        gb1m_ref[...] = gb1_ref[:, pl.ds(pl.multiple_of(core * n, PAN), n)]
        gb1s_ref[...] = gb1_ref[:, pl.ds(pl.multiple_of((1 - core) * n, PAN), n)]
        gatt_ref[...] = nt(gb1, wp_ref[...]).astype(BF)


def mlp_bwd_specs(rows, width, ff, tile, mine):
    half = ff // tile // 2
    at = lambda i, c: i + half * (c[0] if mine else 1 - c[0])
    col = lambda n: pl.BlockSpec((n, tile), lambda i, c: (0, at(i, c)))
    return half, [whole((rows, width)), col(rows), col(width), pl.BlockSpec((tile, width), lambda i, c: (at(i, c), 0))]


def mlp_bwd_first_call(order, gb2, dg, w1, w2, tile=512):
    rows, width = gb2.shape
    ff = w1.shape[1]
    half, ins = mlp_bwd_specs(rows, width, ff, tile, False)
    return pl.pallas_call(
        mlp_bwd_first_body,
        grid_spec=pltpu.PrefetchScalarGridSpec(
            num_scalar_prefetch=1, grid=(half,), in_specs=ins,
            out_specs=[pl.BlockSpec((rows, tile), lambda i, c: (0, i)), pl.BlockSpec((8, tile), lambda i, c: (0, i)),
                       whole((rows, width))]),
        out_shape=[sd((rows, ff // 2)), sd((8, ff // 2), F32), sd((rows, width), F32)],
        compiler_params=params(24),
        cost_estimate=cost(rows * width * ff, 2 * (width * ff + rows * ff)),
        name="mlp_bwd_first",
    )(order, gb2, *far_in(dg, w1, w2))


def mlp_bwd_second_call(order, gb2, dg, w1, w2, first, b1_first, hid, br1, gout, wp, sa, gain, tile=512):
    rows, width = hid.shape
    ff = w1.shape[1]
    half, ins = mlp_bwd_specs(rows, width, ff, tile, True)
    mat, vec, halfm = whole((rows, width)), whole((1, width)), whole((rows, width // 2))
    return pl.pallas_call(
        mlp_bwd_second_body,
        grid_spec=pltpu.PrefetchScalarGridSpec(
            num_scalar_prefetch=1, grid=(half,),
            in_specs=ins + [mat, whole((8, ff // 2)), mat, mat, mat, whole((width, width)), vec, vec],
            out_specs=[pl.BlockSpec((rows, tile), lambda i, c: (0, i)), whole((8, ff)), mat, mat, halfm, halfm, mat,
                       whole((8, width))],
            scratch_shapes=[pltpu.VMEM((rows, width), F32)]),
        out_shape=[sd((rows, ff // 2)), sd((8, ff), F32), sd((rows, width), F32), sd((rows, width)),
                   sd((rows, width // 2)), sd((rows, width // 2)), sd((rows, width)), sd((8, width), F32)],
        compiler_params=params(32),
        cost_estimate=cost(rows * width * (ff + width), 2 * (width * ff + rows * ff + 6 * rows * width)),
        name="mlp_bwd_second",
    )(order, gb2, *far_in(dg, w1, w2), first, b1_first, hid, br1, gout, wp, sa, gain)


def vector_panels(vectors, z):
    r = lax.broadcasted_iota(jnp.int32, (256, 1), 0)
    device = jnp.where(r % 16 < 2, r // 16 * 2 + r % 16, -1)
    total, at = None, 0
    for vector in vectors:
        n = vector.shape[1] // 4
        per = n // 32
        lane = lax.broadcasted_iota(jnp.int32, (1, n), 1)
        spread = jnp.where(lane // per == device, vector[:, z * n:(z + 1) * n], 0.0).astype(BF)
        pick_r = lax.broadcasted_iota(jnp.int32, (n, PAN), 0)
        pick_c = lax.broadcasted_iota(jnp.int32, (n, PAN), 1)
        part = nn(spread, jnp.where(pick_r % per + at == pick_c, 1.0, 0.0).astype(BF))
        total = part if total is None else total + part
        at += per
    return total.astype(BF)


def stacked(a0, a1):
    n = a0.shape[0] - TAIL
    return jnp.concatenate((a0[0:n], a1[0:n], a0[n:], a1[n:]), 0)


def dw_body(jobs, axis, order_ref, *refs):
    send_ref, keep_ref = refs[-2:]
    i = pl.program_id(0)
    done, at, base = [], 0, 0
    for rows, panels in jobs:
        a0, a1, g0, g1 = (ref[...] for ref in refs[at:at + 4])
        done.append((tn(stacked(a0, a1), stacked(g0, g1)).astype(BF), base, rows))
        at, base = at + 4, base + panels

    def write(ref, place, xs):
        for value, first, rows in done:
            n = value.shape[1] // PAN
            for yh, x, yl, rg, pc in itertools.product(range(2), xs, range(2), range(rows // 16), range(n)):
                r0 = ((yh * 4 + x) * 2 + yl) * rows + rg * 16
                ref[place(yh, x, yl) + (first + rg * n + pc,)] = value[r0:r0 + 16, pc * PAN:(pc + 1) * PAN]

    if axis == "z":
        place = lambda yh, x, yl: (0, yh, x, yl)
        pl.when(i < 2)(lambda: write(send_ref, place, range(4)))
        pl.when(i >= 2)(lambda: write(keep_ref, place, range(4)))
    else:
        for target in range(4):
            slot = order_ref[5 + target]
            pl.when(slot < 2)(lambda: write(send_ref, lambda yh, x, yl: (slot, 0, yh, yl), (target,)))
            pl.when(slot >= 2)(lambda: write(keep_ref, lambda yh, x, yl: (slot - 2, 0, yh, yl), (target,)))


def dw_call(order, axis, jobs):
    ins, args, shapes, macs = [], [], [], 0
    at = (lambda i, c: c[1 + i]) if axis == "z" else (lambda i, c: i)
    for a0, a1, g0, g1 in jobs:
        rows, k = a0.shape
        n = g0.shape[1]
        lhs = pl.BlockSpec((rows, k // 4), lambda i, c: (0, at(i, c)))
        ins += [lhs, lhs, whole((rows, n)), whole((rows, n))]
        args += far_in(a0, a1) + [g0, g1]
        shapes.append((k // 64, k // 1024 * (n // PAN)))
        macs += 2 * rows * k * n
    panels = sum(p for _, p in shapes)
    if axis == "z":
        out = (2, 2, 4, 2, panels, 16, PAN)
        block = lambda f: pl.BlockSpec((1,) + out[1:], lambda i, c: (f(i),) + (0,) * 6)
        outs = [block(lambda i: jnp.minimum(i, 1)), block(lambda i: jnp.maximum(i - 2, 0))]
    else:
        out = (2, 4, 2, 2, panels, 16, PAN)
        outs = [pl.BlockSpec((2, 1) + out[2:], lambda i, c: (0, i) + (0,) * 5)] * 2
    return pl.pallas_call(
        functools.partial(dw_body, tuple(shapes), axis),
        grid_spec=pltpu.PrefetchScalarGridSpec(num_scalar_prefetch=1, grid=(4,), in_specs=ins, out_specs=outs),
        out_shape=[sd(out), pltpu.HBM(out, BF)],
        compiler_params=params(24),
        cost_estimate=cost(macs, 2 * sum(a.size for a in args) + 8 * 64 * panels * 16 * PAN),
        name="dw",
    )(order, *args)


def tok_bwd_body(half, order_ref, g0_mine, g0_send, g1_mine, g1_send, *refs):
    w0, w1 = refs[0:3], refs[3:6]
    (tok_ref, ghid_ref, gain_ref, mask_ref, vf_ref, vb_ref, b1_ref, own_ref, send_ref, cls_ref, *panel_refs,
     qv_ref, pos_ref, vecs_ref, acc_ref) = refs[6:]
    i = pl.program_id(0)
    width = tok_ref.shape[1]
    core = order_ref[0]
    first = 0
    for step, (g_ref, ws) in enumerate(((g0_mine, w0), (g0_send, w0), (g1_mine, w1), (g1_send, w1))):
        n = ws[0].shape[1]
        side = core if step % 2 == 0 else 1 - core

        @pl.when(i == step)
        def _():
            part = sum(nt(g_ref[:, j * n:(j + 1) * n], w[...]) for j, w in enumerate(ws))
            if step == 0:
                acc_ref[...] = part
            else:
                acc_ref[...] += part
            sums = jnp.sum(g_ref[...].astype(F32), 0, keepdims=True)
            at = pl.multiple_of(first + side * n, PAN)
            qv_ref[0:1, pl.ds(at, n)] = sums[:, 0:n]
            qv_ref[0:1, pl.ds(width + at, n)] = sums[:, 2 * n:]

        if step == 1:
            first = 2 * n

    @pl.when(i == 3)
    def _():
        unit, inv = unit_of(tok_ref[...])
        gn = acc_ref[...]
        gtok = ghid_ref[...] + unit_grad(gn * gain_ref[...], unit, inv)
        own_ref[...] = gtok[0:half]
        send_ref[...] = gtok[half:].astype(BF)
        cls_ref[...] = gtok[2 * half:2 * half + 8]
        pos_ref[...] = gtok[0:2 * half].T.astype(BF)
        column = lambda v: jnp.sum(v, 0, keepdims=True)
        vectors = [vf_ref[0:1, :], vf_ref[1:2, :]] + [vb_ref[j:j + 1, :] for j in range(4)]
        vectors += [column(gn * unit), column(gn), column(gtok * mask_ref[:, 0:1].astype(F32)), b1_ref[0:1, :],
                    qv_ref[0:1, :]]
        for z in range(4):
            vecs_ref[z] = vector_panels(vectors, z)
        for slot in range(4):
            ref = panel_refs[slot // 2]
            target = order_ref[1 + slot]
            for z, yh, part in itertools.product(range(4), range(2), range(2)):
                rows = pl.ds(pl.multiple_of(z * 256 + (yh * 4 + target) * 32 + part * 16, 16), 16)
                for side, pc in itertools.product(range(2), range(2)):
                    yl = order_ref[9] if side == 0 else 1 - order_ref[9]
                    c0 = side * half + pc * PAN
                    ref[slot % 2, z, yh, yl, part * 2 + pc] = pos_ref[rows, c0:c0 + PAN]
                chip = pl.ds(pl.multiple_of((yh * 4 + target) * 32 + part * 16, 16), 16)
                ref[slot % 2, z, yh, part, 4] = vecs_ref[z, chip, :]


def tok_bwd_call(order, gs, w, tok, ghid, gain, mask, vf, vb, b1):
    rows, width = tok.shape
    half = (rows - TAIL) // 2
    mat, vec = whole((rows, width)), whole((1, width))
    n0, n1 = gs[0].shape[1] // 3, gs[2].shape[1] // 3
    panels = (2, 4, 2, 2, 5, 16, PAN)
    side = lambda i, c: jnp.where(i % 2 == 0, c[0], 1 - c[0])
    ws = [pl.BlockSpec((pl.Element(width), pl.Element(n0)),
                       lambda i, c, j=j: (0, pl.multiple_of(j * width + side(jnp.minimum(i, 1), c) * n0, PAN))) for j in range(3)]
    ws += [pl.BlockSpec((pl.Element(width), pl.Element(n1)),
                        lambda i, c, j=j: (0, pl.multiple_of(j * width + 2 * n0 + side(jnp.maximum(i, 2), c) * n1, PAN)))
           for j in range(3)]
    return pl.pallas_call(
        functools.partial(tok_bwd_body, half),
        grid_spec=pltpu.PrefetchScalarGridSpec(
            num_scalar_prefetch=1,
            grid=(4,),
            in_specs=[whole(g.shape) for g in gs] + ws + [mat, mat, vec, whole((rows, PAN))]
            + [whole(v.shape) for v in (vf, vb, b1)],
            out_specs=[whole((half, width)), whole((half + TAIL, width)), whole((8, width))] + [whole(panels)] * 2,
            scratch_shapes=[pltpu.VMEM((8, 2 * width), F32), pltpu.VMEM((width, 2 * half), BF),
                            pltpu.VMEM((4, 256, PAN), BF), pltpu.VMEM((rows, width), F32)]),
        out_shape=[sd((half, width), F32), sd((half + TAIL, width)), sd((8, width), F32)] + [sd(panels)] * 2,
        compiler_params=params(36),
        cost_estimate=cost(rows * width * 3 * width, 2 * (3 * width * width + 8 * rows * width)),
        name="tok_bwd",
    )(order, *gs, *[w] * 6, tok, ghid, gain, mask, vf, vb, b1)


def near_sum_body(keep_ref, came_ref, kept_ref, send_ref):
    kept_ref[...] = keep_ref[0].astype(F32) + came_ref[0].astype(F32)
    send_ref[...] = (keep_ref[1].astype(F32) + came_ref[1].astype(F32)).astype(BF)


def near_sum(keep, came, parts=4):
    shape = keep.shape
    m = keep.size // (2 * 16 * PAN)
    flat = lambda a: a.reshape(2, m, 16, PAN)
    parts = parts if m % parts == 0 and m >= 16 else 1
    two = pl.BlockSpec((2, m // parts, 16, PAN), lambda i: (0, i, 0, 0))
    one = pl.BlockSpec((m // parts, 16, PAN), lambda i: (i, 0, 0))
    kept, send = pl.pallas_call(
        near_sum_body, grid=(parts,), in_specs=[two, two], out_specs=[one, one],
        out_shape=[sd((m, 16, PAN), F32), sd((m, 16, PAN))],
        compiler_params=params(24), cost_estimate=cost(0, keep.size * 6), name="near_sum",
    )(flat(keep), flat(came))
    return kept.reshape(shape[1:]), send.reshape(shape[1:])


def far_sum_body(labels, axis, counts, order_ref, *refs):
    ins, outs = refs[:-2], refs[-2:]
    for slot in range(4):
        target = order_ref[1 + slot]
        place = {"y": {"yh": target // 2, "yl": target % 2}}.get(axis, {axis: target})
        where = tuple(place.get(label, slice(None)) for label in labels)
        out = outs[slot // 2]
        at, j = 0, 0
        for count in counts:
            n = ins[j].shape[-3]
            total = ins[j][where].astype(F32)
            for came in ins[j + 1:j + count]:
                total = total + came[where].astype(F32)
            out[(slot % 2,) + (slice(None),) * (total.ndim - 3) + (slice(at, at + n),)] = total.astype(out.dtype)
            at += n
            j += count


def far_sum(order, items, labels, axis):
    gone = ("yh", "yl") if axis == "y" else (axis,)
    left = [l for l in labels if l not in gone]
    panels = sum(item[0].shape[-3] for item in items)
    out = (2,) + tuple(SIZES[l] for l in left) + (panels, 16, PAN)
    args = [a for item in items for a in item]
    outs = [sd(out), sd(out, F32)]
    return left, pl.pallas_call(
        functools.partial(far_sum_body, labels, axis, tuple(len(item) for item in items)),
        grid_spec=pltpu.PrefetchScalarGridSpec(
            num_scalar_prefetch=1, grid=(1,),
            in_specs=[whole(a.shape) for a in args],
            out_specs=[whole(o.shape) for o in outs]),
        out_shape=outs,
        compiler_params=params(24), cost_estimate=cost(0, sum(a.size for a in args) * 6), name="far_sum",
    )(order, *args)


def last_sum_body(counts, order_ref, *refs):
    ins, (cls_ref, mine_ref, gone_ref, pos_ref, tot_ref) = refs[:-5], refs[-5:]
    core = order_ref[0]
    at, j = 0, 0
    for count in counts:
        total = ins[j][...]
        for came in ins[j + 1:j + count]:
            total = total + came[...].astype(F32)
        tot_ref[at:at + total.shape[0]] = total
        at += total.shape[0]
        j += count
    at = 0

    def put(panel, start):
        nonlocal at
        for ref, side in ((mine_ref, core), (gone_ref, 1 - core)):
            ref[at] = tot_ref[panel, pl.ds(pl.multiple_of(start(side), 8), 8), :]
        at += 1

    for rg, pc, part in itertools.product(range(2), range(4), range(2)):
        for ref, side in ((mine_ref, core), (gone_ref, 1 - core)):
            ref[at] = tot_ref[(2 * side + rg) * 4 + pc, 8 * part:8 * part + 8, :]
        at += 1
    for panel in range(16, 48):
        put(panel, lambda side: side * 8)
    mine_ref[at] = tot_ref[52, 0:8, :]
    gone_ref[at] = tot_ref[52, 0:8, :]
    for part in range(2):
        mine_ref[at + 1 + part] = cls_ref[8 * part:8 * part + 8, :]
        gone_ref[at + 1 + part] = cls_ref[8 * part:8 * part + 8, :]
    for rg, pc in itertools.product(range(2), range(2)):
        pos_ref[16 * rg:16 * rg + 16, pc * PAN:(pc + 1) * PAN] = tot_ref[48 + rg * 2 + pc]


SWAPPED = 16 + 32 + 3


def last_sum(order, items, cls16):
    shape = sd((SWAPPED, 8, PAN), F32)
    args = [a for item in items for a in item] + [cls16]
    panels = sum(item[0].shape[0] for item in items)
    return pl.pallas_call(
        functools.partial(last_sum_body, tuple(len(item) for item in items)),
        grid_spec=pltpu.PrefetchScalarGridSpec(
            num_scalar_prefetch=1, grid=(1,),
            in_specs=[whole(a.shape) for a in args],
            out_specs=[whole(shape.shape), whole(shape.shape), whole((32, 256))],
            scratch_shapes=[pltpu.VMEM((panels, 16, PAN), F32)]),
        out_shape=[shape, shape, sd((32, 256), F32)],
        compiler_params=params(24), cost_estimate=cost(0, panels * 2048 * 10), name="last_sum",
    )(order, *args)


def finish_body(order_ref, mine_ref, came_ref, fc2_ref, fc1_ref, proj_ref, qkv_ref, cls_ref, *vec_refs):
    first = order_ref[0] == 0
    at = 0

    def halves():
        nonlocal at
        mine, came = mine_ref[at], came_ref[at]
        at += 1
        return jnp.where(first, mine, came), jnp.where(first, came, mine)

    for rg, pc, part in itertools.product(range(2), range(4), range(2)):
        r0 = rg * 16 + part * 8
        for h, value in enumerate(halves()):
            fc2_ref[r0:r0 + 8, 512 * h + pc * PAN:512 * h + (pc + 1) * PAN] = value
    for pc in range(16):
        for h, value in enumerate(halves()):
            fc1_ref[:, 2048 * h + pc * PAN:2048 * h + (pc + 1) * PAN] = value
    for pc in range(4):
        for h, value in enumerate(halves()):
            proj_ref[:, 512 * h + pc * PAN:512 * h + (pc + 1) * PAN] = value
    for c0, per in ((0, 3), (768, 1)):
        for kind, pc in itertools.product(range(3), range(per)):
            for h, value in enumerate(halves()):
                at0 = kind * 1024 + c0 + (h * per + pc) * PAN
                qkv_ref[:, at0:at0 + PAN] = value
    both = mine_ref[at] + came_ref[at]
    row = jnp.where(first, both[0:1], both[1:2])
    start = 0
    for ref in vec_refs:
        n = ref.shape[1]
        ref[...] = row[:, start:start + n]
        start += n
    for part in range(2):
        total = mine_ref[at + 1 + part] + came_ref[at + 1 + part]
        for j in range(8):
            cls_ref[part:part + 1, j * PAN:(j + 1) * PAN] = total[j:j + 1]


def finish(order, mine, came):
    outs = [(32, 1024), (8, 4096), (8, 1024), (8, 3072), (2, 1024)] + [(1, 8)] * 9 + [(1, 32), (1, 16)]
    return pl.pallas_call(
        finish_body,
        grid_spec=pltpu.PrefetchScalarGridSpec(
            num_scalar_prefetch=1, grid=(1,), in_specs=[whole(mine.shape)] * 2, out_specs=[whole(s) for s in outs]),
        out_shape=[sd(s, F32) for s in outs],
        compiler_params=params(24), cost_estimate=cost(0, mine.size * 16), name="finish",
    )(order, mine, came)


def crops_body(order_ref, out_ref, out_came_ref, own_ref, came_ref, keep_ref, patches_ref, grad_ref):
    mine = lax.broadcasted_iota(jnp.int32, (1, 2, 1), 1) == order_ref[9]
    wide = lambda t: jnp.broadcast_to(t[:, None, :].astype(F32), (t.shape[0], 2, t.shape[1]))
    patches_ref[...] = jnp.where(mine, wide(out_ref[...]), wide(out_came_ref[...])).astype(BF)
    grad_ref[...] = jnp.where(mine, wide(own_ref[...]), wide(came_ref[...])) * keep_ref[...]


def crops_call(order, out, out_came, own, came, keep, parts=4):
    half, width = own.shape
    n = half // parts
    rows = pl.BlockSpec((n, width), lambda i, c: (i, 0))
    both = pl.BlockSpec((n, 2, width), lambda i, c: (i, 0, 0))
    return pl.pallas_call(
        crops_body,
        grid_spec=pltpu.PrefetchScalarGridSpec(
            num_scalar_prefetch=1, grid=(parts,),
            in_specs=[rows] * 4 + [pl.BlockSpec((n, 2, 1), lambda i, c: (i, 0, 0))], out_specs=[both, both]),
        out_shape=[sd((half, 2, width)), sd((half, 2, width), F32)],
        compiler_params=params(20), cost_estimate=cost(0, 22 * half * width), name="crops",
    )(order, out, out_came, own, came, keep)


def swap(x, axis):
    return lax.ppermute(x, axis, [(0, 1), (1, 0)])


def after(x, *others):
    return lax.optimization_barrier((x,) + others)[0] if others else x


def partners(axis, turn):
    pairs = []
    for z, yh, x, yl, core in itertools.product(*(range(SIZES[a]) for a in ALL)):
        at = {"z": z, "y": yh * 2 + yl, "x": x}
        flat = lambda p: (((p["z"] * 2 + p["y"] // 2) * 4 + p["x"]) * 2 + p["y"] % 2) * 2 + core
        there = dict(at)
        there[axis] ^= 1 if core == turn else 3
        pairs.append((flat(at), flat(there)))
    return pairs


def pass_on(x, axis, turn):
    return lax.ppermute(x, ALL, partners(axis, turn))


def order_of(axis):
    me = lax.axis_index("yh") * 2 + lax.axis_index("yl") if axis == "y" else lax.axis_index(axis)
    first = jnp.where(lax.axis_index("core") == 0, 1, 3)
    targets = [me ^ first, me ^ 2, me, me ^ first ^ 2]
    places = [sum(jnp.where(t == want, at, 0) for at, t in enumerate(targets)) for want in range(4)]
    return jnp.stack([lax.axis_index("core")] + targets + places + [lax.axis_index("yl")]).astype(jnp.int32)


class Scatter:
    def __init__(self, orders, sums, axis, *others):
        self.orders, self.axis = orders, axis
        self.labels = {"z": ["yh", "x", "yl"], "x": ["z", "yh", "yl"]}[axis]
        self.begin(sums, others)

    def begin(self, sums, others):
        send, self.keep = sums
        self.came = pass_on(after(send, *others), self.axis, 0)

    def near(self, *others):
        kept, send = near_sum(self.keep, self.came)
        self.item = [kept, pass_on(after(send, *others), self.axis, 1)]

    def far(self, axis, *others, merge=()):
        items = [s.item for s in (self,) + tuple(merge)]
        self.labels, sums = far_sum(self.orders[axis], items, self.labels, axis)
        self.axis = axis
        self.begin(sums, others)


def local(patches, cls_tokens, patch_masks, mask_token, pos_embed, ln1_gain, ln1_bias, qkv_weight, qv_bias, proj_weight,
          proj_bias, scale_attn, ln2_gain, ln2_bias, fc1_weight, fc1_bias, fc2_weight, fc2_bias, scale_mlp, cot_patches,
          cot_cls):
    half, _, width = patches.shape
    core, yl = lax.axis_index("core"), lax.axis_index("yl")
    row = lambda v: v.reshape(1, -1)
    sides = lambda a: (jnp.where(yl == 0, a[:, 0], a[:, 1]), jnp.where(yl == 0, a[:, 1], a[:, 0]))
    both = lambda mine, other, axis: jnp.where(yl == 0, jnp.stack((mine, other), axis), jnp.stack((other, mine), axis))
    pad = jnp.zeros((TAIL - 1, width), BF)
    orders = {a: order_of(a) for a in "zxy"}
    order = orders["z"]

    mask_f = patch_masks.astype(F32)
    mask3 = patch_masks[..., None]
    mixed = jnp.where(mask3 != 0, mask_token, patches)
    own, send = sides(mixed)
    came = swap(send, "yl")
    pos_came = lax.ppermute(pos_embed, Y, [(0, 3), (3, 0), (1, 2), (2, 1)])
    cls_row = jnp.where(yl == 0, cls_tokens[0:1], cls_tokens[1:2])
    tok = jnp.concatenate((own.astype(F32) + pos_embed.astype(F32), came.astype(F32) + pos_came.astype(F32),
                           cls_row.astype(F32), pad.astype(F32)), 0)

    add = row(jnp.concatenate((qv_bias[:width], jnp.zeros((width,), F32), qv_bias[width:])))
    n1, kv0 = project_call(tok, qkv_weight, add, lambda i: 4 + i % 3 + i // 3 * 4, 6, norm=(row(ln1_gain), row(ln1_bias)))
    kv0_p = swap(kv0, "core")
    kv1 = project_call(after(n1, kv0), qkv_weight, add, lambda i: 7 + i * 4, 2)
    q = project_call(after(n1, kv1), qkv_weight, add, lambda i: i, 2, scale=0.125, tile=512)
    kv1_p = swap(after(kv1, kv0_p), "core")

    mask_own, mask_send = sides(mask_f)
    cot_own, cot_send = sides(jnp.where(mask3 != 0, cot_patches, jnp.zeros_like(cot_patches)))
    lanes = lambda m: jnp.broadcast_to(m.astype(BF)[:, None], (half, PAN))
    cot_came = swap(after(jnp.concatenate((cot_send, lanes(mask_send)), 1), came, q), "yl")

    att, lse0 = att_fwd_call(after(q, kv0_p), kv0, kv0_p, 0, 6)
    n1_p = swap(after(n1, kv1_p), "core")
    att, lse1 = att_fwd_call(after(q, cot_came, n1_p), kv1, kv1_p, 6, 2, into=att)
    cot_came = after(cot_came, att)
    att_p = swap(after(att, n1_p), "core")
    cls_cot = jnp.where(yl == 0, cot_cls[0:1], cot_cls[1:2]) * (core == 0).astype(BF)
    gout = jnp.concatenate((cot_own, cot_came[:, :width], cls_cot, pad), 0)
    mask_rows = jnp.concatenate((lanes(mask_own), cot_came[:, width:], jnp.zeros((TAIL, PAN), BF)), 0)
    hid, br1, n2, act, dg, out, gb2, gb2_mine, gb2_send, vec_f = mlp_fwd_call(
        order, att, tok, proj_weight, row(proj_bias), row(scale_attn), row(ln2_gain), row(ln2_bias), fc1_weight,
        row(fc1_bias), fc2_weight, row(fc2_bias), row(scale_mlp), gout)

    act_p = swap(after(act, att_p), "core")
    gb2_p = swap(gb2_send, "core")
    gpre_send, b1_first, first = mlp_bwd_first_call(order, gb2, dg, fc1_weight, fc2_weight)
    gpre_p = swap(after(gpre_send, act_p, gb2_p), "core")
    n2_p = swap(after(n2, act_p, gb2_p, gpre_send), "core")
    sums = dw_call(order, "z", [(act, act_p, gb2_mine, gb2_p)])
    fc2 = Scatter(orders, sums, "z", gpre_p, n2_p)
    out_came = swap(after(out[half:], gpre_p, n2_p, sums[0]), "yl")
    gpre, fc1_vec, ghid, gb1, gb1_mine, gb1_send, gatt, vec_b = mlp_bwd_second_call(
        order, after(gb2, sums[0]), dg, fc1_weight, fc2_weight, first, b1_first, hid, br1, gout, proj_weight,
        row(scale_attn), row(ln2_gain))
    gb1_p = swap(gb1_send, "core")
    sums = dw_call(orders["x"], "x", [(n2, n2_p, gpre, gpre_p), (att, att_p, gb1_mine, gb1_p)])
    fc1 = Scatter(orders, sums, "x", fc2.came, out_came)
    fc2.near(sums[0])
    dq0, dkv0, part0 = att_bwd_call(q, kv0, kv0_p, after(gatt, sums[0], fc2.item[0]), att, lse0, 0, 6)
    part0_p = swap(after(part0, fc1.came, fc2.item[1]), "core")
    fc1.near(part0)
    dq1, dkv1, part1 = att_bwd_call(q, kv1, kv1_p, after(gatt, fc1.item[0]), att, lse1, 6, 2)
    mine0, send0 = trip_call(order, dq0, dkv0, after(part0_p, part1))
    part1_p = swap(after(part1, part0_p), "core")
    trip0_p = swap(after(send0, part1_p), "core")
    mine1, send1 = trip_call(order, dq1, dkv1, after(part1_p, send0))
    trip1_p = swap(after(send1, trip0_p), "core")
    sums = dw_call(order, "z", [(after(n1, trip0_p), n1_p, mine0, trip0_p), (n1, n1_p, mine1, trip1_p)])
    mid = Scatter(orders, sums, "z", fc1.item[1])
    fc1.far("z", sums[0])
    fc2.far("x", sums[0])
    own, gtok_send, cls8, *panels = tok_bwd_call(
        orders["x"], (mine0, send0, after(mine1, sums[0], fc1.keep, fc2.keep), send1), qkv_weight, tok, ghid,
        row(ln1_gain), mask_rows, vec_f, vec_b, fc1_vec)
    end = Scatter(orders, panels, "x", fc2.came)
    gtok_came = swap(after(gtok_send, own), "yl")
    mid.near(panels[0])
    end.near()
    end.far("z")
    mid.item[0] = after(mid.item[0], end.keep)
    mid.far("x")
    fc1.came = after(fc1.came, end.came)
    fc1.near()
    end.near()
    fc2.came = after(fc2.came, end.item[0])
    fc2.near()
    mid.near()
    fc2.far("y", merge=(fc1, mid, end))

    out_patches, grad_patches = crops_call(order, out, after(out_came, gtok_send), own, gtok_came, 1.0 - mask_f[..., None])
    cls_part = both(cls8[0], gtok_came[half].astype(F32), 0)
    out_cls = both(out[2 * half], out_came[half], 0)
    fc2.came = after(fc2.came, grad_patches, cls_part, out_cls)
    fc2.near()
    mine, gone, grad_pos = last_sum(order, [fc2.item], cls_part.reshape(16, PAN))
    fc2_g, fc1_g, proj_g, qkv_g, grad_cls, *v = finish(order, mine, swap(gone, "core"))
    v = [a.reshape(-1) for a in v]
    return (out_patches, out_cls, grad_patches, grad_cls, v[8], grad_pos.T, v[6], v[7], qkv_g, v[10],
            proj_g, v[5], v[4], v[2], v[3], fc1_g, v[9], fc2_g, v[1], v[0])


def solution(mesh):
    fine = Mesh(mesh.devices.reshape([SIZES[a] for a in ALL]), ALL)
    img, blk = ("z", "yh", "x"), ("yl", "core")
    every = img + blk
    rep, crops, rows = P(), P(img, None), P(blk, img, None)
    vec, mat = P(every), P(every, None)
    return jax.shard_map(
        local,
        mesh=fine,
        in_specs=(rows, crops, P(blk, img), rep, P(blk, None)) + (rep,) * 14 + (rows, crops),
        out_specs=(rows, crops, rows, crops, vec, P(blk, img), vec, vec, mat, vec, mat, vec, vec, vec, vec, mat, vec, mat,
                   vec, vec),
        check_vma=False,
    )
```

```python
import functools
import itertools

import jax
import jax.numpy as jnp
from jax import lax
from jax.experimental import pallas as pl
from jax.experimental.pallas import tpu as pltpu
from jax.sharding import Mesh
from jax.sharding import PartitionSpec as P

EPS = 1e-06
BF = jnp.bfloat16
F32 = jnp.float32
TAIL = 16
INV_SQRT2 = 0.7071067811865476
INV_SQRT2PI = 0.3989422804014327
PAN = 128

ALL = ("z", "yh", "x", "yl", "core")
SIZES = {"z": 4, "yh": 2, "x": 4, "yl": 2, "core": 2}
Y = ("yh", "yl")


def nn(a, b):
    return jnp.dot(a, b, preferred_element_type=F32)


def nt(a, b):
    return lax.dot_general(a, b, (((1,), (1,)), ((), ())), preferred_element_type=F32)


def tn(a, b):
    return lax.dot_general(a, b, (((0,), (0,)), ((), ())), preferred_element_type=F32)


def params(mib):
    return pltpu.CompilerParams(vmem_limit_bytes=mib << 20)


def cost(macs, nbytes, exps=0):
    return pl.CostEstimate(flops=2 * macs, bytes_accessed=nbytes, transcendentals=exps)


def whole(shape):
    return pl.BlockSpec(shape, lambda *_: (0,) * len(shape))


def sd(shape, dtype=BF):
    return jax.ShapeDtypeStruct(shape, dtype)


def far_in(*arrays):
    return [pltpu.with_memory_space_constraint(a, pltpu.HBM) for a in arrays]


def unit_of(x):
    center = x - jnp.mean(x, -1, keepdims=True)
    inv = lax.rsqrt(jnp.mean(center * center, -1, keepdims=True) + EPS)
    return center * inv, inv


def unit_grad(gu, unit, inv):
    return (gu - jnp.mean(gu, -1, keepdims=True) - unit * jnp.mean(gu * unit, -1, keepdims=True)) * inv


def norm_project_body(x_ref, gain_ref, bias_ref, w_ref, add_ref, normed_ref, out_ref):
    @pl.when(pl.program_id(0) == 0)
    def _():
        unit, _ = unit_of(x_ref[...])
        normed_ref[...] = (unit * gain_ref[...] + bias_ref[...]).astype(BF)

    out_ref[...] = (nn(normed_ref[...], w_ref[...]) + add_ref[...]).astype(BF)


def project_body(scale, x_ref, w_ref, add_ref, out_ref):
    out_ref[...] = ((nn(x_ref[...], w_ref[...]) + add_ref[...]) * scale).astype(BF)


def project_call(x, w, add, at, steps, norm=None, scale=1.0, tile=256):
    rows, width = x.shape
    mat, vec = whole((rows, width)), whole((1, width))
    out = pl.BlockSpec((rows, tile), lambda i: (0, i))
    shape = sd((rows, steps * tile))
    ins = [pl.BlockSpec((width, tile), lambda i: (0, at(i))), pl.BlockSpec((1, tile), lambda i: (0, at(i)))]
    common = dict(grid=(steps,), compiler_params=params(32),
                  cost_estimate=cost(rows * width * steps * tile, 2 * steps * (width * tile + rows * tile)))
    if norm is None:
        return pl.pallas_call(functools.partial(project_body, scale), in_specs=[mat] + ins, out_specs=out,
                              out_shape=shape, name="project", **common)(x, w, add)
    return pl.pallas_call(norm_project_body, in_specs=[mat, vec, vec] + ins, out_specs=[mat, out],
                          out_shape=[sd((rows, width)), shape], name="norm_project", **common)(x, *norm, w, add)


def half_mask(h):
    return (lax.broadcasted_iota(jnp.int32, (1, PAN), 1) // 64) == h


def att_fwd_body(np_, q_ref, ko_ref, vo_ref, kp_ref, vp_ref, *refs, chunk):
    out_ref, lse_ref = refs[-2:]
    rows = q_ref.shape[0]
    k_tail = ko_ref[np_:np_ + TAIL, :]
    v_cls = vo_ref[np_:np_ + 1, :].astype(F32)
    ko, kp = ko_ref[0:np_, :], kp_ref[0:np_, :]
    vo, vp = vo_ref[0:np_, :], vp_ref[0:np_, :]
    for r0 in range(0, rows, chunk):
        q = q_ref[r0:r0 + chunk, :]
        outs, lses = [], []
        for h in range(2):
            qh = jnp.where(half_mask(h), q, jnp.zeros_like(q))
            s1, s2 = nt(qh, ko), nt(qh, kp)
            sc = nt(qh, k_tail)[:, 0:1]
            top = jnp.maximum(jnp.maximum(jnp.max(s1, -1, keepdims=True), jnp.max(s2, -1, keepdims=True)), sc)
            p1, p2, pc = jnp.exp(s1 - top), jnp.exp(s2 - top), jnp.exp(sc - top)
            total = jnp.sum(p1, -1, keepdims=True) + jnp.sum(p2, -1, keepdims=True) + pc
            o = nn(p1.astype(BF), vo) + nn(p2.astype(BF), vp) + pc * v_cls
            outs.append(o / total)
            lses.append(top + jnp.log(total))
        out_ref[r0:r0 + chunk, :] = jnp.where(half_mask(0), outs[0], outs[1]).astype(BF)
        lse_ref[r0:r0 + chunk, :] = jnp.where(half_mask(0), lses[0], lses[1])


def att_fwd_call(q, kv, kv_p, at, pairs, into=None, chunk=264):
    rows, width = q.shape
    np_ = rows - TAIL
    col = lambda a: pl.BlockSpec((rows, PAN), lambda i: (0, a + i))
    ins = [col(at), col(0), col(pairs), col(0), col(pairs)]
    args = far_in(q, kv, kv, kv_p, kv_p)
    if into is not None:
        ins.append(pl.BlockSpec(memory_space=pl.ANY))
        args.append(into)
    return pl.pallas_call(
        functools.partial(att_fwd_body, np_, chunk=chunk),
        grid=(pairs,),
        in_specs=ins,
        out_specs=[col(at), col(0)],
        out_shape=[sd((rows, width)), pltpu.HBM((rows, pairs * PAN), F32)],
        input_output_aliases={} if into is None else {5: 0},
        compiler_params=params(24),
        cost_estimate=cost(rows * 2 * np_ * PAN * 2 * pairs * 2, 2 * rows * PAN * pairs * 8, rows * 2 * np_ * 2 * pairs),
        name="att_fwd",
    )(*args)


def att_bwd_body(np_, q_ref, ko_ref, vo_ref, kp_ref, vp_ref, go_ref, o_ref, lse_ref, dq_ref, own_ref, part_ref):
    q, go = q_ref[...], go_ref[...]
    ko, kp = ko_ref[0:np_, :], kp_ref[0:np_, :]
    vo, vp = vo_ref[0:np_, :], vp_ref[0:np_, :]
    k_tail, v_tail = ko_ref[np_:np_ + TAIL, :], vo_ref[np_:np_ + TAIL, :]
    k_cls = k_tail[0:1].astype(F32)
    qt, gt = q.T, go.T
    qf, gf = q.astype(F32), go.astype(F32)
    prod = gf * o_ref[...].astype(F32)
    dq = dkc = dvc = None
    dk1, dk2, dv1, dv2 = [], [], [], []
    for h in range(2):
        mask = half_mask(h)
        qh = jnp.where(mask, q, jnp.zeros_like(q))
        gh = jnp.where(mask, go, jnp.zeros_like(go))
        delta = jnp.sum(jnp.where(mask, prod, 0.0), -1, keepdims=True)
        lse = lse_ref[:, 64 * h:64 * h + 1]
        qth, gth = qt[64 * h:64 * h + 64], gt[64 * h:64 * h + 64]
        dqh = None
        for k, v, dk, dv in ((ko, vo, dk1, dv1), (kp, vp, dk2, dv2)):
            p = jnp.exp(nt(qh, k) - lse)
            ds = (p * (nt(gh, v) - delta)).astype(BF)
            part = nn(ds, k)
            dqh = part if dqh is None else dqh + part
            dk.append(nn(qth, ds))
            dv.append(nn(gth, p.astype(BF)))
        pc = jnp.exp(nt(qh, k_tail)[:, 0:1] - lse)
        dsc = pc * (nt(gh, v_tail)[:, 0:1] - delta)
        dqh = (dqh + dsc * k_cls) * 0.125
        kc = jnp.sum(dsc * qf, 0, keepdims=True)
        vc = jnp.sum(pc * gf, 0, keepdims=True)
        dq = dqh if h == 0 else jnp.where(mask, dqh, dq)
        dkc = kc if h == 0 else jnp.where(mask, kc, dkc)
        dvc = vc if h == 0 else jnp.where(mask, vc, dvc)
    dq_ref[...] = dq.astype(BF)
    both = lambda parts: jnp.concatenate(parts, 0).T.astype(BF)
    own_ref[0:np_, 0:PAN] = both(dk1)
    own_ref[0:np_, PAN:2 * PAN] = both(dv1)
    part_ref[:, 0:PAN] = both(dk2)
    part_ref[:, PAN:2 * PAN] = both(dv2)
    first = lax.broadcasted_iota(jnp.int32, (TAIL, PAN), 0) == 0
    own_ref[np_:np_ + TAIL, 0:PAN] = jnp.where(first, dkc, 0.0).astype(BF)
    own_ref[np_:np_ + TAIL, PAN:2 * PAN] = jnp.where(first, dvc, 0.0).astype(BF)


def att_bwd_call(q, kv, kv_p, go, o, lse, at, pairs):
    rows = q.shape[0]
    np_ = rows - TAIL
    col = lambda a: pl.BlockSpec((rows, PAN), lambda i: (0, a + i))
    two = lambda n: pl.BlockSpec((n, 2 * PAN), lambda i: (0, i))
    return pl.pallas_call(
        functools.partial(att_bwd_body, np_),
        grid=(pairs,),
        in_specs=[col(at), col(0), col(pairs), col(0), col(pairs), col(at), col(at), col(0)],
        out_specs=[col(0), two(rows), two(np_)],
        out_shape=[sd((rows, pairs * PAN)), sd((rows, pairs * 2 * PAN)), sd((np_, pairs * 2 * PAN))],
        compiler_params=params(32),
        cost_estimate=cost(rows * 2 * np_ * PAN * 5 * pairs * 2, 2 * rows * PAN * pairs * 16, rows * 2 * np_ * 2 * pairs),
        name="att_bwd",
    )(*far_in(q, kv, kv, kv_p, kv_p, go, o, lse))


def trip_body(np_, pairs, order_ref, dq_ref, own_ref, came_ref, mine_ref, send_ref):
    core = order_ref[0]
    n = pairs // 2 * PAN
    for out_ref, side in ((mine_ref, core), (send_ref, 1 - core)):
        out_ref[:, 0:n] = dq_ref[:, pl.ds(pl.multiple_of(side * n, PAN), n)]
        for j in range(pairs // 2):
            for kind in range(2):
                src = pl.ds(pl.multiple_of(side * 2 * n + (2 * j + kind) * PAN, PAN), PAN)
                dst = slice((1 + kind) * n + j * PAN, (1 + kind) * n + (j + 1) * PAN)
                out_ref[0:np_, dst] = (own_ref[0:np_, src].astype(F32) + came_ref[:, src].astype(F32)).astype(BF)
                out_ref[np_:, dst] = own_ref[np_:, src]


def trip_call(order, dq, own, came):
    rows, n = dq.shape
    np_ = rows - TAIL
    shape = sd((rows, n // 2 * 3))
    return pl.pallas_call(
        functools.partial(trip_body, np_, n // PAN),
        grid_spec=pltpu.PrefetchScalarGridSpec(
            num_scalar_prefetch=1, grid=(1,),
            in_specs=[whole(a.shape) for a in (dq, own, came)],
            out_specs=[whole(shape.shape)] * 2),
        out_shape=[shape, shape],
        compiler_params=params(24),
        cost_estimate=cost(0, 2 * rows * n * 8),
        name="trip",
    )(order, dq, own, came)


def mlp_fwd_body(order_ref, att_ref, tok_ref, wp_ref, bp_ref, sa_ref, gain_ref, bias_ref, w1_ref, b1_ref, w2_ref, b2_ref,
                 sm_ref, gout_ref, hid_ref, br1_ref, n2_ref, act_ref, dg_ref, out_ref, gb2_ref, gb2m_ref, gb2s_ref, vec_ref, acc_ref):
    i = pl.program_id(0)

    @pl.when(i == 0)
    def _():
        br1 = nn(att_ref[...], wp_ref[...]) + bp_ref[...]
        br1_ref[...] = br1.astype(BF)
        hid = tok_ref[...] + sa_ref[...] * br1
        hid_ref[...] = hid
        unit, _ = unit_of(hid)
        n2_ref[...] = (unit * gain_ref[...] + bias_ref[...]).astype(BF)

    pre = nn(n2_ref[...], w1_ref[...]) + b1_ref[...]
    cdf = 0.5 + 0.5 * lax.erf(pre * INV_SQRT2)
    act = (pre * cdf).astype(BF)
    act_ref[...] = act
    dg_ref[...] = (cdf + pre * (jnp.exp(-0.5 * pre * pre) * INV_SQRT2PI)).astype(BF)
    part = nn(act, w2_ref[...])

    @pl.when(i == 0)
    def _():
        acc_ref[...] = part

    @pl.when(i > 0)
    def _():
        acc_ref[...] += part

    @pl.when(i == pl.num_programs(0) - 1)
    def _():
        br2 = acc_ref[...] + b2_ref[...]
        out_ref[...] = (hid_ref[...] + sm_ref[...] * br2).astype(BF)
        gout = gout_ref[...].astype(F32)
        gb2 = (sm_ref[...] * gout).astype(BF)
        gb2_ref[...] = gb2
        vec_ref[0:1, :] = jnp.sum(gout * br2, 0, keepdims=True)
        vec_ref[1:2, :] = jnp.sum(gb2.astype(F32), 0, keepdims=True)
        n = gb2s_ref.shape[1]
        gb2m_ref[...] = gb2_ref[:, pl.ds(pl.multiple_of(order_ref[0] * n, PAN), n)]
        gb2s_ref[...] = gb2_ref[:, pl.ds(pl.multiple_of((1 - order_ref[0]) * n, PAN), n)]


def mlp_fwd_call(order, att, tok, wp, bp, sa, gain, bias, w1, b1, w2, b2, sm, gout, tile=512):
    rows, width = tok.shape
    ff = w1.shape[1]
    mat, vec = whole((rows, width)), whole((1, width))
    col = pl.BlockSpec((rows, tile), lambda i, c: (0, i))
    return pl.pallas_call(
        mlp_fwd_body,
        grid_spec=pltpu.PrefetchScalarGridSpec(
            num_scalar_prefetch=1,
            grid=(ff // tile,),
            in_specs=[mat, mat, whole((width, width)), vec, vec, vec, vec,
                      pl.BlockSpec((width, tile), lambda i, c: (0, i)), pl.BlockSpec((1, tile), lambda i, c: (0, i)),
                      pl.BlockSpec((tile, width), lambda i, c: (i, 0)), vec, vec, mat],
            out_specs=[mat, mat, mat, col, col, mat, mat] + [whole((rows, width // 2))] * 2 + [whole((8, width))],
            scratch_shapes=[pltpu.VMEM((rows, width), F32)]),
        out_shape=[sd((rows, width), F32), pltpu.HBM((rows, width), BF), sd((rows, width)), sd((rows, ff)), pltpu.HBM((rows, ff), BF),
                   sd((rows, width)), sd((rows, width))] + [sd((rows, width // 2))] * 2 + [sd((8, width), F32)],
        compiler_params=params(36),
        cost_estimate=cost(rows * width * (2 * ff + width), 2 * (2 * width * ff + 2 * rows * ff + 6 * rows * width), rows * ff),
        name="mlp_fwd",
    )(order, att, tok, wp, bp, sa, gain, bias, w1, b1, w2, b2, sm, gout)


def mlp_bwd_step(gb2_ref, dg_ref, w1_ref, w2_ref, gpre_ref, b1_ref, at):
    gpre = (nt(gb2_ref[...], w2_ref[...]) * dg_ref[...].astype(F32)).astype(BF)
    gpre_ref[...] = gpre
    b1_ref[0:1, at] = jnp.sum(gpre.astype(F32), 0, keepdims=True)
    return nt(gpre, w1_ref[...])


def mlp_bwd_first_body(order_ref, gb2_ref, dg_ref, w1_ref, w2_ref, gpre_ref, b1_ref, acc_ref):
    i = pl.program_id(0)
    part = mlp_bwd_step(gb2_ref, dg_ref, w1_ref, w2_ref, gpre_ref, b1_ref, slice(None))

    @pl.when(i == 0)
    def _():
        acc_ref[...] = part

    @pl.when(i > 0)
    def _():
        acc_ref[...] += part


def mlp_bwd_second_body(order_ref, gb2_ref, dg_ref, w1_ref, w2_ref, first_ref, b1_first_ref, hid_ref, br1_ref, gout_ref,
                        wp_ref, sa_ref, gain_ref, gpre_ref, b1_ref, ghid_ref, gb1_ref, gb1m_ref, gb1s_ref, gatt_ref,
                        vec_ref, acc_ref):
    i = pl.program_id(0)
    core = order_ref[0]
    tile, half = gpre_ref.shape[1], b1_first_ref.shape[1]
    part = mlp_bwd_step(gb2_ref, dg_ref, w1_ref, w2_ref, gpre_ref, b1_ref,
                        pl.ds(pl.multiple_of(core * half + i * tile, PAN), tile))

    @pl.when(i == 0)
    def _():
        acc_ref[...] = first_ref[...] + part
        b1_ref[0:1, pl.ds(pl.multiple_of((1 - core) * half, PAN), half)] = b1_first_ref[0:1, :]

    @pl.when(i > 0)
    def _():
        acc_ref[...] += part

    @pl.when(i == pl.num_programs(0) - 1)
    def _():
        unit, inv = unit_of(hid_ref[...])
        gn = acc_ref[...]
        vec_ref[0:1, :] = jnp.sum(gn * unit, 0, keepdims=True)
        vec_ref[1:2, :] = jnp.sum(gn, 0, keepdims=True)
        ghid = gout_ref[...].astype(F32) + unit_grad(gn * gain_ref[...], unit, inv)
        ghid_ref[...] = ghid
        vec_ref[2:3, :] = jnp.sum(ghid * br1_ref[...].astype(F32), 0, keepdims=True)
        gb1 = (sa_ref[...] * ghid).astype(BF)
        gb1_ref[...] = gb1
        vec_ref[3:4, :] = jnp.sum(gb1.astype(F32), 0, keepdims=True)
        n = gb1s_ref.shape[1]
        gb1m_ref[...] = gb1_ref[:, pl.ds(pl.multiple_of(core * n, PAN), n)]
        gb1s_ref[...] = gb1_ref[:, pl.ds(pl.multiple_of((1 - core) * n, PAN), n)]
        gatt_ref[...] = nt(gb1, wp_ref[...]).astype(BF)


def mlp_bwd_specs(rows, width, ff, tile, mine):
    half = ff // tile // 2
    at = lambda i, c: i + half * (c[0] if mine else 1 - c[0])
    col = lambda n: pl.BlockSpec((n, tile), lambda i, c: (0, at(i, c)))
    return half, [whole((rows, width)), col(rows), col(width), pl.BlockSpec((tile, width), lambda i, c: (at(i, c), 0))]


def mlp_bwd_first_call(order, gb2, dg, w1, w2, tile=512):
    rows, width = gb2.shape
    ff = w1.shape[1]
    half, ins = mlp_bwd_specs(rows, width, ff, tile, False)
    return pl.pallas_call(
        mlp_bwd_first_body,
        grid_spec=pltpu.PrefetchScalarGridSpec(
            num_scalar_prefetch=1, grid=(half,), in_specs=ins,
            out_specs=[pl.BlockSpec((rows, tile), lambda i, c: (0, i)), pl.BlockSpec((8, tile), lambda i, c: (0, i)),
                       whole((rows, width))]),
        out_shape=[sd((rows, ff // 2)), sd((8, ff // 2), F32), sd((rows, width), F32)],
        compiler_params=params(24),
        cost_estimate=cost(rows * width * ff, 2 * (width * ff + rows * ff)),
        name="mlp_bwd_first",
    )(order, gb2, *far_in(dg, w1, w2))


def mlp_bwd_second_call(order, gb2, dg, w1, w2, first, b1_first, hid, br1, gout, wp, sa, gain, tile=512):
    rows, width = hid.shape
    ff = w1.shape[1]
    half, ins = mlp_bwd_specs(rows, width, ff, tile, True)
    mat, vec, halfm = whole((rows, width)), whole((1, width)), whole((rows, width // 2))
    return pl.pallas_call(
        mlp_bwd_second_body,
        grid_spec=pltpu.PrefetchScalarGridSpec(
            num_scalar_prefetch=1, grid=(half,),
            in_specs=ins + [mat, whole((8, ff // 2)), mat, mat, mat, whole((width, width)), vec, vec],
            out_specs=[pl.BlockSpec((rows, tile), lambda i, c: (0, i)), whole((8, ff)), mat, mat, halfm, halfm, mat,
                       whole((8, width))],
            scratch_shapes=[pltpu.VMEM((rows, width), F32)]),
        out_shape=[sd((rows, ff // 2)), sd((8, ff), F32), sd((rows, width), F32), sd((rows, width)),
                   sd((rows, width // 2)), sd((rows, width // 2)), sd((rows, width)), sd((8, width), F32)],
        compiler_params=params(32),
        cost_estimate=cost(rows * width * (ff + width), 2 * (width * ff + rows * ff + 6 * rows * width)),
        name="mlp_bwd_second",
    )(order, gb2, *far_in(dg, w1, w2), first, b1_first, hid, br1, gout, wp, sa, gain)


def vector_panels(vectors, z):
    r = lax.broadcasted_iota(jnp.int32, (256, 1), 0)
    device = jnp.where(r % 16 < 2, r // 16 * 2 + r % 16, -1)
    total, at = None, 0
    for vector in vectors:
        n = vector.shape[1] // 4
        per = n // 32
        lane = lax.broadcasted_iota(jnp.int32, (1, n), 1)
        spread = jnp.where(lane // per == device, vector[:, z * n:(z + 1) * n], 0.0).astype(BF)
        pick_r = lax.broadcasted_iota(jnp.int32, (n, PAN), 0)
        pick_c = lax.broadcasted_iota(jnp.int32, (n, PAN), 1)
        part = nn(spread, jnp.where(pick_r % per + at == pick_c, 1.0, 0.0).astype(BF))
        total = part if total is None else total + part
        at += per
    return total.astype(BF)


def stacked(a0, a1):
    n = a0.shape[0] - TAIL
    return jnp.concatenate((a0[0:n], a1[0:n], a0[n:], a1[n:]), 0)


def dw_body(jobs, axis, order_ref, *refs):
    send_ref, keep_ref = refs[-2:]
    i = pl.program_id(0)
    done, at, base = [], 0, 0
    for rows, panels in jobs:
        a0, a1, g0, g1 = (ref[...] for ref in refs[at:at + 4])
        done.append((tn(stacked(a0, a1), stacked(g0, g1)).astype(BF), base, rows))
        at, base = at + 4, base + panels

    def write(ref, place, xs):
        for value, first, rows in done:
            n = value.shape[1] // PAN
            for yh, x, yl, rg, pc in itertools.product(range(2), xs, range(2), range(rows // 16), range(n)):
                r0 = ((yh * 4 + x) * 2 + yl) * rows + rg * 16
                ref[place(yh, x, yl) + (first + rg * n + pc,)] = value[r0:r0 + 16, pc * PAN:(pc + 1) * PAN]

    if axis == "z":
        place = lambda yh, x, yl: (0, yh, x, yl)
        pl.when(i < 2)(lambda: write(send_ref, place, range(4)))
        pl.when(i >= 2)(lambda: write(keep_ref, place, range(4)))
    else:
        for target in range(4):
            slot = order_ref[5 + target]
            pl.when(slot < 2)(lambda: write(send_ref, lambda yh, x, yl: (slot, 0, yh, yl), (target,)))
            pl.when(slot >= 2)(lambda: write(keep_ref, lambda yh, x, yl: (slot - 2, 0, yh, yl), (target,)))


def dw_call(order, axis, jobs):
    ins, args, shapes, macs = [], [], [], 0
    at = (lambda i, c: c[1 + i]) if axis == "z" else (lambda i, c: i)
    for a0, a1, g0, g1 in jobs:
        rows, k = a0.shape
        n = g0.shape[1]
        lhs = pl.BlockSpec((rows, k // 4), lambda i, c: (0, at(i, c)))
        ins += [lhs, lhs, whole((rows, n)), whole((rows, n))]
        args += far_in(a0, a1) + [g0, g1]
        shapes.append((k // 64, k // 1024 * (n // PAN)))
        macs += 2 * rows * k * n
    panels = sum(p for _, p in shapes)
    if axis == "z":
        out = (2, 2, 4, 2, panels, 16, PAN)
        block = lambda f: pl.BlockSpec((1,) + out[1:], lambda i, c: (f(i),) + (0,) * 6)
        outs = [block(lambda i: jnp.minimum(i, 1)), block(lambda i: jnp.maximum(i - 2, 0))]
    else:
        out = (2, 4, 2, 2, panels, 16, PAN)
        outs = [pl.BlockSpec((2, 1) + out[2:], lambda i, c: (0, i) + (0,) * 5)] * 2
    return pl.pallas_call(
        functools.partial(dw_body, tuple(shapes), axis),
        grid_spec=pltpu.PrefetchScalarGridSpec(num_scalar_prefetch=1, grid=(4,), in_specs=ins, out_specs=outs),
        out_shape=[sd(out), pltpu.HBM(out, BF)],
        compiler_params=params(24),
        cost_estimate=cost(macs, 2 * sum(a.size for a in args) + 8 * 64 * panels * 16 * PAN),
        name="dw",
    )(order, *args)


def tok_bwd_body(half, order_ref, g0_mine, g0_send, g1_mine, g1_send, *refs):
    w0, w1 = refs[0:3], refs[3:6]
    (tok_ref, ghid_ref, gain_ref, mask_ref, vf_ref, vb_ref, b1_ref, own_ref, send_ref, cls_ref, *panel_refs,
     qv_ref, pos_ref, vecs_ref, acc_ref) = refs[6:]
    i = pl.program_id(0)
    width = tok_ref.shape[1]
    core = order_ref[0]
    first = 0
    for step, (g_ref, ws) in enumerate(((g0_mine, w0), (g0_send, w0), (g1_mine, w1), (g1_send, w1))):
        n = ws[0].shape[1]
        side = core if step % 2 == 0 else 1 - core

        @pl.when(i == step)
        def _():
            part = sum(nt(g_ref[:, j * n:(j + 1) * n], w[...]) for j, w in enumerate(ws))
            if step == 0:
                acc_ref[...] = part
            else:
                acc_ref[...] += part
            sums = jnp.sum(g_ref[...].astype(F32), 0, keepdims=True)
            at = pl.multiple_of(first + side * n, PAN)
            qv_ref[0:1, pl.ds(at, n)] = sums[:, 0:n]
            qv_ref[0:1, pl.ds(width + at, n)] = sums[:, 2 * n:]

        if step == 1:
            first = 2 * n

    @pl.when(i == 3)
    def _():
        unit, inv = unit_of(tok_ref[...])
        gn = acc_ref[...]
        gtok = ghid_ref[...] + unit_grad(gn * gain_ref[...], unit, inv)
        own_ref[...] = gtok[0:half]
        send_ref[...] = gtok[half:].astype(BF)
        cls_ref[...] = gtok[2 * half:2 * half + 8]
        pos_ref[...] = gtok[0:2 * half].T.astype(BF)
        column = lambda v: jnp.sum(v, 0, keepdims=True)
        vectors = [vf_ref[0:1, :], vf_ref[1:2, :]] + [vb_ref[j:j + 1, :] for j in range(4)]
        vectors += [column(gn * unit), column(gn), column(gtok * mask_ref[:, 0:1].astype(F32)), b1_ref[0:1, :],
                    qv_ref[0:1, :]]
        for z in range(4):
            vecs_ref[z] = vector_panels(vectors, z)
        for slot in range(4):
            ref = panel_refs[slot // 2]
            target = order_ref[1 + slot]
            for z, yh, part in itertools.product(range(4), range(2), range(2)):
                rows = pl.ds(pl.multiple_of(z * 256 + (yh * 4 + target) * 32 + part * 16, 16), 16)
                for side, pc in itertools.product(range(2), range(2)):
                    yl = order_ref[9] if side == 0 else 1 - order_ref[9]
                    c0 = side * half + pc * PAN
                    ref[slot % 2, z, yh, yl, part * 2 + pc] = pos_ref[rows, c0:c0 + PAN]
                chip = pl.ds(pl.multiple_of((yh * 4 + target) * 32 + part * 16, 16), 16)
                ref[slot % 2, z, yh, part, 4] = vecs_ref[z, chip, :]


def tok_bwd_call(order, gs, w, tok, ghid, gain, mask, vf, vb, b1):
    rows, width = tok.shape
    half = (rows - TAIL) // 2
    mat, vec = whole((rows, width)), whole((1, width))
    n0, n1 = gs[0].shape[1] // 3, gs[2].shape[1] // 3
    panels = (2, 4, 2, 2, 5, 16, PAN)
    side = lambda i, c: jnp.where(i % 2 == 0, c[0], 1 - c[0])
    ws = [pl.BlockSpec((pl.Element(width), pl.Element(n0)),
                       lambda i, c, j=j: (0, pl.multiple_of(j * width + side(jnp.minimum(i, 1), c) * n0, PAN))) for j in range(3)]
    ws += [pl.BlockSpec((pl.Element(width), pl.Element(n1)),
                        lambda i, c, j=j: (0, pl.multiple_of(j * width + 2 * n0 + side(jnp.maximum(i, 2), c) * n1, PAN)))
           for j in range(3)]
    return pl.pallas_call(
        functools.partial(tok_bwd_body, half),
        grid_spec=pltpu.PrefetchScalarGridSpec(
            num_scalar_prefetch=1,
            grid=(4,),
            in_specs=[whole(g.shape) for g in gs] + ws + [mat, mat, vec, whole((rows, PAN))]
            + [whole(v.shape) for v in (vf, vb, b1)],
            out_specs=[whole((half, width)), whole((half + TAIL, width)), whole((8, width))] + [whole(panels)] * 2,
            scratch_shapes=[pltpu.VMEM((8, 2 * width), F32), pltpu.VMEM((width, 2 * half), BF),
                            pltpu.VMEM((4, 256, PAN), BF), pltpu.VMEM((rows, width), F32)]),
        out_shape=[sd((half, width), F32), sd((half + TAIL, width)), sd((8, width), F32)] + [sd(panels)] * 2,
        compiler_params=params(36),
        cost_estimate=cost(rows * width * 3 * width, 2 * (3 * width * width + 8 * rows * width)),
        name="tok_bwd",
    )(order, *gs, *[w] * 6, tok, ghid, gain, mask, vf, vb, b1)


def near_sum_body(keep_ref, came_ref, kept_ref, send_ref):
    kept_ref[...] = keep_ref[0].astype(F32) + came_ref[0].astype(F32)
    send_ref[...] = (keep_ref[1].astype(F32) + came_ref[1].astype(F32)).astype(BF)


def near_sum(keep, came, parts=4):
    shape = keep.shape
    m = keep.size // (2 * 16 * PAN)
    flat = lambda a: a.reshape(2, m, 16, PAN)
    parts = parts if m % parts == 0 and m >= 16 else 1
    two = pl.BlockSpec((2, m // parts, 16, PAN), lambda i: (0, i, 0, 0))
    one = pl.BlockSpec((m // parts, 16, PAN), lambda i: (i, 0, 0))
    kept, send = pl.pallas_call(
        near_sum_body, grid=(parts,), in_specs=[two, two], out_specs=[one, one],
        out_shape=[sd((m, 16, PAN), F32), sd((m, 16, PAN))],
        compiler_params=params(24), cost_estimate=cost(0, keep.size * 6), name="near_sum",
    )(flat(keep), flat(came))
    return kept.reshape(shape[1:]), send.reshape(shape[1:])


def far_sum_body(labels, axis, counts, order_ref, *refs):
    ins, outs = refs[:-2], refs[-2:]
    for slot in range(4):
        target = order_ref[1 + slot]
        place = {"y": {"yh": target // 2, "yl": target % 2}}.get(axis, {axis: target})
        where = tuple(place.get(label, slice(None)) for label in labels)
        out = outs[slot // 2]
        at, j = 0, 0
        for count in counts:
            n = ins[j].shape[-3]
            total = ins[j][where].astype(F32)
            for came in ins[j + 1:j + count]:
                total = total + came[where].astype(F32)
            out[(slot % 2,) + (slice(None),) * (total.ndim - 3) + (slice(at, at + n),)] = total.astype(out.dtype)
            at += n
            j += count


def far_sum(order, items, labels, axis):
    gone = ("yh", "yl") if axis == "y" else (axis,)
    left = [l for l in labels if l not in gone]
    panels = sum(item[0].shape[-3] for item in items)
    out = (2,) + tuple(SIZES[l] for l in left) + (panels, 16, PAN)
    args = [a for item in items for a in item]
    outs = [sd(out), sd(out, F32)]
    return left, pl.pallas_call(
        functools.partial(far_sum_body, labels, axis, tuple(len(item) for item in items)),
        grid_spec=pltpu.PrefetchScalarGridSpec(
            num_scalar_prefetch=1, grid=(1,),
            in_specs=[whole(a.shape) for a in args],
            out_specs=[whole(o.shape) for o in outs]),
        out_shape=outs,
        compiler_params=params(24), cost_estimate=cost(0, sum(a.size for a in args) * 6), name="far_sum",
    )(order, *args)


def last_sum_body(counts, order_ref, *refs):
    ins, (cls_ref, mine_ref, gone_ref, pos_ref, tot_ref) = refs[:-5], refs[-5:]
    core = order_ref[0]
    at, j = 0, 0
    for count in counts:
        total = ins[j][...]
        for came in ins[j + 1:j + count]:
            total = total + came[...].astype(F32)
        tot_ref[at:at + total.shape[0]] = total
        at += total.shape[0]
        j += count
    at = 0

    def put(panel, start):
        nonlocal at
        for ref, side in ((mine_ref, core), (gone_ref, 1 - core)):
            ref[at] = tot_ref[panel, pl.ds(pl.multiple_of(start(side), 8), 8), :]
        at += 1

    for rg, pc, part in itertools.product(range(2), range(4), range(2)):
        for ref, side in ((mine_ref, core), (gone_ref, 1 - core)):
            ref[at] = tot_ref[(2 * side + rg) * 4 + pc, 8 * part:8 * part + 8, :]
        at += 1
    for panel in range(16, 48):
        put(panel, lambda side: side * 8)
    mine_ref[at] = tot_ref[52, 0:8, :]
    gone_ref[at] = tot_ref[52, 0:8, :]
    for part in range(2):
        mine_ref[at + 1 + part] = cls_ref[8 * part:8 * part + 8, :]
        gone_ref[at + 1 + part] = cls_ref[8 * part:8 * part + 8, :]
    for rg, pc in itertools.product(range(2), range(2)):
        pos_ref[16 * rg:16 * rg + 16, pc * PAN:(pc + 1) * PAN] = tot_ref[48 + rg * 2 + pc]


SWAPPED = 16 + 32 + 3


def last_sum(order, items, cls16):
    shape = sd((SWAPPED, 8, PAN), F32)
    args = [a for item in items for a in item] + [cls16]
    panels = sum(item[0].shape[0] for item in items)
    return pl.pallas_call(
        functools.partial(last_sum_body, tuple(len(item) for item in items)),
        grid_spec=pltpu.PrefetchScalarGridSpec(
            num_scalar_prefetch=1, grid=(1,),
            in_specs=[whole(a.shape) for a in args],
            out_specs=[whole(shape.shape), whole(shape.shape), whole((32, 256))],
            scratch_shapes=[pltpu.VMEM((panels, 16, PAN), F32)]),
        out_shape=[shape, shape, sd((32, 256), F32)],
        compiler_params=params(24), cost_estimate=cost(0, panels * 2048 * 10), name="last_sum",
    )(order, *args)


def finish_body(order_ref, mine_ref, came_ref, fc2_ref, fc1_ref, proj_ref, qkv_ref, cls_ref, *vec_refs):
    first = order_ref[0] == 0
    at = 0

    def halves():
        nonlocal at
        mine, came = mine_ref[at], came_ref[at]
        at += 1
        return jnp.where(first, mine, came), jnp.where(first, came, mine)

    for rg, pc, part in itertools.product(range(2), range(4), range(2)):
        r0 = rg * 16 + part * 8
        for h, value in enumerate(halves()):
            fc2_ref[r0:r0 + 8, 512 * h + pc * PAN:512 * h + (pc + 1) * PAN] = value
    for pc in range(16):
        for h, value in enumerate(halves()):
            fc1_ref[:, 2048 * h + pc * PAN:2048 * h + (pc + 1) * PAN] = value
    for pc in range(4):
        for h, value in enumerate(halves()):
            proj_ref[:, 512 * h + pc * PAN:512 * h + (pc + 1) * PAN] = value
    for c0, per in ((0, 3), (768, 1)):
        for kind, pc in itertools.product(range(3), range(per)):
            for h, value in enumerate(halves()):
                at0 = kind * 1024 + c0 + (h * per + pc) * PAN
                qkv_ref[:, at0:at0 + PAN] = value
    both = mine_ref[at] + came_ref[at]
    row = jnp.where(first, both[0:1], both[1:2])
    start = 0
    for ref in vec_refs:
        n = ref.shape[1]
        ref[...] = row[:, start:start + n]
        start += n
    for part in range(2):
        total = mine_ref[at + 1 + part] + came_ref[at + 1 + part]
        for j in range(8):
            cls_ref[part:part + 1, j * PAN:(j + 1) * PAN] = total[j:j + 1]


def finish(order, mine, came):
    outs = [(32, 1024), (8, 4096), (8, 1024), (8, 3072), (2, 1024)] + [(1, 8)] * 9 + [(1, 32), (1, 16)]
    return pl.pallas_call(
        finish_body,
        grid_spec=pltpu.PrefetchScalarGridSpec(
            num_scalar_prefetch=1, grid=(1,), in_specs=[whole(mine.shape)] * 2, out_specs=[whole(s) for s in outs]),
        out_shape=[sd(s, F32) for s in outs],
        compiler_params=params(24), cost_estimate=cost(0, mine.size * 16), name="finish",
    )(order, mine, came)


def crops_body(order_ref, out_ref, out_came_ref, own_ref, came_ref, keep_ref, patches_ref, grad_ref):
    mine = lax.broadcasted_iota(jnp.int32, (1, 2, 1), 1) == order_ref[9]
    wide = lambda t: jnp.broadcast_to(t[:, None, :].astype(F32), (t.shape[0], 2, t.shape[1]))
    patches_ref[...] = jnp.where(mine, wide(out_ref[...]), wide(out_came_ref[...])).astype(BF)
    grad_ref[...] = jnp.where(mine, wide(own_ref[...]), wide(came_ref[...])) * keep_ref[...]


def crops_call(order, out, out_came, own, came, keep, parts=4):
    half, width = own.shape
    n = half // parts
    rows = pl.BlockSpec((n, width), lambda i, c: (i, 0))
    both = pl.BlockSpec((n, 2, width), lambda i, c: (i, 0, 0))
    return pl.pallas_call(
        crops_body,
        grid_spec=pltpu.PrefetchScalarGridSpec(
            num_scalar_prefetch=1, grid=(parts,),
            in_specs=[rows] * 4 + [pl.BlockSpec((n, 2, 1), lambda i, c: (i, 0, 0))], out_specs=[both, both]),
        out_shape=[sd((half, 2, width)), sd((half, 2, width), F32)],
        compiler_params=params(20), cost_estimate=cost(0, 22 * half * width), name="crops",
    )(order, out, out_came, own, came, keep)


def swap(x, axis):
    return lax.ppermute(x, axis, [(0, 1), (1, 0)])


def after(x, *others):
    return lax.optimization_barrier((x,) + others)[0] if others else x


def partners(axis, turn):
    pairs = []
    for z, yh, x, yl, core in itertools.product(*(range(SIZES[a]) for a in ALL)):
        at = {"z": z, "y": yh * 2 + yl, "x": x}
        flat = lambda p: (((p["z"] * 2 + p["y"] // 2) * 4 + p["x"]) * 2 + p["y"] % 2) * 2 + core
        there = dict(at)
        there[axis] ^= 1 if core == turn else 3
        pairs.append((flat(at), flat(there)))
    return pairs


def pass_on(x, axis, turn):
    return lax.ppermute(x, ALL, partners(axis, turn))


def order_of(axis):
    me = lax.axis_index("yh") * 2 + lax.axis_index("yl") if axis == "y" else lax.axis_index(axis)
    first = jnp.where(lax.axis_index("core") == 0, 1, 3)
    targets = [me ^ first, me ^ 2, me, me ^ first ^ 2]
    places = [sum(jnp.where(t == want, at, 0) for at, t in enumerate(targets)) for want in range(4)]
    return jnp.stack([lax.axis_index("core")] + targets + places + [lax.axis_index("yl")]).astype(jnp.int32)


class Scatter:
    def __init__(self, orders, sums, axis, *others):
        self.orders, self.axis = orders, axis
        self.labels = {"z": ["yh", "x", "yl"], "x": ["z", "yh", "yl"]}[axis]
        self.begin(sums, others)

    def begin(self, sums, others):
        send, self.keep = sums
        self.came = pass_on(after(send, *others), self.axis, 0)

    def near(self, *others):
        kept, send = near_sum(self.keep, self.came)
        self.item = [kept, pass_on(after(send, *others), self.axis, 1)]

    def far(self, axis, *others, merge=()):
        items = [s.item for s in (self,) + tuple(merge)]
        self.labels, sums = far_sum(self.orders[axis], items, self.labels, axis)
        self.axis = axis
        self.begin(sums, others)


def local(patches, cls_tokens, patch_masks, mask_token, pos_embed, ln1_gain, ln1_bias, qkv_weight, qv_bias, proj_weight,
          proj_bias, scale_attn, ln2_gain, ln2_bias, fc1_weight, fc1_bias, fc2_weight, fc2_bias, scale_mlp, cot_patches,
          cot_cls):
    half, _, width = patches.shape
    core, yl = lax.axis_index("core"), lax.axis_index("yl")
    row = lambda v: v.reshape(1, -1)
    sides = lambda a: (jnp.where(yl == 0, a[:, 0], a[:, 1]), jnp.where(yl == 0, a[:, 1], a[:, 0]))
    both = lambda mine, other, axis: jnp.where(yl == 0, jnp.stack((mine, other), axis), jnp.stack((other, mine), axis))
    pad = jnp.zeros((TAIL - 1, width), BF)
    orders = {a: order_of(a) for a in "zxy"}
    order = orders["z"]

    mask_f = patch_masks.astype(F32)
    mask3 = patch_masks[..., None]
    mixed = jnp.where(mask3 != 0, mask_token, patches)
    own, send = sides(mixed)
    came = swap(send, "yl")
    pos_came = lax.ppermute(pos_embed, Y, [(0, 3), (3, 0), (1, 2), (2, 1)])
    cls_row = jnp.where(yl == 0, cls_tokens[0:1], cls_tokens[1:2])
    tok = jnp.concatenate((own.astype(F32) + pos_embed.astype(F32), came.astype(F32) + pos_came.astype(F32),
                           cls_row.astype(F32), pad.astype(F32)), 0)

    add = row(jnp.concatenate((qv_bias[:width], jnp.zeros((width,), F32), qv_bias[width:])))
    n1, kv0 = project_call(tok, qkv_weight, add, lambda i: 4 + i % 3 + i // 3 * 4, 6, norm=(row(ln1_gain), row(ln1_bias)))
    kv0_p = swap(kv0, "core")
    kv1 = project_call(after(n1, kv0), qkv_weight, add, lambda i: 7 + i * 4, 2)
    q = project_call(after(n1, kv1), qkv_weight, add, lambda i: i, 2, scale=0.125, tile=512)
    kv1_p = swap(after(kv1, kv0_p), "core")

    mask_own, mask_send = sides(mask_f)
    cot_own, cot_send = sides(jnp.where(mask3 != 0, cot_patches, jnp.zeros_like(cot_patches)))
    lanes = lambda m: jnp.broadcast_to(m.astype(BF)[:, None], (half, PAN))
    cot_came = swap(after(jnp.concatenate((cot_send, lanes(mask_send)), 1), came, q), "yl")

    att, lse0 = att_fwd_call(after(q, kv0_p), kv0, kv0_p, 0, 6)
    n1_p = swap(after(n1, kv1_p), "core")
    att, lse1 = att_fwd_call(after(q, cot_came, n1_p), kv1, kv1_p, 6, 2, into=att)
    cot_came = after(cot_came, att)
    att_p = swap(after(att, n1_p), "core")
    cls_cot = jnp.where(yl == 0, cot_cls[0:1], cot_cls[1:2]) * (core == 0).astype(BF)
    gout = jnp.concatenate((cot_own, cot_came[:, :width], cls_cot, pad), 0)
    mask_rows = jnp.concatenate((lanes(mask_own), cot_came[:, width:], jnp.zeros((TAIL, PAN), BF)), 0)
    hid, br1, n2, act, dg, out, gb2, gb2_mine, gb2_send, vec_f = mlp_fwd_call(
        order, att, tok, proj_weight, row(proj_bias), row(scale_attn), row(ln2_gain), row(ln2_bias), fc1_weight,
        row(fc1_bias), fc2_weight, row(fc2_bias), row(scale_mlp), gout)

    act_p = swap(after(act, att_p), "core")
    gb2_p = swap(gb2_send, "core")
    gpre_send, b1_first, first = mlp_bwd_first_call(order, gb2, dg, fc1_weight, fc2_weight)
    gpre_p = swap(after(gpre_send, act_p, gb2_p), "core")
    n2_p = swap(after(n2, act_p, gb2_p, gpre_send), "core")
    sums = dw_call(order, "z", [(act, act_p, gb2_mine, gb2_p)])
    fc2 = Scatter(orders, sums, "z", gpre_p, n2_p)
    out_came = swap(after(out[half:], gpre_p, n2_p, sums[0]), "yl")
    gpre, fc1_vec, ghid, gb1, gb1_mine, gb1_send, gatt, vec_b = mlp_bwd_second_call(
        order, after(gb2, sums[0]), dg, fc1_weight, fc2_weight, first, b1_first, hid, br1, gout, proj_weight,
        row(scale_attn), row(ln2_gain))
    gb1_p = swap(gb1_send, "core")
    sums = dw_call(orders["x"], "x", [(n2, n2_p, gpre, gpre_p)])
    fc1 = Scatter(orders, sums, "x", fc2.came, out_came, gb1_p)
    fc2.near(sums[0])
    dq0, dkv0, part0 = att_bwd_call(q, kv0, kv0_p, after(gatt, sums[0], fc2.item[0]), att, lse0, 0, 6)
    part0_p = swap(after(part0, fc1.came, fc2.item[1]), "core")
    fc1.near(part0)
    dq1, dkv1, part1 = att_bwd_call(q, kv1, kv1_p, after(gatt, fc1.item[0]), att, lse1, 6, 2)
    mine0, send0 = trip_call(order, dq0, dkv0, after(part0_p, part1))
    part1_p = swap(after(part1, part0_p), "core")
    trip0_p = swap(after(send0, part1_p), "core")
    mine1, send1 = trip_call(order, dq1, dkv1, after(part1_p, send0))
    trip1_p = swap(after(send1, trip0_p), "core")
    sums = dw_call(order, "z", [(att, att_p, gb1_mine, gb1_p), (after(n1, trip0_p), n1_p, mine0, trip0_p),
                                (n1, n1_p, mine1, trip1_p)])
    mid = Scatter(orders, sums, "z", fc1.item[1])
    fc1.far("z", sums[0])
    fc2.far("x", sums[0])
    own, gtok_send, cls8, *panels = tok_bwd_call(
        orders["x"], (mine0, send0, after(mine1, sums[0], fc1.keep, fc2.keep), send1), qkv_weight, tok, ghid,
        row(ln1_gain), mask_rows, vec_f, vec_b, fc1_vec)
    end = Scatter(orders, panels, "x", fc2.came)
    gtok_came = swap(after(gtok_send, own), "yl")
    mid.came = after(mid.came, end.came)
    end.near()
    mid.near(end.item[0])
    end.far("z")
    mid.item[0] = after(mid.item[0], end.keep)
    mid.far("x")
    fc1.came = after(fc1.came, end.came)
    fc1.near()
    end.near()
    fc2.came = after(fc2.came, end.item[0])
    fc2.near()
    mid.near()
    fc2.far("y", merge=(fc1, mid, end))

    out_patches, grad_patches = crops_call(order, out, after(out_came, gtok_send), own, gtok_came, 1.0 - mask_f[..., None])
    cls_part = both(cls8[0], gtok_came[half].astype(F32), 0)
    out_cls = both(out[2 * half], out_came[half], 0)
    fc2.came = after(fc2.came, grad_patches, cls_part, out_cls)
    fc2.near()
    mine, gone, grad_pos = last_sum(order, [fc2.item], cls_part.reshape(16, PAN))
    fc2_g, fc1_g, proj_g, qkv_g, grad_cls, *v = finish(order, mine, swap(gone, "core"))
    v = [a.reshape(-1) for a in v]
    return (out_patches, out_cls, grad_patches, grad_cls, v[8], grad_pos.T, v[6], v[7], qkv_g, v[10],
            proj_g, v[5], v[4], v[2], v[3], fc1_g, v[9], fc2_g, v[1], v[0])


def solution(mesh):
    fine = Mesh(mesh.devices.reshape([SIZES[a] for a in ALL]), ALL)
    img, blk = ("z", "yh", "x"), ("yl", "core")
    every = img + blk
    rep, crops, rows = P(), P(img, None), P(blk, img, None)
    vec, mat = P(every), P(every, None)
    return jax.shard_map(
        local,
        mesh=fine,
        in_specs=(rows, crops, P(blk, img), rep, P(blk, None)) + (rep,) * 14 + (rows, crops),
        out_specs=(rows, crops, rows, crops, vec, P(blk, img), vec, vec, mat, vec, mat, vec, vec, vec, vec, mat, vec, mat,
                   vec, vec),
        check_vma=False,
    )
```
